128 devices in a mesh: grid: 32 (over z, x, core), lev: 4 (over y).
Axes of the slice: x: 4, y: 4, z: 4, core: 2. Of those that a mesh axis runs over, the one named last changes fastest.
Arguments:
- tiles: bfloat16 [8192, 48, 144], P('grid'), may hold values from 0 to 1
- farm_area: int32 [8192], P('grid'), may hold values from 0 to 511, as said below
- capacity: int32 [8192], P('grid'), may hold values from 20 to 200
- offsets: int32 [512], P('grid'), may hold values from 1 to 12
- state: bfloat16 [48, 8, 262144], P(None, 'lev', 'grid'), may hold values from -6 to 6
Outputs:
- sensitivity: bfloat16 [512, 8, 262144], P(None, 'lev', 'grid')
The draws below stay inside these ranges and needn't reach their ends.
Inputs may be any that keep to these rules, and one draw needn't show every extreme that they name: `farm_area`: among the 256 farms of one grid index (aligned blocks of farms), at most 16 lie in areas of one owner, the owner of area a being a // 16; one owner, drawn from the seed, has exactly 16 farms from every grid index.
All inputs are finite; a program needn't handle non-finite values.
Results may differ from the reference program's by a relative error of at most 0.0056.
Values may be sent and summed in bfloat16 or wider, within the bound.
A program may use at most 128 MiB of HBM per device.

```python
import jax
import jax.numpy as jnp
from jax import lax

M = 48
TS = 144
WMAX = 12
LG = 8
FARM_DEV = 256
AREA_DEV = 16
FARMS = 8192
AREAS = 512
COLUMNS = 262144
CAP = 16
RAMPS = 132


def draw_farm_area(key, part):
    key = jax.random.fold_in(key, 7)
    blocks = FARMS // FARM_DEV
    key_heavy, key_slots, key_local = jax.random.split(key, 3)
    heavy = jax.random.randint(key_heavy, (), 0, blocks).astype(jnp.int32)

    def one_block(block_key):
        slot_key, mix_key = jax.random.split(block_key)
        picks = jax.random.permutation(slot_key, (blocks - 1) * CAP)[:FARM_DEV - CAP] // CAP
        others = (picks + (picks >= heavy).astype(jnp.int32)).astype(jnp.int32)
        owners = jnp.concatenate([jnp.full((CAP,), heavy, jnp.int32), others])
        return owners[jax.random.permutation(mix_key, FARM_DEV)]
    owner = jax.vmap(one_block)(jax.random.split(key_slots, blocks))
    local = jax.random.randint(key_local, (blocks, FARM_DEV), 0, AREA_DEV)
    return (owner * AREA_DEV + local).reshape(FARMS).astype(jnp.int32)


def set_ends(drawn, own_key, low, largest):
    longest = drawn.shape.index(max(drawn.shape))
    spots = []
    for shift in (0, 1):
        where = [jax.random.randint(jax.random.fold_in(own_key, axis), (), 0, length) for axis, length in enumerate(drawn.shape)]
        where[longest] = (where[longest] + shift) % drawn.shape[longest]
        spots.append(tuple(where))
    return drawn.at[spots[0]].set(low).at[spots[1]].set(largest)


def levels(stream_key, shape, shards, least, top_value):
    factor_of = 1.0
    for dim, blocks in shards:
        heights = jax.random.uniform(jax.random.fold_in(jax.random.fold_in(stream_key, 6), dim), (blocks,), jnp.float32, least / len(shards), top_value / len(shards))
        factor_of = factor_of * jnp.repeat(jnp.exp(heights), shape[dim] // blocks).reshape((-1,) + (1,) * (len(shape) - 1 - dim))
    return factor_of


def centred(rng, shape, scale, bound, cuts=(), kind=jnp.bfloat16):
    entries = scale * jax.random.normal(rng, shape, jnp.float32)
    if cuts:
        entries = entries * levels(rng, shape, cuts, -0.22, 0.18)
    return jnp.clip(entries, -bound, bound).astype(kind)


def setup_inputs(seed: int = 0) -> dict:
    key_of = jax.random.split(jax.random.key(seed), 6)
    return {
        "tiles": jnp.clip(1.0 * jax.random.uniform(key_of[0], (FARMS, M, TS), jnp.float32) ** levels(key_of[0], (FARMS, M, TS), ((0, 32),), -0.2, 0.2), 0.0, 1.0).astype(jnp.bfloat16),
        "farm_area": draw_farm_area(jax.random.fold_in(key_of[5], 71), 0),
        "capacity": set_ends(jax.random.randint(key_of[2], (FARMS,), 20, 201), jax.random.fold_in(key_of[2], 1), 20, 200).astype(jnp.int32),
        "offsets": set_ends(jax.random.randint(key_of[3], (AREAS,), 1, WMAX + 1), jax.random.fold_in(key_of[3], 1), 1, WMAX).astype(jnp.int32),
        "state": centred(key_of[4], (M, LG, COLUMNS), 1.0, 6.0, ((1, 4), (2, 32))),
    }


capacity_floor = 200.0
spread_floor = 0.05

def reference(tiles, farm_area, capacity, offsets, state):
    weights = capacity.astype(jnp.float32)
    weighted = tiles.astype(jnp.float32) * weights[:, None, None]
    summed = jax.ops.segment_sum(weighted, farm_area, num_segments=AREAS)
    total = jax.ops.segment_sum(weights, farm_area, num_segments=AREAS)
    power = summed / jnp.maximum(total, capacity_floor)[:, None, None]
    times = jnp.arange(RAMPS, dtype=jnp.int32)
    later_idx = (times[None, :] + offsets[:, None]).astype(jnp.int32)
    later_idx = jnp.broadcast_to(later_idx[:, None, :], (AREAS, M, RAMPS))
    later = jnp.take_along_axis(power, later_idx, axis=2)
    metric = lax.optimization_barrier(jnp.max(later - power[:, :, :RAMPS], axis=2))
    anomaly = metric - lax.optimization_barrier(jnp.mean(metric, axis=1, keepdims=True))
    spread = jnp.sqrt(lax.optimization_barrier(jnp.sum(anomaly * anomaly, axis=1)) / (M - 1))
    scores = (anomaly / jnp.maximum(spread, spread_floor)[:, None]).astype(jnp.bfloat16)
    wide = state.astype(jnp.float32)
    state_anomaly = (wide - lax.optimization_barrier(jnp.mean(wide, axis=0, keepdims=True))).astype(jnp.bfloat16)

    def one_level(level):
        return (jnp.dot(scores, level, preferred_element_type=jnp.float32) / (M - 1)).astype(jnp.bfloat16)
    result = lax.map(one_level, jnp.moveaxis(state_anomaly, 1, 0))
    return jnp.moveaxis(result, 0, 1)
```

```python
import jax
import jax.numpy as jnp
from jax import lax
from jax.experimental import pallas as pl
from jax.experimental.pallas import tpu as pltpu
from jax.sharding import PartitionSpec as P

MESH = pl.DeviceIdType.MESH
M = 48
T = 144
F = 256
AREAS = 512
LANES = 128
RING = 4
PAD_X = 160
ROWS_Z = 80
PAD_Z = 96
HALF = 64
RAMPS = 132
RAMPS_Z = 68
KEEP_X = 152
KEEP_Z = 88
QUADS = 8
ROWS = 256
capacity_floor = 200.0
spread_floor = 0.05


def iota(shape, dim):
    return lax.broadcasted_iota(jnp.int32, shape, dim)


def swap_halves(u, v):
    low = iota(u.shape, 1) < 4
    first = jnp.where(low, u, pltpu.roll(v, 4, 1))
    second = jnp.where(low, pltpu.roll(u, 4, 1), v)
    return first, second


def ramp_metric(summed, steps, offset, ramps):
    total = jnp.maximum(summed[steps : steps + 1], capacity_floor)
    power = summed[:steps] / total
    wide = jnp.broadcast_to(offset, power.shape).astype(jnp.int32)
    later = power
    for bit in (1, 2, 4, 8):
        later = jnp.where((wide & bit) != 0, pltpu.roll(later, steps - bit, 0), later)
    row = iota(power.shape, 0)
    return jnp.max(jnp.where(row < ramps, later - power, -3e38), axis=0, keepdims=True)


STEP = (0, 0, 1, 1, 3, 3, 2, 2)
BACK = (0, 1, 4, 5, 2, 3, 6, 7)
NEAR = 6
ORDER = (6, 7, 2, 4, 3, 5, 1)


def exchange_kernel(
    tiles, farm_area, capacity, offsets, state, metric_out, slab_out,
    area_in, capacity_in, offsets_in,
    facts_x, facts_z, got_x, got_z, weight_x, weight_z,
    part_x, part_z, sum_x, sum_z, off_x, off_z,
    small, gathered, z_rows, st,
    local_sem, fx_send, fx_recv, fz_send, fz_recv, x_send, x_recv, z_send, z_recv,
    bx_send, bx_recv, bz_send, bz_recv,
    s1_send, s1_recv, s2_send, s2_recv,
):
    g = lax.axis_index("grid")
    y = lax.axis_index("lev")
    z = lax.div(g, 8)
    x = lax.rem(lax.div(g, 2), 4)
    c = lax.rem(g, 2)
    mine_x = 2 * x + c
    mine_z = 2 * z + c
    xs = [x] + [lax.rem(x + d, 4) for d in range(1, 4)]
    zs = [z] + [lax.rem(z + d, 4) for d in range(1, 4)]
    ys = [y] + [lax.rem(y + d, 4) for d in range(1, 4)]
    cs = [c, 1 - c]

    def device(xx, zz, cc, yy):
        return (zz * 8 + xx * 2 + cc, yy)

    sibling = device(x, z, 1 - c, y)
    x_peers = [(xs[STEP[i]], cs[i % 2]) for i in range(8)]
    z_peers = [(zs[STEP[i]], cs[i % 2]) for i in range(8)]

    def remote(src, dst, send_sem, recv_sem, to):
        return pltpu.make_async_remote_copy(
            src_ref=src, dst_ref=dst, send_sem=send_sem, recv_sem=recv_sem,
            device_id=to, device_id_type=MESH)

    def wait_for(slot, send, recv):
        remote(slot, slot, send, recv, sibling).wait_recv()

    def loop(first, last):
        def run(body):
            lax.fori_loop(first, last, lambda i, carry: (body(i), carry)[1], 0)
        return run

    barrier = pltpu.get_barrier_semaphore()

    def greet(to):
        pl.semaphore_signal(barrier, inc=1, device_id=to, device_id_type=MESH)

    for i in ORDER:
        xx, cc = x_peers[i]
        greet(device(xx, z, cc, y))
        if i != 1:
            zz, cc = z_peers[i]
            greet(device(x, zz, cc, y))
    for d in (2, 1, 3):
        greet(device(x, z, c, ys[d]))

    def x_slot(i):
        return got_x.at[pl.ds(0, T), pl.ds(F * i, F)]

    def z_slot(i):
        return got_z.at[pl.ds(0, ROWS_Z), pl.ds(F * i, F)]

    def x_tile(xx, cc):
        return tiles.at[12 * y + 2 * xx + cc]

    def z_tile(zz, cc):
        return tiles.at[12 * y + 8 + zz, pl.ds(pl.multiple_of(HALF * cc, HALF), ROWS_Z)]

    local = [
        pltpu.make_async_copy(farm_area, area_in, local_sem.at[0]),
        pltpu.make_async_copy(capacity, capacity_in, local_sem.at[1]),
        pltpu.make_async_copy(offsets, offsets_in, local_sem.at[2]),
        pltpu.make_async_copy(z_tile(z, c), z_slot(0), local_sem.at[3]),
        pltpu.make_async_copy(x_tile(x, c), x_slot(0), local_sem.at[4]),
        pltpu.make_async_copy(state, st, local_sem.at[5]),
    ]
    for copy in local:
        copy.start()
    for copy in local[:3]:
        copy.wait()

    lane = iota((1, F), 1)
    offset = jnp.zeros((1, F), jnp.int32)
    for k in range(16):
        offset = jnp.where((lane & 15) == k, offsets_in[k], offset)
    area = area_in[...]
    turned = ((area >> 5) & 3) * 128 + (area >> 7) * 32 + (area & 31)
    for facts, ids, spot in ((facts_z, turned, mine_z), (facts_x, area, mine_x)):
        placed = jnp.where((lane >> 4) == spot, offset, 0)
        rows = jnp.concatenate(
            [ids, capacity_in[...], placed, jnp.zeros((1, F), jnp.int32)], axis=0)
        facts[0] = rows.astype(jnp.float32)
    pl.semaphore_wait(barrier, 16)

    def fx_copy(i):
        xx, cc = x_peers[i]
        return remote(facts_x.at[0], facts_x.at[BACK[i]], fx_send.at[i], fx_recv.at[BACK[i]],
                      device(xx, z, cc, y))

    def fz_copy(i):
        zz, cc = z_peers[i]
        return remote(facts_z.at[0], facts_z.at[BACK[i]], fz_send.at[i], fz_recv.at[BACK[i]],
                      device(x, zz, cc, y))

    def x_copy(i):
        xx, cc = x_peers[i]
        return remote(x_tile(xx, cc), x_slot(BACK[i]), x_send.at[i], x_recv.at[BACK[i]],
                      device(xx, z, cc, y))

    def z_copy(i):
        zz, cc = z_peers[i]
        return remote(z_tile(zz, cc), z_slot(BACK[i]), z_send.at[i], z_recv.at[BACK[i]],
                      device(x, zz, cc, y))

    sends = [x_copy(6), x_copy(7), z_copy(6), z_copy(7)]
    sends += [f(i) for i in ORDER for f in (fz_copy, fx_copy)]
    sends += [f(i) for i in ORDER[2:] for f in (x_copy, z_copy)]
    for copy in sends:
        copy.start()

    local[5].wait()

    @loop(0, QUADS)
    def _(i):
        values = st[:, i].astype(jnp.float32).reshape(M, 2, 8, LANES)
        values = values - (jnp.sum(values, axis=0) / M)[None]
        pairs = values.reshape(M // 2, 2, 2, 8, LANES)
        for h in range(2):
            both = swap_halves(pairs[:, 0, h], pairs[:, 1, h])
            for k in range(2):
                slab_out[i, :, pl.ds((2 * h + k) * LANES, LANES)] = (
                    both[k].reshape(4 * M, LANES).astype(jnp.bfloat16))

    got_x[pl.ds(T, 16)] = jnp.ones((16, 8 * F), jnp.bfloat16)
    got_z[pl.ds(ROWS_Z, 16)] = jnp.ones((16, 8 * F), jnp.bfloat16)
    off_x[...] = jnp.zeros_like(off_x)
    off_z[...] = jnp.zeros_like(off_z)
    area_ids = iota((F, AREAS), 1).astype(jnp.float32)

    @loop(0, 8)
    def _(i):
        for facts, recv, send, weight, off in (
                (facts_z, fz_recv, fz_send, weight_z, off_z),
                (facts_x, fx_recv, fx_send, weight_x, off_x)):
            @pl.when(i > 0)
            def _():
                wait_for(facts.at[i], send.at[i], recv.at[i])

            rows = facts[i]
            off[...] = off[...] + rows[2:3, :LANES]
            columns = jnp.transpose(jnp.concatenate([rows, rows], axis=0))
            placed = jnp.where(area_ids == columns[:, 0:1], columns[:, 1:2], 0.0)
            weight[pl.ds(pl.multiple_of(F * i, F), F)] = placed.astype(jnp.bfloat16)

    local[3].wait()
    for i in range(1, 8):
        wait_for(z_slot(i), z_send.at[i], z_recv.at[i])
    for h in range(2):
        value = jnp.dot(got_z[...], weight_z[:, pl.ds(2 * LANES * h, 2 * LANES)],
                        preferred_element_type=jnp.float32)
        for b in range(2):
            part_z[2 * h + b] = value[:KEEP_Z, b * LANES : (b + 1) * LANES]
    bz, bx = [], []
    for d in (2, 1, 3):
        bz.append(remote(part_z.at[xs[d]], sum_z.at[3 - d], bz_send.at[d - 1], bz_recv.at[3 - d],
                         device(xs[d], z, c, y)))
        bz[-1].start()

    local[4].wait()
    for i in range(1, NEAR):
        wait_for(x_slot(i), x_send.at[i], x_recv.at[i])
    near, far = pl.ds(0, NEAR * F), pl.ds(NEAR * F, (8 - NEAR) * F)
    for h in range(2):
        value = jnp.dot(got_x[:, near], weight_x[near, pl.ds(2 * LANES * h, 2 * LANES)],
                        preferred_element_type=jnp.float32)
        for b in range(2):
            part_x[2 * h + b] = value[:KEEP_X, b * LANES : (b + 1) * LANES]
    for i in range(NEAR, 8):
        wait_for(x_slot(i), x_send.at[i], x_recv.at[i])
    for pair in ((2, 1), (3, 0)):
        chosen = jnp.concatenate(
            [weight_x[far, pl.ds(pl.multiple_of(LANES * zs[d], LANES), LANES)] for d in pair],
            axis=1)
        value = jnp.dot(got_x[:, far], chosen, preferred_element_type=jnp.float32)
        for k, d in enumerate(pair):
            part_x[zs[d]] = part_x[zs[d]] + value[:KEEP_X, k * LANES : (k + 1) * LANES]
            if d > 0:
                bx.append(remote(part_x.at[zs[d]], sum_x.at[3 - d], bx_send.at[d - 1],
                                 bx_recv.at[3 - d], device(x, zs[d], c, y)))
                bx[-1].start()

    for copy in bz:
        copy.wait_recv()
    summed = part_z[x] + sum_z[0] + sum_z[1] + sum_z[2]
    small[mine_x, pl.ds(1, 1)] = ramp_metric(summed, ROWS_Z, off_z[...], RAMPS_Z)

    for copy in bx:
        copy.wait_recv()

    summed = part_x[z] + sum_x[0] + sum_x[1] + sum_x[2]
    small[mine_x, pl.ds(0, 1)] = ramp_metric(summed, T, off_x[...], RAMPS)

    def swap(ref, slot, far, send_sem, recv_sem, to):
        copy = remote(ref.at[slot], ref.at[slot], send_sem, recv_sem.at[slot], to)
        copy.start()
        sends.append(copy)
        return remote(ref.at[far], ref.at[far], send_sem, recv_sem.at[far], to)

    back = []
    for i in ORDER:
        xx, cc = x_peers[i]
        back.append(swap(small, mine_x, 2 * xx + cc, s1_send.at[i], s1_recv,
                         device(xx, z, cc, y)))
    for copy in reversed(back):
        copy.wait_recv()

    joined = gathered.at[y, z]
    for s in range(8):
        joined[s // 4, pl.ds(s % 4, 1)] = small[s, pl.ds(0, 1)]
    for b in range(RING):
        joined[2, pl.ds(b, 1)] = jnp.maximum(
            small[2 * b, pl.ds(1, 1)], small[2 * b + 1, pl.ds(1, 1)])

    sends_now = [(dy, dz) for dy in (2, 1, 3, 0) for dz in (2, 1, 3, 0)][:-1]
    back = []
    for k, (dy, dz) in enumerate(sends_now):
        out = remote(joined, joined, s2_send.at[k], s2_recv.at[4 * y + z],
                     device(x, zs[dz], c, ys[dy]))
        out.start()
        sends.append(out)
        slot = gathered.at[ys[dy], zs[dz]]
        back.append((slot, s2_send.at[k], s2_recv.at[4 * ys[dy] + zs[dz]]))
    for slot, send, recv in reversed(back):
        wait_for(slot, send, recv)

    for zz in range(4):
        for yy in range(4):
            slot = 4 * yy + zz
            for h in range(2):
                metric_out[pl.ds(8 * yy + 4 * h, 4), pl.ds(zz * LANES, LANES)] = gathered[yy, zz, h]
            for b in range(RING):
                z_rows[b, pl.ds(slot, 1)] = gathered[yy, zz, 2, pl.ds(b, 1)]
    quarter = iota((16, LANES), 1) >> 5
    blocks = [z_rows[b] for b in range(RING)]
    for zz in range(4):
        value = jnp.zeros((16, LANES), jnp.float32)
        for b in range(RING):
            move = (32 * (b - zz)) % LANES
            moved = pltpu.roll(blocks[b], move, 1) if move else blocks[b]
            value = jnp.where(quarter == b, moved, value)
        metric_out[pl.ds(32, 16), pl.ds(zz * LANES, LANES)] = value

    for copy in sends + bx + bz:
        copy.wait_send()


def exchange(tiles, farm_area, capacity, offsets, state):
    any_space = pl.BlockSpec(memory_space=pl.ANY)
    vmem = pl.BlockSpec(memory_space=pltpu.VMEM)
    dma = pltpu.SemaphoreType.DMA
    f32, bf16 = jnp.float32, jnp.bfloat16
    return pl.pallas_call(
        exchange_kernel,
        out_shape=(
            pltpu.VMEM((M, AREAS), f32),
            pltpu.VMEM((QUADS, 4 * M, 4 * LANES), bf16),
        ),
        in_specs=[any_space] * 5,
        out_specs=(vmem, vmem),
        scratch_shapes=[
            pltpu.VMEM((1, F), jnp.int32),
            pltpu.VMEM((1, F), jnp.int32),
            pltpu.SMEM((16,), jnp.int32),
            pltpu.VMEM((8, 4, F), f32),
            pltpu.VMEM((8, 4, F), f32),
            pltpu.VMEM((PAD_X, 8 * F), bf16),
            pltpu.VMEM((PAD_Z, 8 * F), bf16),
            pltpu.VMEM((8 * F, AREAS), bf16),
            pltpu.VMEM((8 * F, AREAS), bf16),
            pltpu.VMEM((RING, KEEP_X, LANES), f32),
            pltpu.VMEM((RING, KEEP_Z, LANES), f32),
            pltpu.VMEM((3, KEEP_X, LANES), f32),
            pltpu.VMEM((3, KEEP_Z, LANES), f32),
            pltpu.VMEM((1, LANES), f32),
            pltpu.VMEM((1, LANES), f32),
            pltpu.VMEM((8, 2, LANES), f32),
            pltpu.VMEM((4, 4, 3, 4, LANES), f32),
            pltpu.VMEM((RING, 16, LANES), f32),
            pltpu.VMEM((M, QUADS, 16, LANES), bf16),
            dma((6,)), dma((8,)), dma((8,)), dma((8,)), dma((8,)),
            dma((8,)), dma((8,)), dma((8,)), dma((8,)),
            dma((3,)), dma((3,)), dma((3,)), dma((3,)),
            dma((8,)), dma((8,)), dma((16,)), dma((16,)),
        ],
        compiler_params=pltpu.CompilerParams(
            collective_id=0, has_side_effects=True, vmem_limit_bytes=60 * 2**20),
        cost_estimate=pl.CostEstimate(
            flops=2 * 256 * 2048 * 512, bytes_accessed=5 * 2**20, transcendentals=0),
        name="exchange",
    )(tiles, farm_area, capacity, offsets, state)


def product_kernel(metric, slab, out, wide, lhs, stage, out_sem):
    values = metric[...]
    anomaly = values - jnp.mean(values, axis=0, keepdims=True)
    spread = jnp.sqrt(jnp.sum(anomaly * anomaly, axis=0, keepdims=True) / (M - 1))
    scores = anomaly / jnp.maximum(spread, spread_floor)
    scores = jnp.transpose(scores).astype(jnp.bfloat16)

    held = iota((M, 4 * M), 0)
    rest = held - 32
    member = jnp.where(
        held < 32,
        12 * (held >> 3) + (held & 7),
        12 * (rest >> 2) + 8 + (rest & 3))
    widen = ((iota((M, 4 * M), 1) >> 2) == member).astype(jnp.bfloat16)
    wide[...] = jnp.dot(scores, widen, preferred_element_type=jnp.float32).astype(jnp.bfloat16)
    repeat = ((iota((ROWS, ROWS // 4), 0) >> 2) == iota((ROWS, ROWS // 4), 1)).astype(
        jnp.bfloat16)
    keep = (iota((ROWS, 4 * M), 0) & 3) == (iota((ROWS, 4 * M), 1) & 3)
    areas = ROWS // 4

    for r in range(4 * AREAS // ROWS):
        rows = jnp.dot(repeat, wide[pl.ds(r * areas, areas)], preferred_element_type=jnp.float32)
        lhs[pl.ds(r * ROWS, ROWS)] = jnp.where(keep, rows, 0.0).astype(jnp.bfloat16)

    def part(i, q):
        some = pl.ds(128 * q, 128)
        return pltpu.make_async_copy(stage.at[i, some], out.at[some, i], out_sem.at[4 * i + q])

    def step(j, carry):
        for k in range(2):
            i = 2 * j + k
            for r in range(4 * AREAS // ROWS):
                left = lhs[pl.ds(r * ROWS, ROWS)]
                parts = []
                for h in range(2):
                    acc = jnp.dot(left, slab[i, :, pl.ds(2 * LANES * h, 2 * LANES)],
                                  preferred_element_type=jnp.float32)
                    acc = (acc * (1.0 / (M - 1))).reshape(ROWS // 8, 8, 2 * LANES)
                    both = swap_halves(acc[:, :, :LANES], acc[:, :, LANES:])
                    parts.append(jnp.stack(both, axis=1).reshape(areas, 8, LANES))
                done = jnp.stack(parts, axis=1).reshape(areas, 16, LANES)
                stage[i, pl.ds(r * areas, areas)] = done.astype(jnp.bfloat16)
                if (r + 1) * areas % 128 == 0:
                    part(i, r * areas // 128).start()
        return carry

    lax.fori_loop(0, QUADS // 2, step, 0)

    def finish(i, carry):
        for q in range(4):
            part(i, q).wait()
        return carry

    lax.fori_loop(0, QUADS, finish, 0)


def product(metric, slab):
    any_space = pl.BlockSpec(memory_space=pl.ANY)
    dma = pltpu.SemaphoreType.DMA
    return pl.pallas_call(
        product_kernel,
        out_shape=jax.ShapeDtypeStruct((AREAS, QUADS, 16, LANES), jnp.bfloat16),
        in_specs=[pl.BlockSpec(memory_space=pltpu.VMEM)] * 2,
        out_specs=any_space,
        scratch_shapes=[
            pltpu.VMEM((AREAS, 4 * M), jnp.bfloat16),
            pltpu.VMEM((4 * AREAS, 4 * M), jnp.bfloat16),
            pltpu.VMEM((QUADS, AREAS, 16, LANES), jnp.bfloat16),
            dma((32,)),
        ],
        compiler_params=pltpu.CompilerParams(vmem_limit_bytes=32 * 2**20),
        cost_estimate=pl.CostEstimate(
            flops=2 * 2048 * 192 * 4096, bytes_accessed=20 * 2**20, transcendentals=0),
        name="product",
    )(metric, slab)


def body(tiles, farm_area, capacity, offsets, state):
    by_member = jnp.transpose(tiles, (1, 2, 0))
    columns = state.reshape(M, 2, 64, LANES)
    columns = jnp.transpose(columns, (0, 2, 1, 3)).reshape(M, QUADS, 16, LANES)
    metric, slab = exchange(
        by_member, farm_area.reshape(1, F), capacity.reshape(1, F), offsets, columns)
    out = product(metric, slab)
    out = jnp.transpose(out.reshape(AREAS, 64, 2, LANES), (0, 2, 1, 3))
    return out.reshape(AREAS, 2, 64 * LANES)


def solution(mesh):
    in_specs = (P("grid", None, None), P("grid"), P("grid"), P("grid"), P(None, "lev", "grid"))
    out_specs = P(None, "lev", "grid")
    return jax.shard_map(body, mesh=mesh, in_specs=in_specs, out_specs=out_specs, check_vma=False)
```

```python
import jax
import jax.numpy as jnp
from jax import lax
from jax.experimental import pallas as pl
from jax.experimental.pallas import tpu as pltpu
from jax.sharding import PartitionSpec as P

MESH = pl.DeviceIdType.MESH
M = 48
T = 144
F = 256
AREAS = 512
LANES = 128
RING = 4
PAD_X = 160
ROWS_Z = 80
PAD_Z = 96
HALF = 64
RAMPS = 132
RAMPS_Z = 68
KEEP_X = 152
KEEP_Z = 88
QUADS = 8
ROWS = 256
capacity_floor = 200.0
spread_floor = 0.05


def iota(shape, dim):
    return lax.broadcasted_iota(jnp.int32, shape, dim)


def swap_halves(u, v):
    low = iota(u.shape, 1) < 4
    first = jnp.where(low, u, pltpu.roll(v, 4, 1))
    second = jnp.where(low, pltpu.roll(u, 4, 1), v)
    return first, second


def ramp_metric(summed, steps, offset, ramps):
    total = jnp.maximum(summed[steps : steps + 1], capacity_floor)
    power = summed[:steps] / total
    wide = jnp.broadcast_to(offset, power.shape).astype(jnp.int32)
    later = power
    for bit in (1, 2, 4, 8):
        later = jnp.where((wide & bit) != 0, pltpu.roll(later, steps - bit, 0), later)
    row = iota(power.shape, 0)
    return jnp.max(jnp.where(row < ramps, later - power, -3e38), axis=0, keepdims=True)


STEP = (0, 0, 1, 1, 3, 3, 2, 2)
BACK = (0, 1, 4, 5, 2, 3, 6, 7)
ORDER = (6, 7, 2, 4, 3, 5, 1)
FIRST = 80
HALVES = (pl.ds(0, FIRST), pl.ds(FIRST, T - FIRST))


def exchange_kernel(
    tiles, farm_area, capacity, offsets, state, metric_out, slab_out,
    area_in, capacity_in, offsets_in,
    facts_x, facts_z, got_x, got_z, weight_x, weight_z,
    part_x, part_z, sum_x, sum_z, off_x, off_z,
    small, gathered, z_rows, st,
    local_sem, fx_send, fx_recv, fz_send, fz_recv, x_send, x_recv, z_send, z_recv,
    bx_send, bx_recv, bz_send, bz_recv,
    s1_send, s1_recv, s2_send, s2_recv,
):
    g = lax.axis_index("grid")
    y = lax.axis_index("lev")
    z = lax.div(g, 8)
    x = lax.rem(lax.div(g, 2), 4)
    c = lax.rem(g, 2)
    mine_x = 2 * x + c
    mine_z = 2 * z + c
    xs = [x] + [lax.rem(x + d, 4) for d in range(1, 4)]
    zs = [z] + [lax.rem(z + d, 4) for d in range(1, 4)]
    ys = [y] + [lax.rem(y + d, 4) for d in range(1, 4)]
    cs = [c, 1 - c]

    def device(xx, zz, cc, yy):
        return (zz * 8 + xx * 2 + cc, yy)

    sibling = device(x, z, 1 - c, y)
    x_peers = [(xs[STEP[i]], cs[i % 2]) for i in range(8)]
    z_peers = [(zs[STEP[i]], cs[i % 2]) for i in range(8)]

    def remote(src, dst, send_sem, recv_sem, to):
        return pltpu.make_async_remote_copy(
            src_ref=src, dst_ref=dst, send_sem=send_sem, recv_sem=recv_sem,
            device_id=to, device_id_type=MESH)

    def wait_for(slot, send, recv):
        remote(slot, slot, send, recv, sibling).wait_recv()

    def loop(first, last):
        def run(body):
            lax.fori_loop(first, last, lambda i, carry: (body(i), carry)[1], 0)
        return run

    barrier = pltpu.get_barrier_semaphore()

    def greet(to):
        pl.semaphore_signal(barrier, inc=1, device_id=to, device_id_type=MESH)

    for i in ORDER:
        xx, cc = x_peers[i]
        greet(device(xx, z, cc, y))
        if i != 1:
            zz, cc = z_peers[i]
            greet(device(x, zz, cc, y))
    for d in (2, 1, 3):
        greet(device(x, z, c, ys[d]))

    def x_slot(i, half):
        return got_x.at[HALVES[half], pl.ds(F * i, F)]

    def z_slot(i):
        return got_z.at[pl.ds(0, ROWS_Z), pl.ds(F * i, F)]

    def x_tile(xx, cc):
        return tiles.at[12 * y + 2 * xx + cc]

    def z_tile(zz, cc):
        return tiles.at[12 * y + 8 + zz, pl.ds(pl.multiple_of(HALF * cc, HALF), ROWS_Z)]

    local = [
        pltpu.make_async_copy(farm_area, area_in, local_sem.at[0]),
        pltpu.make_async_copy(capacity, capacity_in, local_sem.at[1]),
        pltpu.make_async_copy(offsets, offsets_in, local_sem.at[2]),
        pltpu.make_async_copy(z_tile(z, c), z_slot(0), local_sem.at[3]),
        pltpu.make_async_copy(x_tile(x, c), got_x.at[pl.ds(0, T), pl.ds(0, F)], local_sem.at[4]),
        pltpu.make_async_copy(state, st, local_sem.at[5]),
    ]
    for copy in local:
        copy.start()
    pl.semaphore_wait(barrier, 16)

    def fx_copy(i):
        xx, cc = x_peers[i]
        return remote(facts_x.at[0], facts_x.at[BACK[i]], fx_send.at[i], fx_recv.at[BACK[i]],
                      device(xx, z, cc, y))

    def fz_copy(i):
        zz, cc = z_peers[i]
        return remote(facts_z.at[0], facts_z.at[BACK[i]], fz_send.at[i], fz_recv.at[BACK[i]],
                      device(x, zz, cc, y))

    def x_copy(i, half):
        xx, cc = x_peers[i]
        return remote(x_tile(xx, cc).at[HALVES[half]], x_slot(BACK[i], half),
                      x_send.at[half, i], x_recv.at[half, BACK[i]], device(xx, z, cc, y))

    def z_copy(i):
        zz, cc = z_peers[i]
        return remote(z_tile(zz, cc), z_slot(BACK[i]), z_send.at[i], z_recv.at[BACK[i]],
                      device(x, zz, cc, y))

    sends = []

    def start(*copies):
        for copy in copies:
            copy.start()
            sends.append(copy)

    start(x_copy(6, 0), x_copy(7, 0), z_copy(6), z_copy(7))
    for copy in local[:3]:
        copy.wait()

    lane = iota((1, F), 1)
    offset = jnp.zeros((1, F), jnp.int32)
    for k in range(16):
        offset = jnp.where((lane & 15) == k, offsets_in[k], offset)
    area = area_in[...]
    turned = ((area >> 5) & 3) * 128 + (area >> 7) * 32 + (area & 31)
    for facts, ids, spot in ((facts_z, turned, mine_z), (facts_x, area, mine_x)):
        placed = jnp.where((lane >> 4) == spot, offset, 0)
        rows = jnp.concatenate(
            [ids, capacity_in[...], placed, jnp.zeros((1, F), jnp.int32)], axis=0)
        facts[0] = rows.astype(jnp.float32)

    for i in ORDER:
        start(fz_copy(i), fx_copy(i))
    for i in ORDER[2:]:
        start(x_copy(i, 0), z_copy(i))

    local[5].wait()

    @loop(0, QUADS)
    def _(i):
        values = st[:, i].astype(jnp.float32).reshape(M, 2, 8, LANES)
        values = values - (jnp.sum(values, axis=0) / M)[None]
        pairs = values.reshape(M // 2, 2, 2, 8, LANES)
        for h in range(2):
            both = swap_halves(pairs[:, 0, h], pairs[:, 1, h])
            for k in range(2):
                slab_out[i, :, pl.ds((2 * h + k) * LANES, LANES)] = (
                    both[k].reshape(4 * M, LANES).astype(jnp.bfloat16))

    for i in ORDER:
        start(x_copy(i, 1))

    got_x[pl.ds(T, 16)] = jnp.ones((16, 8 * F), jnp.bfloat16)
    got_z[pl.ds(ROWS_Z, 16)] = jnp.ones((16, 8 * F), jnp.bfloat16)
    off_x[...] = jnp.zeros_like(off_x)
    off_z[...] = jnp.zeros_like(off_z)
    area_ids = iota((F, AREAS), 1).astype(jnp.float32)

    @loop(0, 8)
    def _(i):
        for facts, recv, send, weight, off in (
                (facts_z, fz_recv, fz_send, weight_z, off_z),
                (facts_x, fx_recv, fx_send, weight_x, off_x)):
            @pl.when(i > 0)
            def _():
                wait_for(facts.at[i], send.at[i], recv.at[i])

            rows = facts[i]
            off[...] = off[...] + rows[2:3, :LANES]
            columns = jnp.transpose(jnp.concatenate([rows, rows], axis=0))
            placed = jnp.where(area_ids == columns[:, 0:1], columns[:, 1:2], 0.0)
            weight[pl.ds(pl.multiple_of(F * i, F), F)] = placed.astype(jnp.bfloat16)

    local[3].wait()
    for i in range(1, 8):
        wait_for(z_slot(i), z_send.at[i], z_recv.at[i])
    for h in range(2):
        value = jnp.dot(got_z[...], weight_z[:, pl.ds(2 * LANES * h, 2 * LANES)],
                        preferred_element_type=jnp.float32)
        for b in range(2):
            part_z[2 * h + b] = value[:KEEP_Z, b * LANES : (b + 1) * LANES]
    local[4].wait()
    bz, bx = [], []

    def part_copy(d, half, first, count):
        rows = pl.ds(first, count)
        return remote(part_x.at[zs[d], rows], sum_x.at[3 - d, rows], bx_send.at[half, d - 1],
                      bx_recv.at[half, 3 - d], device(x, zs[d], c, y))

    for half, (first, count, keep) in enumerate(
            ((0, FIRST, FIRST), (FIRST, PAD_X - FIRST, KEEP_X - FIRST))):
        for i in range(1, 8):
            wait_for(x_slot(i, half), x_send.at[half, i], x_recv.at[half, i])
        for pair in ((2, 1), (3, 0)):
            chosen = jnp.concatenate(
                [weight_x[:, pl.ds(pl.multiple_of(LANES * zs[d], LANES), LANES)] for d in pair],
                axis=1)
            value = jnp.dot(got_x[pl.ds(first, count)], chosen,
                            preferred_element_type=jnp.float32)
            for k, d in enumerate(pair):
                part_x[zs[d], pl.ds(first, keep)] = value[:keep, k * LANES : (k + 1) * LANES]
                if d > 0:
                    bx.append(part_copy(d, half, first, keep))
                    bx[-1].start()
    for d in (2, 1, 3):
        bz.append(remote(part_z.at[xs[d]], sum_z.at[3 - d], bz_send.at[d - 1], bz_recv.at[3 - d],
                         device(xs[d], z, c, y)))
        bz[-1].start()

    for copy in bz:
        copy.wait_recv()
    summed = part_z[x] + sum_z[0] + sum_z[1] + sum_z[2]
    small[mine_x, pl.ds(1, 1)] = ramp_metric(summed, ROWS_Z, off_z[...], RAMPS_Z)

    for copy in bx:
        copy.wait_recv()

    summed = part_x[z] + sum_x[0] + sum_x[1] + sum_x[2]
    small[mine_x, pl.ds(0, 1)] = ramp_metric(summed, T, off_x[...], RAMPS)

    def swap(ref, slot, far, send_sem, recv_sem, to):
        copy = remote(ref.at[slot], ref.at[slot], send_sem, recv_sem.at[slot], to)
        copy.start()
        sends.append(copy)
        return remote(ref.at[far], ref.at[far], send_sem, recv_sem.at[far], to)

    back = []
    for i in ORDER:
        xx, cc = x_peers[i]
        back.append(swap(small, mine_x, 2 * xx + cc, s1_send.at[i], s1_recv,
                         device(xx, z, cc, y)))
    for copy in reversed(back):
        copy.wait_recv()

    joined = gathered.at[y, z]
    for s in range(8):
        joined[s // 4, pl.ds(s % 4, 1)] = small[s, pl.ds(0, 1)]
    for b in range(RING):
        joined[2, pl.ds(b, 1)] = jnp.maximum(
            small[2 * b, pl.ds(1, 1)], small[2 * b + 1, pl.ds(1, 1)])

    sends_now = [(dy, dz) for dy in (2, 1, 3, 0) for dz in (2, 1, 3, 0)][:-1]
    back = []
    for k, (dy, dz) in enumerate(sends_now):
        out = remote(joined, joined, s2_send.at[k], s2_recv.at[4 * y + z],
                     device(x, zs[dz], c, ys[dy]))
        out.start()
        sends.append(out)
        slot = gathered.at[ys[dy], zs[dz]]
        back.append((slot, s2_send.at[k], s2_recv.at[4 * ys[dy] + zs[dz]]))
    for slot, send, recv in reversed(back):
        wait_for(slot, send, recv)

    for zz in range(4):
        for yy in range(4):
            slot = 4 * yy + zz
            for h in range(2):
                metric_out[pl.ds(8 * yy + 4 * h, 4), pl.ds(zz * LANES, LANES)] = gathered[yy, zz, h]
            for b in range(RING):
                z_rows[b, pl.ds(slot, 1)] = gathered[yy, zz, 2, pl.ds(b, 1)]
    quarter = iota((16, LANES), 1) >> 5
    blocks = [z_rows[b] for b in range(RING)]
    for zz in range(4):
        value = jnp.zeros((16, LANES), jnp.float32)
        for b in range(RING):
            move = (32 * (b - zz)) % LANES
            moved = pltpu.roll(blocks[b], move, 1) if move else blocks[b]
            value = jnp.where(quarter == b, moved, value)
        metric_out[pl.ds(32, 16), pl.ds(zz * LANES, LANES)] = value

    for copy in sends + bx + bz:
        copy.wait_send()


def exchange(tiles, farm_area, capacity, offsets, state):
    any_space = pl.BlockSpec(memory_space=pl.ANY)
    vmem = pl.BlockSpec(memory_space=pltpu.VMEM)
    dma = pltpu.SemaphoreType.DMA
    f32, bf16 = jnp.float32, jnp.bfloat16
    return pl.pallas_call(
        exchange_kernel,
        out_shape=(
            pltpu.VMEM((M, AREAS), f32),
            pltpu.VMEM((QUADS, 4 * M, 4 * LANES), bf16),
        ),
        in_specs=[any_space] * 5,
        out_specs=(vmem, vmem),
        scratch_shapes=[
            pltpu.VMEM((1, F), jnp.int32),
            pltpu.VMEM((1, F), jnp.int32),
            pltpu.SMEM((16,), jnp.int32),
            pltpu.VMEM((8, 4, F), f32),
            pltpu.VMEM((8, 4, F), f32),
            pltpu.VMEM((PAD_X, 8 * F), bf16),
            pltpu.VMEM((PAD_Z, 8 * F), bf16),
            pltpu.VMEM((8 * F, AREAS), bf16),
            pltpu.VMEM((8 * F, AREAS), bf16),
            pltpu.VMEM((RING, KEEP_X, LANES), f32),
            pltpu.VMEM((RING, KEEP_Z, LANES), f32),
            pltpu.VMEM((3, KEEP_X, LANES), f32),
            pltpu.VMEM((3, KEEP_Z, LANES), f32),
            pltpu.VMEM((1, LANES), f32),
            pltpu.VMEM((1, LANES), f32),
            pltpu.VMEM((8, 2, LANES), f32),
            pltpu.VMEM((4, 4, 3, 4, LANES), f32),
            pltpu.VMEM((RING, 16, LANES), f32),
            pltpu.VMEM((M, QUADS, 16, LANES), bf16),
            dma((6,)), dma((8,)), dma((8,)), dma((8,)), dma((8,)),
            dma((2, 8)), dma((2, 8)), dma((8,)), dma((8,)),
            dma((2, 3)), dma((2, 3)), dma((3,)), dma((3,)),
            dma((8,)), dma((8,)), dma((16,)), dma((16,)),
        ],
        compiler_params=pltpu.CompilerParams(
            collective_id=0, has_side_effects=True, vmem_limit_bytes=60 * 2**20),
        cost_estimate=pl.CostEstimate(
            flops=2 * 256 * 2048 * 512, bytes_accessed=5 * 2**20, transcendentals=0),
        name="exchange",
    )(tiles, farm_area, capacity, offsets, state)


def product_kernel(metric, slab, out, wide, lhs, stage, out_sem):
    values = metric[...]
    anomaly = values - jnp.mean(values, axis=0, keepdims=True)
    spread = jnp.sqrt(jnp.sum(anomaly * anomaly, axis=0, keepdims=True) / (M - 1))
    scores = anomaly / jnp.maximum(spread, spread_floor)
    scores = jnp.transpose(scores).astype(jnp.bfloat16)

    held = iota((M, 4 * M), 0)
    rest = held - 32
    member = jnp.where(
        held < 32,
        12 * (held >> 3) + (held & 7),
        12 * (rest >> 2) + 8 + (rest & 3))
    widen = ((iota((M, 4 * M), 1) >> 2) == member).astype(jnp.bfloat16)
    wide[...] = jnp.dot(scores, widen, preferred_element_type=jnp.float32).astype(jnp.bfloat16)
    repeat = ((iota((ROWS, ROWS // 4), 0) >> 2) == iota((ROWS, ROWS // 4), 1)).astype(
        jnp.bfloat16)
    keep = (iota((ROWS, 4 * M), 0) & 3) == (iota((ROWS, 4 * M), 1) & 3)
    areas = ROWS // 4

    for r in range(4 * AREAS // ROWS):
        rows = jnp.dot(repeat, wide[pl.ds(r * areas, areas)], preferred_element_type=jnp.float32)
        lhs[pl.ds(r * ROWS, ROWS)] = jnp.where(keep, rows, 0.0).astype(jnp.bfloat16)

    def part(i, q):
        some = pl.ds(128 * q, 128)
        return pltpu.make_async_copy(stage.at[i, some], out.at[some, i], out_sem.at[4 * i + q])

    def step(j, carry):
        for k in range(2):
            i = 2 * j + k
            for r in range(4 * AREAS // ROWS):
                left = lhs[pl.ds(r * ROWS, ROWS)]
                parts = []
                for h in range(2):
                    acc = jnp.dot(left, slab[i, :, pl.ds(2 * LANES * h, 2 * LANES)],
                                  preferred_element_type=jnp.float32)
                    acc = (acc * (1.0 / (M - 1))).reshape(ROWS // 8, 8, 2 * LANES)
                    both = swap_halves(acc[:, :, :LANES], acc[:, :, LANES:])
                    parts.append(jnp.stack(both, axis=1).reshape(areas, 8, LANES))
                done = jnp.stack(parts, axis=1).reshape(areas, 16, LANES)
                stage[i, pl.ds(r * areas, areas)] = done.astype(jnp.bfloat16)
                if (r + 1) * areas % 128 == 0:
                    part(i, r * areas // 128).start()
        return carry

    lax.fori_loop(0, QUADS // 2, step, 0)

    def finish(i, carry):
        for q in range(4):
            part(i, q).wait()
        return carry

    lax.fori_loop(0, QUADS, finish, 0)


def product(metric, slab):
    any_space = pl.BlockSpec(memory_space=pl.ANY)
    dma = pltpu.SemaphoreType.DMA
    return pl.pallas_call(
        product_kernel,
        out_shape=jax.ShapeDtypeStruct((AREAS, QUADS, 16, LANES), jnp.bfloat16),
        in_specs=[pl.BlockSpec(memory_space=pltpu.VMEM)] * 2,
        out_specs=any_space,
        scratch_shapes=[
            pltpu.VMEM((AREAS, 4 * M), jnp.bfloat16),
            pltpu.VMEM((4 * AREAS, 4 * M), jnp.bfloat16),
            pltpu.VMEM((QUADS, AREAS, 16, LANES), jnp.bfloat16),
            dma((32,)),
        ],
        compiler_params=pltpu.CompilerParams(vmem_limit_bytes=32 * 2**20),
        cost_estimate=pl.CostEstimate(
            flops=2 * 2048 * 192 * 4096, bytes_accessed=20 * 2**20, transcendentals=0),
        name="product",
    )(metric, slab)


def body(tiles, farm_area, capacity, offsets, state):
    by_member = jnp.transpose(tiles, (1, 2, 0))
    columns = state.reshape(M, 2, 64, LANES)
    columns = jnp.transpose(columns, (0, 2, 1, 3)).reshape(M, QUADS, 16, LANES)
    metric, slab = exchange(
        by_member, farm_area.reshape(1, F), capacity.reshape(1, F), offsets, columns)
    out = product(metric, slab)
    out = jnp.transpose(out.reshape(AREAS, 64, 2, LANES), (0, 2, 1, 3))
    return out.reshape(AREAS, 2, 64 * LANES)


def solution(mesh):
    in_specs = (P("grid", None, None), P("grid"), P("grid"), P("grid"), P(None, "lev", "grid"))
    out_specs = P(None, "lev", "grid")
    return jax.shard_map(body, mesh=mesh, in_specs=in_specs, out_specs=out_specs, check_vma=False)
```

```python
import jax
import jax.numpy as jnp
from jax import lax
from jax.experimental import pallas as pl
from jax.experimental.pallas import tpu as pltpu
from jax.sharding import PartitionSpec as P

MESH = pl.DeviceIdType.MESH
M = 48
T = 144
F = 256
AREAS = 512
LANES = 128
RING = 4
PAD_X = 160
ROWS_Z = 80
PAD_Z = 96
HALF = 64
RAMPS = 132
RAMPS_Z = 68
KEEP_X = 152
KEEP_Z = 88
QUADS = 8
ROWS = 256
capacity_floor = 200.0
spread_floor = 0.05


def iota(shape, dim):
    return lax.broadcasted_iota(jnp.int32, shape, dim)


def swap_halves(u, v):
    low = iota(u.shape, 1) < 4
    first = jnp.where(low, u, pltpu.roll(v, 4, 1))
    second = jnp.where(low, pltpu.roll(u, 4, 1), v)
    return first, second


def ramp_metric(summed, steps, offset, ramps):
    total = jnp.maximum(summed[steps : steps + 1], capacity_floor)
    power = summed[:steps] / total
    wide = jnp.broadcast_to(offset, power.shape).astype(jnp.int32)
    later = power
    for bit in (1, 2, 4, 8):
        later = jnp.where((wide & bit) != 0, pltpu.roll(later, steps - bit, 0), later)
    row = iota(power.shape, 0)
    return jnp.max(jnp.where(row < ramps, later - power, -3e38), axis=0, keepdims=True)


STEP = (0, 0, 1, 1, 3, 3, 2, 2)
BACK = (0, 1, 4, 5, 2, 3, 6, 7)
ORDER = (6, 7, 2, 4, 3, 5, 1)
FIRST = 80
HALVES = (pl.ds(0, FIRST), pl.ds(FIRST, T - FIRST))


def exchange_kernel(
    tiles, farm_area, capacity, offsets, state, metric_out, slab_out,
    area_in, capacity_in, offsets_in,
    facts_x, facts_z, got_x, got_z, weight_x, weight_z,
    part_x, part_z, sum_x, sum_z, off_x, off_z,
    small, gathered, z_rows, st,
    local_sem, fx_send, fx_recv, fz_send, fz_recv, x_send, x_recv, z_send, z_recv,
    bx_send, bx_recv, bz_send, bz_recv,
    s1_send, s1_recv, s2_send, s2_recv,
):
    g = lax.axis_index("grid")
    y = lax.axis_index("lev")
    z = lax.div(g, 8)
    x = lax.rem(lax.div(g, 2), 4)
    c = lax.rem(g, 2)
    mine_x = 2 * x + c
    mine_z = 2 * z + c
    xs = [x] + [lax.rem(x + d, 4) for d in range(1, 4)]
    zs = [z] + [lax.rem(z + d, 4) for d in range(1, 4)]
    ys = [y] + [lax.rem(y + d, 4) for d in range(1, 4)]
    cs = [c, 1 - c]

    def device(xx, zz, cc, yy):
        return (zz * 8 + xx * 2 + cc, yy)

    sibling = device(x, z, 1 - c, y)
    x_peers = [(xs[STEP[i]], cs[i % 2]) for i in range(8)]
    z_peers = [(zs[STEP[i]], cs[i % 2]) for i in range(8)]

    def remote(src, dst, send_sem, recv_sem, to):
        return pltpu.make_async_remote_copy(
            src_ref=src, dst_ref=dst, send_sem=send_sem, recv_sem=recv_sem,
            device_id=to, device_id_type=MESH)

    def wait_for(slot, send, recv):
        remote(slot, slot, send, recv, sibling).wait_recv()

    def loop(first, last):
        def run(body):
            lax.fori_loop(first, last, lambda i, carry: (body(i), carry)[1], 0)
        return run

    barrier = pltpu.get_barrier_semaphore()

    def greet(to):
        pl.semaphore_signal(barrier, inc=1, device_id=to, device_id_type=MESH)

    for i in ORDER:
        xx, cc = x_peers[i]
        greet(device(xx, z, cc, y))
        if i != 1:
            zz, cc = z_peers[i]
            greet(device(x, zz, cc, y))
    for d in (2, 1, 3):
        greet(device(x, z, c, ys[d]))

    def x_slot(i, half):
        return got_x.at[HALVES[half], pl.ds(F * i, F)]

    def z_slot(i):
        return got_z.at[pl.ds(0, ROWS_Z), pl.ds(F * i, F)]

    def x_tile(xx, cc):
        return tiles.at[12 * y + 2 * xx + cc]

    def z_tile(zz, cc):
        return tiles.at[12 * y + 8 + zz, pl.ds(pl.multiple_of(HALF * cc, HALF), ROWS_Z)]

    local = [
        pltpu.make_async_copy(farm_area, area_in, local_sem.at[0]),
        pltpu.make_async_copy(capacity, capacity_in, local_sem.at[1]),
        pltpu.make_async_copy(offsets, offsets_in, local_sem.at[2]),
        pltpu.make_async_copy(z_tile(z, c), z_slot(0), local_sem.at[3]),
        pltpu.make_async_copy(x_tile(x, c), got_x.at[pl.ds(0, T), pl.ds(0, F)], local_sem.at[4]),
        pltpu.make_async_copy(state, st, local_sem.at[5]),
    ]
    for copy in local:
        copy.start()
    pl.semaphore_wait(barrier, 16)

    def fx_copy(i):
        xx, cc = x_peers[i]
        return remote(facts_x.at[0], facts_x.at[BACK[i]], fx_send.at[i], fx_recv.at[BACK[i]],
                      device(xx, z, cc, y))

    def fz_copy(i):
        zz, cc = z_peers[i]
        return remote(facts_z.at[0], facts_z.at[BACK[i]], fz_send.at[i], fz_recv.at[BACK[i]],
                      device(x, zz, cc, y))

    def x_copy(i, half):
        xx, cc = x_peers[i]
        return remote(x_tile(xx, cc).at[HALVES[half]], x_slot(BACK[i], half),
                      x_send.at[half, i], x_recv.at[half, BACK[i]], device(xx, z, cc, y))

    def z_copy(i):
        zz, cc = z_peers[i]
        return remote(z_tile(zz, cc), z_slot(BACK[i]), z_send.at[i], z_recv.at[BACK[i]],
                      device(x, zz, cc, y))

    sends = []

    def start(*copies):
        for copy in copies:
            copy.start()
            sends.append(copy)

    start(x_copy(6, 0), x_copy(7, 0), z_copy(6), z_copy(7))
    for copy in local[:3]:
        copy.wait()

    lane = iota((1, F), 1)
    offset = jnp.zeros((1, F), jnp.int32)
    for k in range(16):
        offset = jnp.where((lane & 15) == k, offsets_in[k], offset)
    area = area_in[...]
    turned = ((area >> 5) & 3) * 128 + (area >> 7) * 32 + (area & 31)
    for facts, ids, spot in ((facts_z, turned, mine_z), (facts_x, area, mine_x)):
        placed = jnp.where((lane >> 4) == spot, offset, 0)
        rows = jnp.concatenate(
            [ids, capacity_in[...], placed, jnp.zeros((1, F), jnp.int32)], axis=0)
        facts[0] = rows.astype(jnp.float32)

    for i in ORDER:
        start(fz_copy(i), fx_copy(i))
    for i in ORDER[2:]:
        start(x_copy(i, 0), z_copy(i))

    for i in ORDER:
        start(x_copy(i, 1))

    got_x[pl.ds(T, 16)] = jnp.ones((16, 8 * F), jnp.bfloat16)
    got_z[pl.ds(ROWS_Z, 16)] = jnp.ones((16, 8 * F), jnp.bfloat16)
    off_x[...] = jnp.zeros_like(off_x)
    off_z[...] = jnp.zeros_like(off_z)
    area_ids = iota((AREAS, F), 0).astype(jnp.float32)

    def weigh(i, facts, weight, off):
        rows = facts[i]
        off[...] = off[...] + rows[2:3, :LANES]
        placed = jnp.where(area_ids == rows[0:1], rows[1:2], 0.0)
        weight[:, pl.ds(pl.multiple_of(F * i, F), F)] = placed.astype(jnp.bfloat16)

    @loop(0, 8)
    def _(i):
        for facts, recv, send, weight, off in (
                (facts_z, fz_recv, fz_send, weight_z, off_z),
                (facts_x, fx_recv, fx_send, weight_x, off_x)):
            @pl.when(i > 0)
            def _():
                wait_for(facts.at[i], send.at[i], recv.at[i])

            weigh(i, facts, weight, off)

    def sum_up(values, weights):
        return lax.dot_general(values, weights, (((1,), (1,)), ((), ())),
                               preferred_element_type=jnp.float32)

    local[3].wait()
    for i in range(1, 8):
        wait_for(z_slot(i), z_send.at[i], z_recv.at[i])
    for h in range(2):
        value = sum_up(got_z[...], weight_z[pl.ds(2 * LANES * h, 2 * LANES)])
        for b in range(2):
            part_z[2 * h + b] = value[:KEEP_Z, b * LANES : (b + 1) * LANES]
    local[4].wait()
    bz, bx = [], []

    def part_copy(d, half, first, count):
        rows = pl.ds(first, count)
        return remote(part_x.at[zs[d], rows], sum_x.at[3 - d, rows], bx_send.at[half, d - 1],
                      bx_recv.at[half, 3 - d], device(x, zs[d], c, y))

    for half, (first, count, keep) in enumerate(
            ((0, FIRST, FIRST), (FIRST, PAD_X - FIRST, KEEP_X - FIRST))):
        for i in range(1, 8):
            wait_for(x_slot(i, half), x_send.at[half, i], x_recv.at[half, i])
        for pair in ((2, 1), (3, 0)):
            chosen = jnp.concatenate(
                [weight_x[pl.ds(pl.multiple_of(LANES * zs[d], LANES), LANES)] for d in pair],
                axis=0)
            value = sum_up(got_x[pl.ds(first, count)], chosen)
            for k, d in enumerate(pair):
                part_x[zs[d], pl.ds(first, keep)] = value[:keep, k * LANES : (k + 1) * LANES]
                if d > 0:
                    bx.append(part_copy(d, half, first, keep))
                    bx[-1].start()
    for d in (2, 1, 3):
        bz.append(remote(part_z.at[xs[d]], sum_z.at[3 - d], bz_send.at[d - 1], bz_recv.at[3 - d],
                         device(xs[d], z, c, y)))
        bz[-1].start()

    local[5].wait()

    @loop(0, QUADS)
    def _(i):
        values = st[:, i].astype(jnp.float32).reshape(M, 2, 8, LANES)
        values = values - (jnp.sum(values, axis=0) / M)[None]
        pairs = values.reshape(M // 2, 2, 2, 8, LANES)
        for h in range(2):
            both = swap_halves(pairs[:, 0, h], pairs[:, 1, h])
            for k in range(2):
                slab_out[i, :, pl.ds((2 * h + k) * LANES, LANES)] = (
                    both[k].reshape(4 * M, LANES).astype(jnp.bfloat16))

    for copy in bz:
        copy.wait_recv()
    summed = part_z[x] + sum_z[0] + sum_z[1] + sum_z[2]
    small[mine_x, pl.ds(1, 1)] = ramp_metric(summed, ROWS_Z, off_z[...], RAMPS_Z)

    for copy in bx:
        copy.wait_recv()

    summed = part_x[z] + sum_x[0] + sum_x[1] + sum_x[2]
    small[mine_x, pl.ds(0, 1)] = ramp_metric(summed, T, off_x[...], RAMPS)

    def swap(ref, slot, far, send_sem, recv_sem, to):
        copy = remote(ref.at[slot], ref.at[slot], send_sem, recv_sem.at[slot], to)
        copy.start()
        sends.append(copy)
        return remote(ref.at[far], ref.at[far], send_sem, recv_sem.at[far], to)

    back = []
    for i in ORDER:
        xx, cc = x_peers[i]
        back.append(swap(small, mine_x, 2 * xx + cc, s1_send.at[i], s1_recv,
                         device(xx, z, cc, y)))
    for copy in reversed(back):
        copy.wait_recv()

    joined = gathered.at[y, z]
    for s in range(8):
        joined[s // 4, pl.ds(s % 4, 1)] = small[s, pl.ds(0, 1)]
    for b in range(RING):
        joined[2, pl.ds(b, 1)] = jnp.maximum(
            small[2 * b, pl.ds(1, 1)], small[2 * b + 1, pl.ds(1, 1)])

    sends_now = [(dy, dz) for dy in (2, 1, 3, 0) for dz in (2, 1, 3, 0)][:-1]
    back = []
    for k, (dy, dz) in enumerate(sends_now):
        out = remote(joined, joined, s2_send.at[k], s2_recv.at[4 * y + z],
                     device(x, zs[dz], c, ys[dy]))
        out.start()
        sends.append(out)
        slot = gathered.at[ys[dy], zs[dz]]
        back.append((slot, s2_send.at[k], s2_recv.at[4 * ys[dy] + zs[dz]]))
    for slot, send, recv in reversed(back):
        wait_for(slot, send, recv)

    for zz in range(4):
        for yy in range(4):
            slot = 4 * yy + zz
            for h in range(2):
                metric_out[pl.ds(8 * yy + 4 * h, 4), pl.ds(zz * LANES, LANES)] = gathered[yy, zz, h]
            for b in range(RING):
                z_rows[b, pl.ds(slot, 1)] = gathered[yy, zz, 2, pl.ds(b, 1)]
    quarter = iota((16, LANES), 1) >> 5
    blocks = [z_rows[b] for b in range(RING)]
    for zz in range(4):
        value = jnp.zeros((16, LANES), jnp.float32)
        for b in range(RING):
            move = (32 * (b - zz)) % LANES
            moved = pltpu.roll(blocks[b], move, 1) if move else blocks[b]
            value = jnp.where(quarter == b, moved, value)
        metric_out[pl.ds(32, 16), pl.ds(zz * LANES, LANES)] = value

    for copy in sends + bx + bz:
        copy.wait_send()


def exchange(tiles, farm_area, capacity, offsets, state):
    any_space = pl.BlockSpec(memory_space=pl.ANY)
    vmem = pl.BlockSpec(memory_space=pltpu.VMEM)
    dma = pltpu.SemaphoreType.DMA
    f32, bf16 = jnp.float32, jnp.bfloat16
    return pl.pallas_call(
        exchange_kernel,
        out_shape=(
            pltpu.VMEM((M, AREAS), f32),
            pltpu.VMEM((QUADS, 4 * M, 4 * LANES), bf16),
        ),
        in_specs=[any_space] * 5,
        out_specs=(vmem, vmem),
        scratch_shapes=[
            pltpu.VMEM((1, F), jnp.int32),
            pltpu.VMEM((1, F), jnp.int32),
            pltpu.SMEM((16,), jnp.int32),
            pltpu.VMEM((8, 4, F), f32),
            pltpu.VMEM((8, 4, F), f32),
            pltpu.VMEM((PAD_X, 8 * F), bf16),
            pltpu.VMEM((PAD_Z, 8 * F), bf16),
            pltpu.VMEM((AREAS, 8 * F), bf16),
            pltpu.VMEM((AREAS, 8 * F), bf16),
            pltpu.VMEM((RING, KEEP_X, LANES), f32),
            pltpu.VMEM((RING, KEEP_Z, LANES), f32),
            pltpu.VMEM((3, KEEP_X, LANES), f32),
            pltpu.VMEM((3, KEEP_Z, LANES), f32),
            pltpu.VMEM((1, LANES), f32),
            pltpu.VMEM((1, LANES), f32),
            pltpu.VMEM((8, 2, LANES), f32),
            pltpu.VMEM((4, 4, 3, 4, LANES), f32),
            pltpu.VMEM((RING, 16, LANES), f32),
            pltpu.VMEM((M, QUADS, 16, LANES), bf16),
            dma((6,)), dma((8,)), dma((8,)), dma((8,)), dma((8,)),
            dma((2, 8)), dma((2, 8)), dma((8,)), dma((8,)),
            dma((2, 3)), dma((2, 3)), dma((3,)), dma((3,)),
            dma((8,)), dma((8,)), dma((16,)), dma((16,)),
        ],
        compiler_params=pltpu.CompilerParams(
            collective_id=0, has_side_effects=True, vmem_limit_bytes=60 * 2**20),
        cost_estimate=pl.CostEstimate(
            flops=2 * 256 * 2048 * 512, bytes_accessed=5 * 2**20, transcendentals=0),
        name="exchange",
    )(tiles, farm_area, capacity, offsets, state)


def product_kernel(metric, slab, out, wide, lhs, stage, out_sem):
    values = metric[...]
    anomaly = values - jnp.mean(values, axis=0, keepdims=True)
    spread = jnp.sqrt(jnp.sum(anomaly * anomaly, axis=0, keepdims=True) / (M - 1))
    scores = anomaly / jnp.maximum(spread, spread_floor)
    scores = jnp.transpose(scores).astype(jnp.bfloat16)

    held = iota((M, 4 * M), 0)
    rest = held - 32
    member = jnp.where(
        held < 32,
        12 * (held >> 3) + (held & 7),
        12 * (rest >> 2) + 8 + (rest & 3))
    widen = ((iota((M, 4 * M), 1) >> 2) == member).astype(jnp.bfloat16)
    wide[...] = jnp.dot(scores, widen, preferred_element_type=jnp.float32).astype(jnp.bfloat16)
    repeat = ((iota((ROWS, ROWS // 4), 0) >> 2) == iota((ROWS, ROWS // 4), 1)).astype(
        jnp.bfloat16)
    keep = (iota((ROWS, 4 * M), 0) & 3) == (iota((ROWS, 4 * M), 1) & 3)
    areas = ROWS // 4

    def make(r):
        rows = jnp.dot(repeat, wide[pl.ds(r * areas, areas)], preferred_element_type=jnp.float32)
        left = jnp.where(keep, rows, 0.0).astype(jnp.bfloat16)
        lhs[pl.ds(r * ROWS, ROWS)] = left
        return left

    def part(i, q):
        some = pl.ds(128 * q, 128)
        return pltpu.make_async_copy(stage.at[i, some], out.at[some, i], out_sem.at[4 * i + q])

    def step(j, carry, fresh=False):
        for k in range(2):
            i = 2 * j + k
            for r in range(4 * AREAS // ROWS):
                left = make(r) if fresh and k == 0 else lhs[pl.ds(r * ROWS, ROWS)]
                parts = []
                for h in range(2):
                    acc = jnp.dot(left, slab[i, :, pl.ds(2 * LANES * h, 2 * LANES)],
                                  preferred_element_type=jnp.float32)
                    acc = (acc * (1.0 / (M - 1))).reshape(ROWS // 8, 8, 2 * LANES)
                    both = swap_halves(acc[:, :, :LANES], acc[:, :, LANES:])
                    parts.append(jnp.stack(both, axis=1).reshape(areas, 8, LANES))
                done = jnp.stack(parts, axis=1).reshape(areas, 16, LANES)
                stage[i, pl.ds(r * areas, areas)] = done.astype(jnp.bfloat16)
                if (r + 1) * areas % 128 == 0:
                    part(i, r * areas // 128).start()
        return carry

    step(0, 0, fresh=True)
    lax.fori_loop(1, QUADS // 2, step, 0)

    def finish(i, carry):
        for q in range(4):
            part(i, q).wait()
        return carry

    lax.fori_loop(0, QUADS, finish, 0)


def product(metric, slab):
    any_space = pl.BlockSpec(memory_space=pl.ANY)
    dma = pltpu.SemaphoreType.DMA
    return pl.pallas_call(
        product_kernel,
        out_shape=jax.ShapeDtypeStruct((AREAS, QUADS, 16, LANES), jnp.bfloat16),
        in_specs=[pl.BlockSpec(memory_space=pltpu.VMEM)] * 2,
        out_specs=any_space,
        scratch_shapes=[
            pltpu.VMEM((AREAS, 4 * M), jnp.bfloat16),
            pltpu.VMEM((4 * AREAS, 4 * M), jnp.bfloat16),
            pltpu.VMEM((QUADS, AREAS, 16, LANES), jnp.bfloat16),
            dma((32,)),
        ],
        compiler_params=pltpu.CompilerParams(vmem_limit_bytes=32 * 2**20),
        cost_estimate=pl.CostEstimate(
            flops=2 * 2048 * 192 * 4096, bytes_accessed=20 * 2**20, transcendentals=0),
        name="product",
    )(metric, slab)


def body(tiles, farm_area, capacity, offsets, state):
    by_member = jnp.transpose(tiles, (1, 2, 0))
    columns = state.reshape(M, 2, 64, LANES)
    columns = jnp.transpose(columns, (0, 2, 1, 3)).reshape(M, QUADS, 16, LANES)
    metric, slab = exchange(
        by_member, farm_area.reshape(1, F), capacity.reshape(1, F), offsets, columns)
    out = product(metric, slab)
    out = jnp.transpose(out.reshape(AREAS, 64, 2, LANES), (0, 2, 1, 3))
    return out.reshape(AREAS, 2, 64 * LANES)


def solution(mesh):
    in_specs = (P("grid", None, None), P("grid"), P("grid"), P("grid"), P(None, "lev", "grid"))
    out_specs = P(None, "lev", "grid")
    return jax.shard_map(body, mesh=mesh, in_specs=in_specs, out_specs=out_specs, check_vma=False)
```

```python
import jax
import jax.numpy as jnp
from jax import lax
from jax.experimental import pallas as pl
from jax.experimental.pallas import tpu as pltpu
from jax.sharding import PartitionSpec as P

MESH = pl.DeviceIdType.MESH
M = 48
T = 144
F = 256
AREAS = 512
LANES = 128
RING = 4
PAD_X = 160
ROWS_Z = 80
PAD_Z = 96
HALF = 64
RAMPS = 132
RAMPS_Z = 68
KEEP_X = 152
KEEP_Z = 88
QUADS = 8
ROWS = 256
capacity_floor = 200.0
spread_floor = 0.05


def iota(shape, dim):
    return lax.broadcasted_iota(jnp.int32, shape, dim)


def swap_halves(u, v):
    low = iota(u.shape, 1) < 4
    crossed = pltpu.roll(jnp.where(low, v, u), 4, 1)
    return jnp.where(low, u, crossed), jnp.where(low, crossed, v)


def ramp_metric(summed, steps, offset, ramps):
    total = jnp.maximum(summed[steps : steps + 1], capacity_floor)
    power = summed[:steps] / total
    wide = jnp.broadcast_to(offset, power.shape).astype(jnp.int32)
    later = power
    for bit in (1, 2, 4, 8):
        later = jnp.where((wide & bit) != 0, pltpu.roll(later, steps - bit, 0), later)
    row = iota(power.shape, 0)
    return jnp.max(jnp.where(row < ramps, later - power, -3e38), axis=0, keepdims=True)


STEP = (0, 0, 1, 1, 3, 3, 2, 2)
BACK = (0, 1, 4, 5, 2, 3, 6, 7)
ORDER = (6, 7, 2, 4, 3, 5, 1)
FIRST = 96
HALVES = (pl.ds(0, FIRST), pl.ds(FIRST, T - FIRST))


def exchange_kernel(
    tiles, farm_area, capacity, offsets, state, metric_out, slab_out,
    area_in, capacity_in, offsets_in,
    facts_x, facts_z, got_x, got_z, weight_x, weight_z,
    part_x, part_z, sum_x, sum_z, off_x, off_z,
    small, gathered, z_rows, st,
    local_sem, fx_send, fx_recv, fz_send, fz_recv, x_send, x_recv, z_send, z_recv,
    bx_send, bx_recv, bz_send, bz_recv,
    s1_send, s1_recv, s2_send, s2_recv,
):
    g = lax.axis_index("grid")
    y = lax.axis_index("lev")
    z = lax.div(g, 8)
    x = lax.rem(lax.div(g, 2), 4)
    c = lax.rem(g, 2)
    mine_x = 2 * x + c
    mine_z = 2 * z + c
    xs = [x] + [lax.rem(x + d, 4) for d in range(1, 4)]
    zs = [z] + [lax.rem(z + d, 4) for d in range(1, 4)]
    ys = [y] + [lax.rem(y + d, 4) for d in range(1, 4)]
    cs = [c, 1 - c]

    def device(xx, zz, cc, yy):
        return (zz * 8 + xx * 2 + cc, yy)

    sibling = device(x, z, 1 - c, y)
    x_peers = [(xs[STEP[i]], cs[i % 2]) for i in range(8)]
    z_peers = [(zs[STEP[i]], cs[i % 2]) for i in range(8)]

    def remote(src, dst, send_sem, recv_sem, to):
        return pltpu.make_async_remote_copy(
            src_ref=src, dst_ref=dst, send_sem=send_sem, recv_sem=recv_sem,
            device_id=to, device_id_type=MESH)

    def wait_for(slot, send, recv):
        remote(slot, slot, send, recv, sibling).wait_recv()

    def loop(first, last):
        def run(body):
            lax.fori_loop(first, last, lambda i, carry: (body(i), carry)[1], 0)
        return run

    barrier = pltpu.get_barrier_semaphore()

    def greet(to):
        pl.semaphore_signal(barrier, inc=1, device_id=to, device_id_type=MESH)

    for i in ORDER:
        xx, cc = x_peers[i]
        greet(device(xx, z, cc, y))
        if i != 1:
            zz, cc = z_peers[i]
            greet(device(x, zz, cc, y))
    for d in (2, 1, 3):
        greet(device(x, z, c, ys[d]))

    def x_slot(i, half):
        return got_x.at[HALVES[half], pl.ds(F * i, F)]

    def z_slot(i):
        return got_z.at[pl.ds(0, ROWS_Z), pl.ds(F * i, F)]

    def x_tile(xx, cc):
        return tiles.at[12 * y + 2 * xx + cc]

    def z_tile(zz, cc):
        return tiles.at[12 * y + 8 + zz, pl.ds(pl.multiple_of(HALF * cc, HALF), ROWS_Z)]

    local = [
        pltpu.make_async_copy(farm_area, area_in, local_sem.at[0]),
        pltpu.make_async_copy(capacity, capacity_in, local_sem.at[1]),
        pltpu.make_async_copy(offsets, offsets_in, local_sem.at[2]),
        pltpu.make_async_copy(z_tile(z, c), z_slot(0), local_sem.at[3]),
        pltpu.make_async_copy(x_tile(x, c), got_x.at[pl.ds(0, T), pl.ds(0, F)], local_sem.at[4]),
        pltpu.make_async_copy(state, st, local_sem.at[5]),
    ]
    for copy in local:
        copy.start()
    pl.semaphore_wait(barrier, 16)

    def fx_copy(i):
        xx, cc = x_peers[i]
        return remote(facts_x.at[0], facts_x.at[BACK[i]], fx_send.at[i], fx_recv.at[BACK[i]],
                      device(xx, z, cc, y))

    def fz_copy(i):
        zz, cc = z_peers[i]
        return remote(facts_z.at[0], facts_z.at[BACK[i]], fz_send.at[i], fz_recv.at[BACK[i]],
                      device(x, zz, cc, y))

    def x_copy(i, half):
        xx, cc = x_peers[i]
        return remote(x_tile(xx, cc).at[HALVES[half]], x_slot(BACK[i], half),
                      x_send.at[half, i], x_recv.at[half, BACK[i]], device(xx, z, cc, y))

    def z_copy(i):
        zz, cc = z_peers[i]
        return remote(z_tile(zz, cc), z_slot(BACK[i]), z_send.at[i], z_recv.at[BACK[i]],
                      device(x, zz, cc, y))

    sends = []

    def start(*copies):
        for copy in copies:
            copy.start()
            sends.append(copy)

    start(x_copy(6, 0), x_copy(7, 0), z_copy(6), z_copy(7))
    for copy in local[:3]:
        copy.wait()

    lane = iota((1, F), 1)
    offset = jnp.zeros((1, F), jnp.int32)
    for k in range(16):
        offset = jnp.where((lane & 15) == k, offsets_in[k], offset)
    area = area_in[...]
    turned = ((area >> 5) & 3) * 128 + (area >> 7) * 32 + (area & 31)
    for facts, ids, spot in ((facts_z, turned, mine_z), (facts_x, area, mine_x)):
        placed = jnp.where((lane >> 4) == spot, offset, 0)
        rows = jnp.concatenate(
            [ids, capacity_in[...], placed, jnp.zeros((1, F), jnp.int32)], axis=0)
        facts[0] = rows.astype(jnp.float32)

    for i in ORDER:
        start(fz_copy(i), fx_copy(i))
    for i in ORDER[2:]:
        start(x_copy(i, 0), z_copy(i))

    for i in ORDER:
        start(x_copy(i, 1))

    got_x[pl.ds(T, 16)] = jnp.ones((16, 8 * F), jnp.bfloat16)
    got_z[pl.ds(ROWS_Z, 16)] = jnp.ones((16, 8 * F), jnp.bfloat16)
    off_x[...] = jnp.zeros_like(off_x)
    off_z[...] = jnp.zeros_like(off_z)
    area_ids = iota((AREAS, F), 0).astype(jnp.float32)

    def weigh(i, facts, weight, off):
        rows = facts[i]
        off[...] = off[...] + rows[2:3, :LANES]
        placed = jnp.where(area_ids == rows[0:1], rows[1:2], 0.0)
        weight[:, pl.ds(pl.multiple_of(F * i, F), F)] = placed.astype(jnp.bfloat16)

    @loop(0, 8)
    def _(i):
        for facts, recv, send, weight, off in (
                (facts_z, fz_recv, fz_send, weight_z, off_z),
                (facts_x, fx_recv, fx_send, weight_x, off_x)):
            @pl.when(i > 0)
            def _():
                wait_for(facts.at[i], send.at[i], recv.at[i])

            weigh(i, facts, weight, off)

    def sum_up(values, weights):
        return lax.dot_general(values, weights, (((1,), (1,)), ((), ())),
                               preferred_element_type=jnp.float32)

    local[3].wait()
    for i in range(1, 8):
        wait_for(z_slot(i), z_send.at[i], z_recv.at[i])
    for h in range(2):
        value = sum_up(got_z[...], weight_z[pl.ds(2 * LANES * h, 2 * LANES)])
        for b in range(2):
            part_z[2 * h + b] = value[:KEEP_Z, b * LANES : (b + 1) * LANES]
    local[4].wait()
    bz, bx = [], []

    def part_copy(d, half, first, count):
        rows = pl.ds(first, count)
        return remote(part_x.at[zs[d], rows], sum_x.at[3 - d, rows], bx_send.at[half, d - 1],
                      bx_recv.at[half, 3 - d], device(x, zs[d], c, y))

    for half, (first, count, keep) in enumerate(
            ((0, FIRST, FIRST), (FIRST, PAD_X - FIRST, KEEP_X - FIRST))):
        for i in range(1, 8):
            wait_for(x_slot(i, half), x_send.at[half, i], x_recv.at[half, i])
        if half == 1:
            for d in (2, 1, 3):
                bz.append(remote(part_z.at[xs[d]], sum_z.at[3 - d], bz_send.at[d - 1], bz_recv.at[3 - d],
                                 device(xs[d], z, c, y)))
                bz[-1].start()
        for pair in ((2, 1), (3, 0)):
            chosen = jnp.concatenate(
                [weight_x[pl.ds(pl.multiple_of(LANES * zs[d], LANES), LANES)] for d in pair],
                axis=0)
            value = sum_up(got_x[pl.ds(first, count)], chosen)
            for k, d in enumerate(pair):
                part_x[zs[d], pl.ds(first, keep)] = value[:keep, k * LANES : (k + 1) * LANES]
                if d > 0:
                    bx.append(part_copy(d, half, first, keep))
                    bx[-1].start()
    local[5].wait()

    @loop(0, QUADS)
    def _(i):
        values = st[:, i].astype(jnp.float32).reshape(M, 2, 8, LANES)
        values = values - (jnp.sum(values, axis=0) / M)[None]
        pairs = values.reshape(M // 2, 2, 2, 8, LANES)
        for h in range(2):
            both = swap_halves(pairs[:, 0, h], pairs[:, 1, h])
            for k in range(2):
                slab_out[i, :, pl.ds((2 * h + k) * LANES, LANES)] = (
                    both[k].reshape(4 * M, LANES).astype(jnp.bfloat16))

    for copy in bz:
        copy.wait_recv()
    summed = part_z[x] + sum_z[0] + sum_z[1] + sum_z[2]
    small[mine_x, pl.ds(1, 1)] = ramp_metric(summed, ROWS_Z, off_z[...], RAMPS_Z)

    for copy in bx:
        copy.wait_recv()

    summed = part_x[z] + sum_x[0] + sum_x[1] + sum_x[2]
    small[mine_x, pl.ds(0, 1)] = ramp_metric(summed, T, off_x[...], RAMPS)

    def swap(ref, slot, far, send_sem, recv_sem, to):
        copy = remote(ref.at[slot], ref.at[slot], send_sem, recv_sem.at[slot], to)
        copy.start()
        sends.append(copy)
        return remote(ref.at[far], ref.at[far], send_sem, recv_sem.at[far], to)

    back = []
    for i in ORDER:
        xx, cc = x_peers[i]
        back.append(swap(small, mine_x, 2 * xx + cc, s1_send.at[i], s1_recv,
                         device(xx, z, cc, y)))
    for copy in reversed(back):
        copy.wait_recv()

    joined = gathered.at[y, z]
    for s in range(8):
        joined[s // 4, pl.ds(s % 4, 1)] = small[s, pl.ds(0, 1)]
    for b in range(RING):
        joined[2, pl.ds(b, 1)] = jnp.maximum(
            small[2 * b, pl.ds(1, 1)], small[2 * b + 1, pl.ds(1, 1)])

    older = sends + bx + bz
    sends = []
    sends_now = [(dy, dz) for dy in (2, 1, 3, 0) for dz in (2, 1, 3, 0)][:-1]
    back = []
    for k, (dy, dz) in enumerate(sends_now):
        out = remote(joined, joined, s2_send.at[k], s2_recv.at[4 * y + z],
                     device(x, zs[dz], c, ys[dy]))
        out.start()
        sends.append(out)
        back.append((dy, dz, s2_send.at[k], s2_recv.at[4 * ys[dy] + zs[dz]]))
    for copy in older:
        copy.wait_send()

    def place(yy, zz):
        lanes = pl.ds(pl.multiple_of(LANES * zz, LANES), LANES)
        rows = pl.ds(pl.multiple_of(8 * yy, 8), 8)
        metric_out[rows, lanes] = gathered[yy, zz, pl.ds(0, 2)].reshape(8, LANES)
        for b in range(RING):
            z_rows[b, pl.ds(4 * yy + zz, 1)] = gathered[yy, zz, 2, pl.ds(b, 1)]

    place(y, z)
    for dy, dz, send, recv in reversed(back):
        wait_for(gathered.at[ys[dy], zs[dz]], send, recv)
        place(ys[dy], zs[dz])
    quarter = iota((16, LANES), 1) >> 5
    blocks = [z_rows[b] for b in range(RING)]
    for zz in range(4):
        value = jnp.zeros((16, LANES), jnp.float32)
        for b in range(RING):
            move = (32 * (b - zz)) % LANES
            moved = pltpu.roll(blocks[b], move, 1) if move else blocks[b]
            value = jnp.where(quarter == b, moved, value)
        metric_out[pl.ds(32, 16), pl.ds(zz * LANES, LANES)] = value

    for copy in sends:
        copy.wait_send()


def exchange(tiles, farm_area, capacity, offsets, state):
    any_space = pl.BlockSpec(memory_space=pl.ANY)
    vmem = pl.BlockSpec(memory_space=pltpu.VMEM)
    dma = pltpu.SemaphoreType.DMA
    f32, bf16 = jnp.float32, jnp.bfloat16
    return pl.pallas_call(
        exchange_kernel,
        out_shape=(
            pltpu.VMEM((M, AREAS), f32),
            pltpu.VMEM((QUADS, 4 * M, 4 * LANES), bf16),
        ),
        in_specs=[any_space] * 5,
        out_specs=(vmem, vmem),
        scratch_shapes=[
            pltpu.VMEM((1, F), jnp.int32),
            pltpu.VMEM((1, F), jnp.int32),
            pltpu.SMEM((16,), jnp.int32),
            pltpu.VMEM((8, 4, F), f32),
            pltpu.VMEM((8, 4, F), f32),
            pltpu.VMEM((PAD_X, 8 * F), bf16),
            pltpu.VMEM((PAD_Z, 8 * F), bf16),
            pltpu.VMEM((AREAS, 8 * F), bf16),
            pltpu.VMEM((AREAS, 8 * F), bf16),
            pltpu.VMEM((RING, KEEP_X, LANES), f32),
            pltpu.VMEM((RING, KEEP_Z, LANES), f32),
            pltpu.VMEM((3, KEEP_X, LANES), f32),
            pltpu.VMEM((3, KEEP_Z, LANES), f32),
            pltpu.VMEM((1, LANES), f32),
            pltpu.VMEM((1, LANES), f32),
            pltpu.VMEM((8, 2, LANES), f32),
            pltpu.VMEM((4, 4, 3, 4, LANES), f32),
            pltpu.VMEM((RING, 16, LANES), f32),
            pltpu.VMEM((M, QUADS, 16, LANES), bf16),
            dma((6,)), dma((8,)), dma((8,)), dma((8,)), dma((8,)),
            dma((2, 8)), dma((2, 8)), dma((8,)), dma((8,)),
            dma((2, 3)), dma((2, 3)), dma((3,)), dma((3,)),
            dma((8,)), dma((8,)), dma((16,)), dma((16,)),
        ],
        compiler_params=pltpu.CompilerParams(
            collective_id=0, has_side_effects=True, vmem_limit_bytes=60 * 2**20),
        cost_estimate=pl.CostEstimate(
            flops=2 * 256 * 2048 * 512, bytes_accessed=5 * 2**20, transcendentals=0),
        name="exchange",
    )(tiles, farm_area, capacity, offsets, state)


def product_kernel(metric, slab, out, wide, lhs, stage, out_sem):
    values = metric[...]
    anomaly = values - jnp.mean(values, axis=0, keepdims=True)
    spread = jnp.sqrt(jnp.sum(anomaly * anomaly, axis=0, keepdims=True) / (M - 1))
    scores = anomaly / jnp.maximum(spread, spread_floor)
    scores = jnp.transpose(scores).astype(jnp.bfloat16)

    held = iota((M, 4 * M), 0)
    rest = held - 32
    member = jnp.where(
        held < 32,
        12 * (held >> 3) + (held & 7),
        12 * (rest >> 2) + 8 + (rest & 3))
    widen = ((iota((M, 4 * M), 1) >> 2) == member).astype(jnp.bfloat16)
    wide[...] = jnp.dot(scores, widen, preferred_element_type=jnp.float32).astype(jnp.bfloat16)
    repeat = ((iota((ROWS, ROWS // 4), 0) >> 2) == iota((ROWS, ROWS // 4), 1)).astype(
        jnp.bfloat16)
    keep = (iota((ROWS, 4 * M), 0) & 3) == (iota((ROWS, 4 * M), 1) & 3)
    areas = ROWS // 4

    half = 4 * AREAS // ROWS // 2

    def part(q, i):
        some = pl.ds(pl.multiple_of(2 * areas * q, 2 * areas), 2 * areas)
        return pltpu.make_async_copy(stage.at[some, i], out.at[some, i], out_sem.at[QUADS * q + i])

    def step(q, carry):
        first = [pl.multiple_of((2 * q + r) * areas, areas) for r in range(2)]
        for r in range(2):
            rows = jnp.dot(repeat, wide[pl.ds(first[r], areas)],
                           preferred_element_type=jnp.float32)
            lhs[r] = jnp.where(keep, rows, 0.0).astype(jnp.bfloat16)
        for i in range(QUADS):
            for r in range(2):
                parts = []
                for h in range(2):
                    acc = jnp.dot(lhs[r], slab[i, :, pl.ds(2 * LANES * h, 2 * LANES)],
                                  preferred_element_type=jnp.float32)
                    acc = (acc * (1.0 / (M - 1))).reshape(ROWS // 8, 8, 2 * LANES)
                    both = swap_halves(acc[:, :, :LANES], acc[:, :, LANES:])
                    parts.append(jnp.stack(both, axis=1).reshape(areas, 8, LANES))
                done = jnp.stack(parts, axis=1).reshape(areas, 16, LANES)
                stage[pl.ds(first[r], areas), i] = done.astype(jnp.bfloat16)
            part(q, i).start()
        return carry

    lax.fori_loop(0, half, step, 0)

    def finish(q, carry):
        for i in range(QUADS):
            part(q, i).wait()
        return carry

    lax.fori_loop(0, half, finish, 0)


def product(metric, slab):
    any_space = pl.BlockSpec(memory_space=pl.ANY)
    dma = pltpu.SemaphoreType.DMA
    return pl.pallas_call(
        product_kernel,
        out_shape=jax.ShapeDtypeStruct((AREAS, QUADS, 16, LANES), jnp.bfloat16),
        in_specs=[pl.BlockSpec(memory_space=pltpu.VMEM)] * 2,
        out_specs=any_space,
        scratch_shapes=[
            pltpu.VMEM((AREAS, 4 * M), jnp.bfloat16),
            pltpu.VMEM((2, ROWS, 4 * M), jnp.bfloat16),
            pltpu.VMEM((AREAS, QUADS, 16, LANES), jnp.bfloat16),
            dma((32,)),
        ],
        compiler_params=pltpu.CompilerParams(vmem_limit_bytes=32 * 2**20),
        cost_estimate=pl.CostEstimate(
            flops=2 * 2048 * 192 * 4096, bytes_accessed=20 * 2**20, transcendentals=0),
        name="product",
    )(metric, slab)


def body(tiles, farm_area, capacity, offsets, state):
    by_member = jnp.transpose(tiles, (1, 2, 0))
    columns = state.reshape(M, 2, 64, LANES)
    columns = jnp.transpose(columns, (0, 2, 1, 3)).reshape(M, QUADS, 16, LANES)
    metric, slab = exchange(
        by_member, farm_area.reshape(1, F), capacity.reshape(1, F), offsets, columns)
    out = product(metric, slab)
    out = jnp.transpose(out.reshape(AREAS, 64, 2, LANES), (0, 2, 1, 3))
    return out.reshape(AREAS, 2, 64 * LANES)


def solution(mesh):
    in_specs = (P("grid", None, None), P("grid"), P("grid"), P("grid"), P(None, "lev", "grid"))
    out_specs = P(None, "lev", "grid")
    return jax.shard_map(body, mesh=mesh, in_specs=in_specs, out_specs=out_specs, check_vma=False)
```

```python
import jax
import jax.numpy as jnp
from jax import lax
from jax.experimental import pallas as pl
from jax.experimental.pallas import tpu as pltpu
from jax.sharding import PartitionSpec as P

MESH = pl.DeviceIdType.MESH
M = 48
T = 144
F = 256
AREAS = 512
LANES = 128
RING = 4
ONES = 16
PAD_X = ONES + T
ROWS_Z = 80
PAD_Z = 96
HALF = 64
RAMPS = 132
RAMPS_Z = 68
KEEP_X = 152
KEEP_Z = 88
QUADS = 8
ROWS = 256
capacity_floor = 200.0
spread_floor = 0.05


def iota(shape, dim):
    return lax.broadcasted_iota(jnp.int32, shape, dim)


def swap_halves(u, v):
    low = iota(u.shape, 1) < 4
    crossed = pltpu.roll(jnp.where(low, v, u), 4, 1)
    return jnp.where(low, u, crossed), jnp.where(low, crossed, v)


def ramp_metric(power, offset, first, last):
    steps = power.shape[0]
    wide = jnp.broadcast_to(offset, power.shape).astype(jnp.int32)
    later = power
    for bit in (1, 2, 4, 8):
        later = jnp.where((wide & bit) != 0, pltpu.roll(later, steps - bit, 0), later)
    row = iota(power.shape, 0)
    inside = (row >= first) & (row < last)
    return jnp.max(jnp.where(inside, later - power, -3e38), axis=0, keepdims=True)


STEP = (0, 0, 1, 1, 3, 3, 2, 2)
BACK = (0, 1, 4, 5, 2, 3, 6, 7)
ORDER = (6, 7, 2, 4, 3, 5, 1)
STARTS, ROWS_X = (0, 96), (96, 48)


def exchange_kernel(
    tiles, farm_area, capacity, offsets, state, metric_out, slab_out,
    area_in, capacity_in, offsets_in,
    facts_x, facts_z, got_x, got_z, weight_x, weight_z,
    part_x, part_z, sum_x, sum_z, off_x, off_z,
    metrics, st,
    local_sem, fx_send, fx_recv, fz_send, fz_recv, x_send, x_recv, z_send, z_recv,
    bx_send, bx_recv, bz_send, bz_recv,
    all_send, all_recv,
):
    g = lax.axis_index("grid")
    y = lax.axis_index("lev")
    z = lax.div(g, 8)
    x = lax.rem(lax.div(g, 2), 4)
    c = lax.rem(g, 2)
    mine_x = 2 * x + c
    mine_z = 2 * z + c
    xs = [x] + [lax.rem(x + d, 4) for d in range(1, 4)]
    zs = [z] + [lax.rem(z + d, 4) for d in range(1, 4)]
    ys = [y] + [lax.rem(y + d, 4) for d in range(1, 4)]
    cs = [c, 1 - c]

    def device(xx, zz, cc, yy):
        return (zz * 8 + xx * 2 + cc, yy)

    sibling = device(x, z, 1 - c, y)
    x_peers = [(xs[STEP[i]], cs[i % 2]) for i in range(8)]
    z_peers = [(zs[STEP[i]], cs[i % 2]) for i in range(8)]

    def remote(src, dst, send_sem, recv_sem, to):
        return pltpu.make_async_remote_copy(
            src_ref=src, dst_ref=dst, send_sem=send_sem, recv_sem=recv_sem,
            device_id=to, device_id_type=MESH)

    def wait_for(slot, send, recv):
        remote(slot, slot, send, recv, sibling).wait_recv()

    def loop(first, last):
        def run(body):
            lax.fori_loop(first, last, lambda i, carry: (body(i), carry)[1], 0)
        return run

    barrier = pltpu.get_barrier_semaphore()

    def greet(to):
        pl.semaphore_signal(barrier, inc=1, device_id=to, device_id_type=MESH)

    for i in ORDER:
        xx, cc = x_peers[i]
        greet(device(xx, z, cc, y))
        if i != 1:
            zz, cc = z_peers[i]
            greet(device(x, zz, cc, y))
    for d in (2, 1, 3):
        greet(device(x, z, c, ys[d]))

    def x_slot(i, half):
        return got_x.at[pl.ds(ONES + STARTS[half], ROWS_X[half]), pl.ds(F * i, F)]

    def z_slot(i):
        return got_z.at[pl.ds(0, ROWS_Z), pl.ds(F * i, F)]

    def x_tile(xx, cc):
        return tiles.at[12 * y + 2 * xx + cc]

    def z_tile(zz, cc):
        return tiles.at[12 * y + 8 + zz, pl.ds(pl.multiple_of(HALF * cc, HALF), ROWS_Z)]

    local = [
        pltpu.make_async_copy(farm_area, area_in, local_sem.at[0]),
        pltpu.make_async_copy(capacity, capacity_in, local_sem.at[1]),
        pltpu.make_async_copy(offsets, offsets_in, local_sem.at[2]),
        pltpu.make_async_copy(z_tile(z, c), z_slot(0), local_sem.at[3]),
        pltpu.make_async_copy(x_tile(x, c), got_x.at[pl.ds(ONES, T), pl.ds(0, F)], local_sem.at[4]),
        pltpu.make_async_copy(state, st, local_sem.at[5]),
    ]
    for copy in local:
        copy.start()
    pl.semaphore_wait(barrier, 16)

    def fx_copy(i):
        xx, cc = x_peers[i]
        return remote(facts_x.at[0], facts_x.at[BACK[i]], fx_send.at[i], fx_recv.at[BACK[i]],
                      device(xx, z, cc, y))

    def fz_copy(i):
        zz, cc = z_peers[i]
        return remote(facts_z.at[0], facts_z.at[BACK[i]], fz_send.at[i], fz_recv.at[BACK[i]],
                      device(x, zz, cc, y))

    def x_copy(i, half):
        xx, cc = x_peers[i]
        return remote(x_tile(xx, cc).at[pl.ds(STARTS[half], ROWS_X[half])], x_slot(BACK[i], half),
                      x_send.at[half, i], x_recv.at[half, BACK[i]], device(xx, z, cc, y))

    def z_copy(i):
        zz, cc = z_peers[i]
        return remote(z_tile(zz, cc), z_slot(BACK[i]), z_send.at[i], z_recv.at[BACK[i]],
                      device(x, zz, cc, y))

    sends = []

    def start(*copies):
        for copy in copies:
            copy.start()
            sends.append(copy)

    start(x_copy(6, 0), x_copy(7, 0), z_copy(6), z_copy(7))
    for copy in local[:3]:
        copy.wait()

    lane = iota((1, F), 1)
    offset = jnp.zeros((1, F), jnp.int32)
    for k in range(16):
        offset = jnp.where((lane & 15) == k, offsets_in[k], offset)
    area = area_in[...]
    turned = ((area >> 5) & 3) * 128 + (area >> 7) * 32 + (area & 31)
    for facts, ids, spot in ((facts_z, turned, mine_z), (facts_x, area, mine_x)):
        placed = jnp.where((lane >> 4) == spot, offset, 0)
        rows = jnp.concatenate(
            [ids, capacity_in[...], placed, jnp.zeros((1, F), jnp.int32)], axis=0)
        facts[0] = rows.astype(jnp.float32)

    for i in ORDER:
        start(fz_copy(i), fx_copy(i))
    for i in ORDER[2:]:
        start(x_copy(i, 0), z_copy(i))

    for i in ORDER:
        start(x_copy(i, 1))

    got_x[pl.ds(0, ONES)] = jnp.ones((ONES, 8 * F), jnp.bfloat16)
    got_z[pl.ds(ROWS_Z, 16)] = jnp.ones((16, 8 * F), jnp.bfloat16)
    off_x[...] = jnp.zeros_like(off_x)
    off_z[...] = jnp.zeros_like(off_z)
    area_ids = iota((AREAS, F), 0).astype(jnp.float32)

    def weigh(i, facts, weight, off):
        rows = facts[i]
        off[...] = off[...] + rows[2:3, :LANES]
        placed = jnp.where(area_ids == rows[0:1], rows[1:2], 0.0)
        weight[:, pl.ds(pl.multiple_of(F * i, F), F)] = placed.astype(jnp.bfloat16)

    @loop(0, 8)
    def _(i):
        for facts, recv, send, weight, off in (
                (facts_z, fz_recv, fz_send, weight_z, off_z),
                (facts_x, fx_recv, fx_send, weight_x, off_x)):
            @pl.when(i > 0)
            def _():
                wait_for(facts.at[i], send.at[i], recv.at[i])

            weigh(i, facts, weight, off)

    def sum_up(values, weights):
        return lax.dot_general(values, weights, (((1,), (1,)), ((), ())),
                               preferred_element_type=jnp.float32)

    bz, bx = [], ([], [])

    def sum_x_half(half, first, count, skip):
        keep = count - skip
        rows = pl.ds(first + skip - 8, keep)
        for pair in ((2, 1), (3, 0)):
            chosen = jnp.concatenate(
                [weight_x[pl.ds(pl.multiple_of(LANES * zs[d], LANES), LANES)] for d in pair],
                axis=0)
            value = sum_up(got_x[pl.ds(first, count)], chosen)
            for k, d in enumerate(pair):
                part_x[zs[d], rows] = value[skip:, k * LANES : (k + 1) * LANES]
                if d > 0:
                    copy = remote(part_x.at[zs[d], rows], sum_x.at[3 - d, rows],
                                  bx_send.at[half, d - 1], bx_recv.at[half, 3 - d],
                                  device(x, zs[d], c, y))
                    copy.start()
                    bx[half].append(copy)

    local[4].wait()
    for i in range(1, 8):
        wait_for(x_slot(i, 0), x_send.at[0, i], x_recv.at[0, i])
    sum_x_half(0, 0, ONES + ROWS_X[0], 8)

    local[3].wait()
    for i in range(1, 8):
        wait_for(z_slot(i), z_send.at[i], z_recv.at[i])
    for h in range(2):
        value = sum_up(got_z[...], weight_z[pl.ds(2 * LANES * h, 2 * LANES)])
        for b in range(2):
            part_z[2 * h + b] = value[:KEEP_Z, b * LANES : (b + 1) * LANES]

    for i in range(1, 8):
        wait_for(x_slot(i, 1), x_send.at[1, i], x_recv.at[1, i])
    for d in (2, 1, 3):
        copy = remote(part_z.at[xs[d]], sum_z.at[3 - d], bz_send.at[d - 1], bz_recv.at[3 - d],
                      device(xs[d], z, c, y))
        copy.start()
        bz.append(copy)
    sum_x_half(1, ONES + ROWS_X[0], ROWS_X[1], 0)

    def whole(copies, own, others, rows):
        for copy in copies:
            copy.wait_recv()
        total = own[rows]
        for k in range(3):
            total = total + others[k, rows]
        return total

    spot = (4 * y + z) * 8 + mine_x

    early_rows, late_rows = pl.ds(0, 8 + ROWS_X[0]), pl.ds(8 + ROWS_X[0], ROWS_X[1])
    first = whole(bx[0], part_x.at[z], sum_x, early_rows)
    total = jnp.maximum(first[:1], capacity_floor)
    power = first[8:] / total
    early = ramp_metric(power, off_x[...], 0, 84)
    last = whole(bz, part_z.at[x], sum_z, pl.ds(0, KEEP_Z))
    metrics[spot, pl.ds(1, 1)] = ramp_metric(
        last[:ROWS_Z] / jnp.maximum(last[ROWS_Z : ROWS_Z + 1], capacity_floor),
        off_z[...], 0, RAMPS_Z)
    last = whole(bx[1], part_x.at[z], sum_x, late_rows)
    power = jnp.concatenate([power[80:], last / total], axis=0)
    late = ramp_metric(power, off_x[...], 4, 52)
    metrics[spot, pl.ds(0, 1)] = jnp.maximum(early, late)

    mine = metrics.at[spot]

    def broadcast(xx, zz, cc, yy):
        remote(mine, mine, all_send, all_recv, device(xx, zz, cc, yy)).start()

    @loop(0, 15)
    def _(k):
        step = 1 + lax.rem(k + 9, 15)
        yy, zz = lax.rem(y + lax.div(step, 4), 4), lax.rem(z + lax.rem(step, 4), 4)
        for i in (6, 7, 2, 3, 4, 5, 0, 1):
            xx, cc = x_peers[i]
            broadcast(xx, zz, cc, yy)

    for i in ORDER:
        xx, cc = x_peers[i]
        broadcast(xx, z, cc, y)

    local[5].wait()

    @loop(0, QUADS)
    def _(i):
        values = st[:, i].astype(jnp.float32).reshape(M, 2, 8, LANES)
        values = values - (jnp.sum(values, axis=0) / M)[None]
        pairs = values.reshape(M // 2, 2, 2, 8, LANES)
        for h in range(2):
            both = swap_halves(pairs[:, 0, h], pairs[:, 1, h])
            for k in range(2):
                slab_out[i, :, pl.ds((2 * h + k) * LANES, LANES)] = (
                    both[k].reshape(4 * M, LANES).astype(jnp.bfloat16))

    for copy in sends + bx[0] + bx[1] + bz:
        copy.wait_send()

    others = metrics.at[pl.ds(0, 127)]
    everything = remote(others, others, all_send, all_recv, sibling)
    everything.wait_recv()

    rows = metrics.reshape(256, LANES)
    for yy in range(4):
        for zz in range(4):
            metric_out[pl.ds(8 * yy, 8), pl.ds(LANES * zz, LANES)] = (
                rows[pl.ds(16 * (4 * yy + zz), 8, stride=2)])
    quarter = iota((16, LANES), 1) >> 5
    blocks = [jnp.maximum(rows[pl.ds(4 * b + 1, 16, stride=16)], rows[pl.ds(4 * b + 3, 16, stride=16)])
              for b in range(RING)]
    for zz in range(4):
        value = jnp.zeros((16, LANES), jnp.float32)
        for b in range(RING):
            move = (32 * (b - zz)) % LANES
            moved = pltpu.roll(blocks[b], move, 1) if move else blocks[b]
            value = jnp.where(quarter == b, moved, value)
        metric_out[pl.ds(32, 16), pl.ds(zz * LANES, LANES)] = value

    everything.wait_send()


def exchange(tiles, farm_area, capacity, offsets, state):
    any_space = pl.BlockSpec(memory_space=pl.ANY)
    vmem = pl.BlockSpec(memory_space=pltpu.VMEM)
    dma = pltpu.SemaphoreType.DMA
    f32, bf16 = jnp.float32, jnp.bfloat16
    return pl.pallas_call(
        exchange_kernel,
        out_shape=(
            pltpu.VMEM((M, AREAS), f32),
            pltpu.VMEM((QUADS, 4 * M, 4 * LANES), bf16),
        ),
        in_specs=[any_space] * 5,
        out_specs=(vmem, vmem),
        scratch_shapes=[
            pltpu.VMEM((1, F), jnp.int32),
            pltpu.VMEM((1, F), jnp.int32),
            pltpu.SMEM((16,), jnp.int32),
            pltpu.VMEM((8, 4, F), f32),
            pltpu.VMEM((8, 4, F), f32),
            pltpu.VMEM((PAD_X, 8 * F), bf16),
            pltpu.VMEM((PAD_Z, 8 * F), bf16),
            pltpu.VMEM((AREAS, 8 * F), bf16),
            pltpu.VMEM((AREAS, 8 * F), bf16),
            pltpu.VMEM((RING, KEEP_X, LANES), f32),
            pltpu.VMEM((RING, KEEP_Z, LANES), f32),
            pltpu.VMEM((3, KEEP_X, LANES), f32),
            pltpu.VMEM((3, KEEP_Z, LANES), f32),
            pltpu.VMEM((1, LANES), f32),
            pltpu.VMEM((1, LANES), f32),
            pltpu.VMEM((128, 2, LANES), f32),
            pltpu.VMEM((M, QUADS, 16, LANES), bf16),
            dma((6,)), dma((8,)), dma((8,)), dma((8,)), dma((8,)),
            dma((2, 8)), dma((2, 8)), dma((8,)), dma((8,)),
            dma((2, 3)), dma((2, 3)), dma((3,)), dma((3,)),
            dma, dma,
        ],
        compiler_params=pltpu.CompilerParams(
            collective_id=0, has_side_effects=True, vmem_limit_bytes=60 * 2**20),
        cost_estimate=pl.CostEstimate(
            flops=2 * 256 * 2048 * 512, bytes_accessed=5 * 2**20, transcendentals=0),
        name="exchange",
    )(tiles, farm_area, capacity, offsets, state)


def product_kernel(metric, slab, out, wide, lhs, stage, out_sem):
    values = metric[...]
    anomaly = values - jnp.mean(values, axis=0, keepdims=True)
    spread = jnp.sqrt(jnp.sum(anomaly * anomaly, axis=0, keepdims=True) / (M - 1))
    scores = anomaly / jnp.maximum(spread, spread_floor)
    scores = jnp.transpose(scores).astype(jnp.bfloat16)

    held = iota((M, 4 * M), 0)
    rest = held - 32
    member = jnp.where(
        held < 32,
        12 * (held >> 3) + (held & 7),
        12 * (rest >> 2) + 8 + (rest & 3))
    widen = ((iota((M, 4 * M), 1) >> 2) == member).astype(jnp.bfloat16)
    wide[...] = jnp.dot(scores, widen, preferred_element_type=jnp.float32).astype(jnp.bfloat16)
    repeat = ((iota((ROWS, ROWS // 4), 0) >> 2) == iota((ROWS, ROWS // 4), 1)).astype(
        jnp.bfloat16)
    keep = (iota((ROWS, 4 * M), 0) & 3) == (iota((ROWS, 4 * M), 1) & 3)
    areas = ROWS // 4

    half = 4 * AREAS // ROWS // 2

    def part(q, i):
        some = pl.ds(pl.multiple_of(2 * areas * q, 2 * areas), 2 * areas)
        return pltpu.make_async_copy(stage.at[some, i], out.at[some, i], out_sem.at[QUADS * q + i])

    def step(q, carry):
        first = [pl.multiple_of((2 * q + r) * areas, areas) for r in range(2)]
        for r in range(2):
            rows = jnp.dot(repeat, wide[pl.ds(first[r], areas)],
                           preferred_element_type=jnp.float32)
            lhs[r] = jnp.where(keep, rows, 0.0).astype(jnp.bfloat16)
        for i in range(QUADS):
            for r in range(2):
                parts = []
                for h in range(2):
                    acc = jnp.dot(lhs[r], slab[i, :, pl.ds(2 * LANES * h, 2 * LANES)],
                                  preferred_element_type=jnp.float32)
                    acc = (acc * (1.0 / (M - 1))).reshape(ROWS // 8, 8, 2 * LANES)
                    both = swap_halves(acc[:, :, :LANES], acc[:, :, LANES:])
                    parts.append(jnp.stack(both, axis=1).reshape(areas, 8, LANES))
                done = jnp.stack(parts, axis=1).reshape(areas, 16, LANES)
                stage[pl.ds(first[r], areas), i] = done.astype(jnp.bfloat16)
            part(q, i).start()
        return carry

    lax.fori_loop(0, half, step, 0)

    def finish(q, carry):
        for i in range(QUADS):
            part(q, i).wait()
        return carry

    lax.fori_loop(0, half, finish, 0)


def product(metric, slab):
    any_space = pl.BlockSpec(memory_space=pl.ANY)
    dma = pltpu.SemaphoreType.DMA
    return pl.pallas_call(
        product_kernel,
        out_shape=jax.ShapeDtypeStruct((AREAS, QUADS, 16, LANES), jnp.bfloat16),
        in_specs=[pl.BlockSpec(memory_space=pltpu.VMEM)] * 2,
        out_specs=any_space,
        scratch_shapes=[
            pltpu.VMEM((AREAS, 4 * M), jnp.bfloat16),
            pltpu.VMEM((2, ROWS, 4 * M), jnp.bfloat16),
            pltpu.VMEM((AREAS, QUADS, 16, LANES), jnp.bfloat16),
            dma((32,)),
        ],
        compiler_params=pltpu.CompilerParams(vmem_limit_bytes=32 * 2**20),
        cost_estimate=pl.CostEstimate(
            flops=2 * 2048 * 192 * 4096, bytes_accessed=20 * 2**20, transcendentals=0),
        name="product",
    )(metric, slab)


def body(tiles, farm_area, capacity, offsets, state):
    by_member = jnp.transpose(tiles, (1, 2, 0))
    columns = state.reshape(M, 2, 64, LANES)
    columns = jnp.transpose(columns, (0, 2, 1, 3)).reshape(M, QUADS, 16, LANES)
    metric, slab = exchange(
        by_member, farm_area.reshape(1, F), capacity.reshape(1, F), offsets, columns)
    out = product(metric, slab)
    out = jnp.transpose(out.reshape(AREAS, 64, 2, LANES), (0, 2, 1, 3))
    return out.reshape(AREAS, 2, 64 * LANES)


def solution(mesh):
    in_specs = (P("grid", None, None), P("grid"), P("grid"), P("grid"), P(None, "lev", "grid"))
    out_specs = P(None, "lev", "grid")
    return jax.shard_map(body, mesh=mesh, in_specs=in_specs, out_specs=out_specs, check_vma=False)
```

```python
import jax
import jax.numpy as jnp
from jax import lax
from jax.experimental import pallas as pl
from jax.experimental.pallas import tpu as pltpu
from jax.sharding import PartitionSpec as P

MESH = pl.DeviceIdType.MESH
M = 48
T = 144
F = 256
AREAS = 512
LANES = 128
RING = 4
ONES = 16
PAD_X = ONES + T
ROWS_Z = 80
PAD_Z = 96
HALF = 64
RAMPS = 132
RAMPS_Z = 68
KEEP_X = 152
KEEP_Z = 88
QUADS = 8
ROWS = 256
capacity_floor = 200.0
spread_floor = 0.05


def iota(shape, dim):
    return lax.broadcasted_iota(jnp.int32, shape, dim)


def swap_halves(u, v):
    low = iota(u.shape, 1) < 4
    crossed = pltpu.roll(jnp.where(low, v, u), 4, 1)
    return jnp.where(low, u, crossed), jnp.where(low, crossed, v)


def ramp_metric(power, offset, first, last):
    steps = power.shape[0]
    wide = jnp.broadcast_to(offset, power.shape).astype(jnp.int32)
    later = power
    for bit in (1, 2, 4, 8):
        later = jnp.where((wide & bit) != 0, pltpu.roll(later, steps - bit, 0), later)
    row = iota(power.shape, 0)
    inside = (row >= first) & (row < last)
    return jnp.max(jnp.where(inside, later - power, -3e38), axis=0, keepdims=True)


STEP = (0, 0, 1, 1, 3, 3, 2, 2)
BACK = (0, 1, 4, 5, 2, 3, 6, 7)
ORDER = (6, 7, 2, 4, 3, 5, 1)
NEAR = 6
STARTS, ROWS_X = (0, 96), (96, 48)


def exchange_kernel(
    tiles, farm_area, capacity, offsets, state, metric_out, slab_out,
    area_in, capacity_in, offsets_in,
    facts_x, facts_z, got_x, got_z, weight_x, weight_z,
    part_x, part_z, sum_x, sum_z, off_x, off_z,
    metrics, st,
    local_sem, fx_send, fx_recv, fz_send, fz_recv, x_send, x_recv, z_send, z_recv,
    bx_send, bx_recv, bz_send, bz_recv,
    all_send, all_recv,
):
    g = lax.axis_index("grid")
    y = lax.axis_index("lev")
    z = lax.div(g, 8)
    x = lax.rem(lax.div(g, 2), 4)
    c = lax.rem(g, 2)
    mine_x = 2 * x + c
    mine_z = 2 * z + c
    xs = [x] + [lax.rem(x + d, 4) for d in range(1, 4)]
    zs = [z] + [lax.rem(z + d, 4) for d in range(1, 4)]
    ys = [y] + [lax.rem(y + d, 4) for d in range(1, 4)]
    cs = [c, 1 - c]

    def device(xx, zz, cc, yy):
        return (zz * 8 + xx * 2 + cc, yy)

    sibling = device(x, z, 1 - c, y)
    x_peers = [(xs[STEP[i]], cs[i % 2]) for i in range(8)]
    z_peers = [(zs[STEP[i]], cs[i % 2]) for i in range(8)]

    def remote(src, dst, send_sem, recv_sem, to):
        return pltpu.make_async_remote_copy(
            src_ref=src, dst_ref=dst, send_sem=send_sem, recv_sem=recv_sem,
            device_id=to, device_id_type=MESH)

    def wait_for(slot, send, recv):
        remote(slot, slot, send, recv, sibling).wait_recv()

    def loop(first, last):
        def run(body):
            lax.fori_loop(first, last, lambda i, carry: (body(i), carry)[1], 0)
        return run

    barrier = pltpu.get_barrier_semaphore()

    def greet(to):
        pl.semaphore_signal(barrier, inc=1, device_id=to, device_id_type=MESH)

    for i in ORDER:
        xx, cc = x_peers[i]
        greet(device(xx, z, cc, y))
        if i != 1:
            zz, cc = z_peers[i]
            greet(device(x, zz, cc, y))
    for d in (2, 1, 3):
        greet(device(x, z, c, ys[d]))

    def x_slot(i, half):
        return got_x.at[pl.ds(ONES + STARTS[half], ROWS_X[half]), pl.ds(F * i, F)]

    def z_slot(i):
        return got_z.at[pl.ds(0, ROWS_Z), pl.ds(F * i, F)]

    def x_tile(xx, cc):
        return tiles.at[12 * y + 2 * xx + cc]

    def z_tile(zz, cc):
        return tiles.at[12 * y + 8 + zz, pl.ds(pl.multiple_of(HALF * cc, HALF), ROWS_Z)]

    local = [
        pltpu.make_async_copy(farm_area, area_in, local_sem.at[0]),
        pltpu.make_async_copy(capacity, capacity_in, local_sem.at[1]),
        pltpu.make_async_copy(offsets, offsets_in, local_sem.at[2]),
        pltpu.make_async_copy(z_tile(z, c), z_slot(0), local_sem.at[3]),
        pltpu.make_async_copy(x_tile(x, c), got_x.at[pl.ds(ONES, T), pl.ds(0, F)], local_sem.at[4]),
        pltpu.make_async_copy(state, st, local_sem.at[5]),
    ]
    for copy in local:
        copy.start()
    pl.semaphore_wait(barrier, 16)

    def fx_copy(i):
        xx, cc = x_peers[i]
        return remote(facts_x.at[0], facts_x.at[BACK[i]], fx_send.at[i], fx_recv.at[BACK[i]],
                      device(xx, z, cc, y))

    def fz_copy(i):
        zz, cc = z_peers[i]
        return remote(facts_z.at[0], facts_z.at[BACK[i]], fz_send.at[i], fz_recv.at[BACK[i]],
                      device(x, zz, cc, y))

    def x_copy(i, half):
        xx, cc = x_peers[i]
        return remote(x_tile(xx, cc).at[pl.ds(STARTS[half], ROWS_X[half])], x_slot(BACK[i], half),
                      x_send.at[half, i], x_recv.at[half, BACK[i]], device(xx, z, cc, y))

    def z_copy(i):
        zz, cc = z_peers[i]
        return remote(z_tile(zz, cc), z_slot(BACK[i]), z_send.at[i], z_recv.at[BACK[i]],
                      device(x, zz, cc, y))

    sends = []

    def start(*copies):
        for copy in copies:
            copy.start()
            sends.append(copy)

    start(x_copy(6, 0), x_copy(7, 0), z_copy(6), z_copy(7))
    for copy in local[:3]:
        copy.wait()

    lane = iota((1, F), 1)
    offset = jnp.zeros((1, F), jnp.int32)
    for k in range(16):
        offset = jnp.where((lane & 15) == k, offsets_in[k], offset)
    area = area_in[...]
    turned = ((area >> 5) & 3) * 128 + (area >> 7) * 32 + (area & 31)
    for facts, ids, spot in ((facts_z, turned, mine_z), (facts_x, area, mine_x)):
        placed = jnp.where((lane >> 4) == spot, offset, 0)
        rows = jnp.concatenate(
            [ids, capacity_in[...], placed, jnp.zeros((1, F), jnp.int32)], axis=0)
        facts[0] = rows.astype(jnp.float32)

    for i in ORDER:
        start(fz_copy(i), fx_copy(i))
    for i in ORDER[2:]:
        start(x_copy(i, 0), z_copy(i))

    for i in ORDER[2:] + ORDER[:2]:
        start(x_copy(i, 1))

    got_x[pl.ds(0, ONES)] = jnp.ones((ONES, 8 * F), jnp.bfloat16)
    got_z[pl.ds(ROWS_Z, 16)] = jnp.ones((16, 8 * F), jnp.bfloat16)
    off_x[...] = jnp.zeros_like(off_x)
    off_z[...] = jnp.zeros_like(off_z)
    area_ids = iota((AREAS, F), 0).astype(jnp.float32)

    def weigh(i, facts, weight, off):
        rows = facts[i]
        off[...] = off[...] + rows[2:3, :LANES]
        placed = jnp.where(area_ids == rows[0:1], rows[1:2], 0.0)
        weight[:, pl.ds(pl.multiple_of(F * i, F), F)] = placed.astype(jnp.bfloat16)

    @loop(0, 8)
    def _(i):
        for facts, recv, send, weight, off in (
                (facts_z, fz_recv, fz_send, weight_z, off_z),
                (facts_x, fx_recv, fx_send, weight_x, off_x)):
            @pl.when(i > 0)
            def _():
                wait_for(facts.at[i], send.at[i], recv.at[i])

            weigh(i, facts, weight, off)

    def sum_up(values, weights):
        return lax.dot_general(values, weights, (((1,), (1,)), ((), ())),
                               preferred_element_type=jnp.float32)

    bz, bx = [], ([], [])

    pairs = ((2, 1), (3, 0))
    near, far = pl.ds(0, NEAR * F), pl.ds(NEAR * F, (8 - NEAR) * F)

    def dot_x(first, count, pair, columns):
        chosen = jnp.concatenate(
            [weight_x[pl.ds(pl.multiple_of(LANES * zs[d], LANES), LANES), columns] for d in pair],
            axis=0)
        return sum_up(got_x[pl.ds(first, count), columns], chosen)

    def leave(half, pair, rows, value):
        for k, d in enumerate(pair):
            part_x[zs[d], rows] = value[:, k * LANES : (k + 1) * LANES]
            if d > 0:
                copy = remote(part_x.at[zs[d], rows], sum_x.at[3 - d, rows],
                              bx_send.at[half, d - 1], bx_recv.at[half, 3 - d],
                              device(x, zs[d], c, y))
                copy.start()
                bx[half].append(copy)

    early_rows, late_rows = pl.ds(0, 8 + ROWS_X[0]), pl.ds(8 + ROWS_X[0], ROWS_X[1])
    local[4].wait()
    for i in range(1, 8):
        wait_for(x_slot(i, 0), x_send.at[0, i], x_recv.at[0, i])
    for pair in pairs:
        leave(0, pair, early_rows, dot_x(0, ONES + ROWS_X[0], pair, pl.ds(0, 8 * F))[8:])

    local[3].wait()
    for i in range(1, 8):
        wait_for(z_slot(i), z_send.at[i], z_recv.at[i])
    for h in range(2):
        value = sum_up(got_z[...], weight_z[pl.ds(2 * LANES * h, 2 * LANES)])
        for b in range(2):
            part_z[2 * h + b] = value[:KEEP_Z, b * LANES : (b + 1) * LANES]
    for d in (2, 1, 3):
        copy = remote(part_z.at[xs[d]], sum_z.at[3 - d], bz_send.at[d - 1], bz_recv.at[3 - d],
                      device(xs[d], z, c, y))
        copy.start()
        bz.append(copy)

    for i in range(1, NEAR):
        wait_for(x_slot(i, 1), x_send.at[1, i], x_recv.at[1, i])
    values = [dot_x(ONES + ROWS_X[0], ROWS_X[1], pair, near) for pair in pairs]
    for i in range(NEAR, 8):
        wait_for(x_slot(i, 1), x_send.at[1, i], x_recv.at[1, i])
    for pair, value in zip(pairs, values):
        leave(1, pair, late_rows, value + dot_x(ONES + ROWS_X[0], ROWS_X[1], pair, far))

    def whole(copies, own, others, rows):
        for copy in copies:
            copy.wait_recv()
        total = own[rows]
        for k in range(3):
            total = total + others[k, rows]
        return total

    spot = (4 * y + z) * 8 + mine_x

    first = whole(bx[0], part_x.at[z], sum_x, early_rows)
    total = jnp.maximum(first[:1], capacity_floor)
    power = first[8:] / total
    early = ramp_metric(power, off_x[...], 0, 84)
    last = whole(bz, part_z.at[x], sum_z, pl.ds(0, KEEP_Z))
    metrics[spot, pl.ds(1, 1)] = ramp_metric(
        last[:ROWS_Z] / jnp.maximum(last[ROWS_Z : ROWS_Z + 1], capacity_floor),
        off_z[...], 0, RAMPS_Z)
    last = whole(bx[1], part_x.at[z], sum_x, late_rows)
    power = jnp.concatenate([power[80:], last / total], axis=0)
    late = ramp_metric(power, off_x[...], 4, 52)
    metrics[spot, pl.ds(0, 1)] = jnp.maximum(early, late)

    mine = metrics.at[spot]

    def broadcast(xx, zz, cc, yy):
        remote(mine, mine, all_send, all_recv, device(xx, zz, cc, yy)).start()

    @loop(0, 15)
    def _(k):
        step = 1 + lax.rem(k + 9, 15)
        yy, zz = lax.rem(y + lax.div(step, 4), 4), lax.rem(z + lax.rem(step, 4), 4)
        for i in (6, 7, 2, 3, 4, 5, 0, 1):
            xx, cc = x_peers[i]
            broadcast(xx, zz, cc, yy)

    for i in ORDER:
        xx, cc = x_peers[i]
        broadcast(xx, z, cc, y)

    local[5].wait()

    @loop(0, QUADS)
    def _(i):
        values = st[:, i].astype(jnp.float32).reshape(M, 2, 8, LANES)
        values = values - (jnp.sum(values, axis=0) / M)[None]
        pairs = values.reshape(M // 2, 2, 2, 8, LANES)
        for h in range(2):
            both = swap_halves(pairs[:, 0, h], pairs[:, 1, h])
            for k in range(2):
                slab_out[i, :, pl.ds((2 * h + k) * LANES, LANES)] = (
                    both[k].reshape(4 * M, LANES).astype(jnp.bfloat16))

    for copy in sends + bx[0] + bx[1] + bz:
        copy.wait_send()

    others = metrics.at[pl.ds(0, 127)]
    everything = remote(others, others, all_send, all_recv, sibling)
    everything.wait_recv()

    rows = metrics.reshape(256, LANES)
    for yy in range(4):
        for zz in range(4):
            metric_out[pl.ds(8 * yy, 8), pl.ds(LANES * zz, LANES)] = (
                rows[pl.ds(16 * (4 * yy + zz), 8, stride=2)])
    quarter = iota((16, LANES), 1) >> 5
    blocks = [jnp.maximum(rows[pl.ds(4 * b + 1, 16, stride=16)], rows[pl.ds(4 * b + 3, 16, stride=16)])
              for b in range(RING)]
    for zz in range(4):
        value = jnp.zeros((16, LANES), jnp.float32)
        for b in range(RING):
            move = (32 * (b - zz)) % LANES
            moved = pltpu.roll(blocks[b], move, 1) if move else blocks[b]
            value = jnp.where(quarter == b, moved, value)
        metric_out[pl.ds(32, 16), pl.ds(zz * LANES, LANES)] = value

    everything.wait_send()


def exchange(tiles, farm_area, capacity, offsets, state):
    any_space = pl.BlockSpec(memory_space=pl.ANY)
    vmem = pl.BlockSpec(memory_space=pltpu.VMEM)
    dma = pltpu.SemaphoreType.DMA
    f32, bf16 = jnp.float32, jnp.bfloat16
    return pl.pallas_call(
        exchange_kernel,
        out_shape=(
            pltpu.VMEM((M, AREAS), f32),
            pltpu.VMEM((QUADS, 4 * M, 4 * LANES), bf16),
        ),
        in_specs=[any_space] * 5,
        out_specs=(vmem, vmem),
        scratch_shapes=[
            pltpu.VMEM((1, F), jnp.int32),
            pltpu.VMEM((1, F), jnp.int32),
            pltpu.SMEM((16,), jnp.int32),
            pltpu.VMEM((8, 4, F), f32),
            pltpu.VMEM((8, 4, F), f32),
            pltpu.VMEM((PAD_X, 8 * F), bf16),
            pltpu.VMEM((PAD_Z, 8 * F), bf16),
            pltpu.VMEM((AREAS, 8 * F), bf16),
            pltpu.VMEM((AREAS, 8 * F), bf16),
            pltpu.VMEM((RING, KEEP_X, LANES), f32),
            pltpu.VMEM((RING, KEEP_Z, LANES), f32),
            pltpu.VMEM((3, KEEP_X, LANES), f32),
            pltpu.VMEM((3, KEEP_Z, LANES), f32),
            pltpu.VMEM((1, LANES), f32),
            pltpu.VMEM((1, LANES), f32),
            pltpu.VMEM((128, 2, LANES), f32),
            pltpu.VMEM((M, QUADS, 16, LANES), bf16),
            dma((6,)), dma((8,)), dma((8,)), dma((8,)), dma((8,)),
            dma((2, 8)), dma((2, 8)), dma((8,)), dma((8,)),
            dma((2, 3)), dma((2, 3)), dma((3,)), dma((3,)),
            dma, dma,
        ],
        compiler_params=pltpu.CompilerParams(
            collective_id=0, has_side_effects=True, vmem_limit_bytes=60 * 2**20),
        cost_estimate=pl.CostEstimate(
            flops=2 * 256 * 2048 * 512, bytes_accessed=5 * 2**20, transcendentals=0),
        name="exchange",
    )(tiles, farm_area, capacity, offsets, state)


def product_kernel(metric, slab, out, wide, lhs, stage, out_sem):
    values = metric[...]
    anomaly = values - jnp.mean(values, axis=0, keepdims=True)
    spread = jnp.sqrt(jnp.sum(anomaly * anomaly, axis=0, keepdims=True) / (M - 1))
    scores = anomaly / jnp.maximum(spread, spread_floor)
    scores = jnp.transpose(scores).astype(jnp.bfloat16)

    held = iota((M, 4 * M), 0)
    rest = held - 32
    member = jnp.where(
        held < 32,
        12 * (held >> 3) + (held & 7),
        12 * (rest >> 2) + 8 + (rest & 3))
    widen = ((iota((M, 4 * M), 1) >> 2) == member).astype(jnp.bfloat16)
    wide[...] = jnp.dot(scores, widen, preferred_element_type=jnp.float32).astype(jnp.bfloat16)
    repeat = ((iota((ROWS, ROWS // 4), 0) >> 2) == iota((ROWS, ROWS // 4), 1)).astype(
        jnp.bfloat16)
    keep = (iota((ROWS, 4 * M), 0) & 3) == (iota((ROWS, 4 * M), 1) & 3)
    areas = ROWS // 4

    half = 4 * AREAS // ROWS // 2

    def part(q, i):
        some = pl.ds(pl.multiple_of(2 * areas * q, 2 * areas), 2 * areas)
        return pltpu.make_async_copy(stage.at[some, i], out.at[some, i], out_sem.at[QUADS * q + i])

    def step(q, carry):
        first = [pl.multiple_of((2 * q + r) * areas, areas) for r in range(2)]
        for r in range(2):
            rows = jnp.dot(repeat, wide[pl.ds(first[r], areas)],
                           preferred_element_type=jnp.float32)
            lhs[r] = jnp.where(keep, rows, 0.0).astype(jnp.bfloat16)
        for i in range(QUADS):
            for r in range(2):
                parts = []
                for h in range(2):
                    acc = jnp.dot(lhs[r], slab[i, :, pl.ds(2 * LANES * h, 2 * LANES)],
                                  preferred_element_type=jnp.float32)
                    acc = (acc * (1.0 / (M - 1))).reshape(ROWS // 8, 8, 2 * LANES)
                    both = swap_halves(acc[:, :, :LANES], acc[:, :, LANES:])
                    parts.append(jnp.stack(both, axis=1).reshape(areas, 8, LANES))
                done = jnp.stack(parts, axis=1).reshape(areas, 16, LANES)
                stage[pl.ds(first[r], areas), i] = done.astype(jnp.bfloat16)
            part(q, i).start(priority=i % 2)
        return carry

    lax.fori_loop(0, half, step, 0)

    def finish(q, carry):
        for i in range(QUADS):
            part(q, i).wait()
        return carry

    lax.fori_loop(0, half, finish, 0)


def product(metric, slab):
    any_space = pl.BlockSpec(memory_space=pl.ANY)
    dma = pltpu.SemaphoreType.DMA
    return pl.pallas_call(
        product_kernel,
        out_shape=jax.ShapeDtypeStruct((AREAS, QUADS, 16, LANES), jnp.bfloat16),
        in_specs=[pl.BlockSpec(memory_space=pltpu.VMEM)] * 2,
        out_specs=any_space,
        scratch_shapes=[
            pltpu.VMEM((AREAS, 4 * M), jnp.bfloat16),
            pltpu.VMEM((2, ROWS, 4 * M), jnp.bfloat16),
            pltpu.VMEM((AREAS, QUADS, 16, LANES), jnp.bfloat16),
            dma((32,)),
        ],
        compiler_params=pltpu.CompilerParams(vmem_limit_bytes=32 * 2**20),
        cost_estimate=pl.CostEstimate(
            flops=2 * 2048 * 192 * 4096, bytes_accessed=20 * 2**20, transcendentals=0),
        name="product",
    )(metric, slab)


def body(tiles, farm_area, capacity, offsets, state):
    by_member = jnp.transpose(tiles, (1, 2, 0))
    columns = state.reshape(M, 2, 64, LANES)
    columns = jnp.transpose(columns, (0, 2, 1, 3)).reshape(M, QUADS, 16, LANES)
    metric, slab = exchange(
        by_member, farm_area.reshape(1, F), capacity.reshape(1, F), offsets, columns)
    out = product(metric, slab)
    out = jnp.transpose(out.reshape(AREAS, 64, 2, LANES), (0, 2, 1, 3))
    return out.reshape(AREAS, 2, 64 * LANES)


def solution(mesh):
    in_specs = (P("grid", None, None), P("grid"), P("grid"), P("grid"), P(None, "lev", "grid"))
    out_specs = P(None, "lev", "grid")
    return jax.shard_map(body, mesh=mesh, in_specs=in_specs, out_specs=out_specs, check_vma=False)
```

```python
import jax
import jax.numpy as jnp
from jax import lax
from jax.experimental import pallas as pl
from jax.experimental.pallas import tpu as pltpu
from jax.sharding import PartitionSpec as P

MESH = pl.DeviceIdType.MESH
M = 48
T = 144
F = 256
AREAS = 512
LANES = 128
RING = 4
ONES = 16
PAD_X = ONES + T
ROWS_Z = 80
PAD_Z = 96
HALF = 64
RAMPS = 132
RAMPS_Z = 68
KEEP_X = 152
KEEP_Z = 88
QUADS = 8
ROWS = 256
capacity_floor = 200.0
spread_floor = 0.05


def iota(shape, dim):
    return lax.broadcasted_iota(jnp.int32, shape, dim)


def swap_halves(u, v):
    low = iota(u.shape, 1) < 4
    crossed = pltpu.roll(jnp.where(low, v, u), 4, 1)
    return jnp.where(low, u, crossed), jnp.where(low, crossed, v)


def ramp_metric(power, offset, first, last):
    steps = power.shape[0]
    wide = jnp.broadcast_to(offset, power.shape).astype(jnp.int32)
    later = power
    for bit in (1, 2, 4, 8):
        later = jnp.where((wide & bit) != 0, pltpu.roll(later, steps - bit, 0), later)
    row = iota(power.shape, 0)
    inside = (row >= first) & (row < last)
    return jnp.max(jnp.where(inside, later - power, -3e38), axis=0, keepdims=True)


STEP = (0, 0, 1, 1, 3, 3, 2, 2)
BACK = (0, 1, 4, 5, 2, 3, 6, 7)
ORDER = (6, 7, 2, 4, 3, 5, 1)
NEAR = 6
STARTS, ROWS_X = (0, 96), (96, 48)


def exchange_kernel(
    tiles, farm_area, capacity, offsets, state, metric_out, slab_out,
    area_in, capacity_in, offsets_in,
    facts_x, facts_z, got_x, got_z, weight_x, weight_z,
    part_x, part_z, sum_x, sum_z, near_x, off_x, off_z,
    metrics, st,
    local_sem, fx_send, fx_recv, fz_send, fz_recv, x_send, x_recv, z_send, z_recv,
    bx_send, bx_recv, bz_send, bz_recv,
    all_send, all_recv,
):
    g = lax.axis_index("grid")
    y = lax.axis_index("lev")
    z = lax.div(g, 8)
    x = lax.rem(lax.div(g, 2), 4)
    c = lax.rem(g, 2)
    mine_x = 2 * x + c
    mine_z = 2 * z + c
    xs = [x] + [lax.rem(x + d, 4) for d in range(1, 4)]
    zs = [z] + [lax.rem(z + d, 4) for d in range(1, 4)]
    ys = [y] + [lax.rem(y + d, 4) for d in range(1, 4)]
    cs = [c, 1 - c]

    def device(xx, zz, cc, yy):
        return (zz * 8 + xx * 2 + cc, yy)

    sibling = device(x, z, 1 - c, y)
    x_peers = [(xs[STEP[i]], cs[i % 2]) for i in range(8)]
    z_peers = [(zs[STEP[i]], cs[i % 2]) for i in range(8)]

    def remote(src, dst, send_sem, recv_sem, to):
        return pltpu.make_async_remote_copy(
            src_ref=src, dst_ref=dst, send_sem=send_sem, recv_sem=recv_sem,
            device_id=to, device_id_type=MESH)

    def wait_for(slot, send, recv):
        remote(slot, slot, send, recv, sibling).wait_recv()

    def loop(first, last):
        def run(body):
            lax.fori_loop(first, last, lambda i, carry: (body(i), carry)[1], 0)
        return run

    barrier = pltpu.get_barrier_semaphore()

    def greet(to):
        pl.semaphore_signal(barrier, inc=1, device_id=to, device_id_type=MESH)

    for i in ORDER:
        xx, cc = x_peers[i]
        greet(device(xx, z, cc, y))
        if i != 1:
            zz, cc = z_peers[i]
            greet(device(x, zz, cc, y))
    for d in (2, 1, 3):
        greet(device(x, z, c, ys[d]))

    def x_slot(i, half):
        return got_x.at[pl.ds(ONES + STARTS[half], ROWS_X[half]), pl.ds(F * i, F)]

    def z_slot(i):
        return got_z.at[pl.ds(0, ROWS_Z), pl.ds(F * i, F)]

    def x_tile(xx, cc):
        return tiles.at[12 * y + 2 * xx + cc]

    def z_tile(zz, cc):
        return tiles.at[12 * y + 8 + zz, pl.ds(pl.multiple_of(HALF * cc, HALF), ROWS_Z)]

    local = [
        pltpu.make_async_copy(farm_area, area_in, local_sem.at[0]),
        pltpu.make_async_copy(capacity, capacity_in, local_sem.at[1]),
        pltpu.make_async_copy(offsets, offsets_in, local_sem.at[2]),
        pltpu.make_async_copy(z_tile(z, c), z_slot(0), local_sem.at[3]),
        pltpu.make_async_copy(x_tile(x, c), got_x.at[pl.ds(ONES, T), pl.ds(0, F)], local_sem.at[4]),
        pltpu.make_async_copy(state, st, local_sem.at[5]),
    ]
    for copy in local:
        copy.start()
    def fx_copy(i):
        xx, cc = x_peers[i]
        return remote(facts_x.at[0], facts_x.at[BACK[i]], fx_send.at[i], fx_recv.at[BACK[i]],
                      device(xx, z, cc, y))

    def fz_copy(i):
        zz, cc = z_peers[i]
        return remote(facts_z.at[0], facts_z.at[BACK[i]], fz_send.at[i], fz_recv.at[BACK[i]],
                      device(x, zz, cc, y))

    def x_copy(i, half):
        xx, cc = x_peers[i]
        return remote(x_tile(xx, cc).at[pl.ds(STARTS[half], ROWS_X[half])], x_slot(BACK[i], half),
                      x_send.at[half, i], x_recv.at[half, BACK[i]], device(xx, z, cc, y))

    def z_copy(i):
        zz, cc = z_peers[i]
        return remote(z_tile(zz, cc), z_slot(BACK[i]), z_send.at[i], z_recv.at[BACK[i]],
                      device(x, zz, cc, y))

    sends = []

    def start(*copies):
        for copy in copies:
            copy.start()
            sends.append(copy)

    for copy in local[:3]:
        copy.wait()

    lane = iota((1, F), 1)
    offset = jnp.zeros((1, F), jnp.int32)
    for k in range(16):
        offset = jnp.where((lane & 15) == k, offsets_in[k], offset)
    area = area_in[...]
    turned = ((area >> 5) & 3) * 128 + (area >> 7) * 32 + (area & 31)
    for facts, ids, spot in ((facts_z, turned, mine_z), (facts_x, area, mine_x)):
        placed = jnp.where((lane >> 4) == spot, offset, 0)
        rows = jnp.concatenate(
            [ids, capacity_in[...], placed, jnp.zeros((1, F), jnp.int32)], axis=0)
        facts[0] = rows.astype(jnp.float32)

    pl.semaphore_wait(barrier, 16)
    for i in ORDER:
        start(fx_copy(i), fz_copy(i))
    for i in ORDER:
        start(x_copy(i, 0), z_copy(i))
    for i in ORDER[2:] + ORDER[:2]:
        start(x_copy(i, 1))

    got_x[pl.ds(0, ONES)] = jnp.ones((ONES, 8 * F), jnp.bfloat16)
    got_z[pl.ds(ROWS_Z, 16)] = jnp.ones((16, 8 * F), jnp.bfloat16)
    off_x[...] = jnp.zeros_like(off_x)
    off_z[...] = jnp.zeros_like(off_z)
    area_ids = iota((AREAS, F), 0).astype(jnp.float32)

    def weigh(i, facts, weight, off):
        rows = facts[i]
        off[...] = off[...] + rows[2:3, :LANES]
        placed = jnp.where(area_ids == rows[0:1], rows[1:2], 0.0)
        weight[:, pl.ds(pl.multiple_of(F * i, F), F)] = placed.astype(jnp.bfloat16)

    @loop(0, 8)
    def _(i):
        for facts, recv, send, weight, off in (
                (facts_z, fz_recv, fz_send, weight_z, off_z),
                (facts_x, fx_recv, fx_send, weight_x, off_x)):
            @pl.when(i > 0)
            def _():
                wait_for(facts.at[i], send.at[i], recv.at[i])

            weigh(i, facts, weight, off)

    def sum_up(values, weights):
        return lax.dot_general(values, weights, (((1,), (1,)), ((), ())),
                               preferred_element_type=jnp.float32)

    bz = []

    near, far = pl.ds(0, NEAR * F), pl.ds(NEAR * F, (8 - NEAR) * F)

    def block_pair(p):
        return lax.rem(z + 2 + p, 4), lax.rem(z + 1 + 3 * p, 4)

    def dot_x(first, count, p, columns):
        chosen = jnp.concatenate(
            [weight_x[pl.ds(pl.multiple_of(LANES * zz, LANES), LANES), columns]
             for zz in block_pair(p)], axis=0)
        return sum_up(got_x[pl.ds(first, count), columns], chosen)

    def sum_copy(half, rows, d, zz):
        return remote(part_x.at[zz, rows], sum_x.at[3 - d, rows], bx_send.at[half, d - 1],
                      bx_recv.at[half, 3 - d], device(x, zz, c, y))

    def leave(half, rows, p, value):
        for k, zz in enumerate(block_pair(p)):
            part_x[zz, rows] = value[:, k * LANES : (k + 1) * LANES]
        sum_copy(half, rows, 2 + p, block_pair(p)[0]).start()

        @pl.when(p == 0)
        def _():
            sum_copy(half, rows, 1, zs[1]).start()

    early_rows, late_rows = pl.ds(0, 8 + ROWS_X[0]), pl.ds(8 + ROWS_X[0], ROWS_X[1])
    local[4].wait()
    for i in range(1, 8):
        wait_for(x_slot(i, 0), x_send.at[0, i], x_recv.at[0, i])

    @loop(0, 2)
    def _(p):
        leave(0, early_rows, p, dot_x(0, ONES + ROWS_X[0], p, pl.ds(0, 8 * F))[8:])

    local[3].wait()
    for i in range(1, 8):
        wait_for(z_slot(i), z_send.at[i], z_recv.at[i])
    for h in range(2):
        value = sum_up(got_z[...], weight_z[pl.ds(2 * LANES * h, 2 * LANES)])
        for b in range(2):
            part_z[2 * h + b] = value[:KEEP_Z, b * LANES : (b + 1) * LANES]
    for d in (2, 1, 3):
        copy = remote(part_z.at[xs[d]], sum_z.at[3 - d], bz_send.at[d - 1], bz_recv.at[3 - d],
                      device(xs[d], z, c, y))
        copy.start()
        bz.append(copy)

    for i in range(1, NEAR):
        wait_for(x_slot(i, 1), x_send.at[1, i], x_recv.at[1, i])

    @loop(0, 2)
    def _(p):
        near_x[p] = dot_x(ONES + ROWS_X[0], ROWS_X[1], p, near)

    for i in range(NEAR, 8):
        wait_for(x_slot(i, 1), x_send.at[1, i], x_recv.at[1, i])

    @loop(0, 2)
    def _(p):
        leave(1, late_rows, p, near_x[p] + dot_x(ONES + ROWS_X[0], ROWS_X[1], p, far))

    bx = [[sum_copy(half, rows, d, zs[d]) for d in range(1, 4)]
          for half, rows in ((0, early_rows), (1, late_rows))]

    def whole(copies, own, others, rows):
        for copy in copies:
            copy.wait_recv()
        total = own[rows]
        for k in range(3):
            total = total + others[k, rows]
        return total

    spot = (4 * y + z) * 8 + mine_x

    first = whole(bx[0], part_x.at[z], sum_x, early_rows)
    total = jnp.maximum(first[:1], capacity_floor)
    power = first[8:] / total
    early = ramp_metric(power, off_x[...], 0, 84)
    last = whole(bz, part_z.at[x], sum_z, pl.ds(0, KEEP_Z))
    metrics[spot, pl.ds(1, 1)] = ramp_metric(
        last[:ROWS_Z] / jnp.maximum(last[ROWS_Z : ROWS_Z + 1], capacity_floor),
        off_z[...], 0, RAMPS_Z)
    last = whole(bx[1], part_x.at[z], sum_x, late_rows)
    power = jnp.concatenate([power[80:], last / total], axis=0)
    late = ramp_metric(power, off_x[...], 4, 52)
    metrics[spot, pl.ds(0, 1)] = jnp.maximum(early, late)

    mine = metrics.at[spot]

    def broadcast(xx, zz, cc, yy):
        remote(mine, mine, all_send, all_recv, device(xx, zz, cc, yy)).start()

    @loop(0, 15)
    def _(k):
        step = 1 + lax.rem(k + 9, 15)
        yy, zz = lax.rem(y + lax.div(step, 4), 4), lax.rem(z + lax.rem(step, 4), 4)
        for i in (6, 7, 2, 3, 4, 5, 0, 1):
            xx, cc = x_peers[i]
            broadcast(xx, zz, cc, yy)

    for i in ORDER:
        xx, cc = x_peers[i]
        broadcast(xx, z, cc, y)

    local[5].wait()

    @loop(0, QUADS)
    def _(i):
        values = st[:, i].astype(jnp.float32).reshape(M, 2, 8, LANES)
        values = values - (jnp.sum(values, axis=0) / M)[None]
        pairs = values.reshape(M // 2, 2, 2, 8, LANES)
        for h in range(2):
            both = swap_halves(pairs[:, 0, h], pairs[:, 1, h])
            for k in range(2):
                slab_out[i, :, pl.ds((2 * h + k) * LANES, LANES)] = (
                    both[k].reshape(4 * M, LANES).astype(jnp.bfloat16))

    for copy in sends + bx[0] + bx[1] + bz:
        copy.wait_send()

    others = metrics.at[pl.ds(0, 127)]
    everything = remote(others, others, all_send, all_recv, sibling)
    everything.wait_recv()

    rows = metrics.reshape(256, LANES)
    for yy in range(4):
        for zz in range(4):
            metric_out[pl.ds(8 * yy, 8), pl.ds(LANES * zz, LANES)] = (
                rows[pl.ds(16 * (4 * yy + zz), 8, stride=2)])
    quarter = iota((16, LANES), 1) >> 5
    blocks = [jnp.maximum(rows[pl.ds(4 * b + 1, 16, stride=16)], rows[pl.ds(4 * b + 3, 16, stride=16)])
              for b in range(RING)]
    for zz in range(4):
        value = jnp.zeros((16, LANES), jnp.float32)
        for b in range(RING):
            move = (32 * (b - zz)) % LANES
            moved = pltpu.roll(blocks[b], move, 1) if move else blocks[b]
            value = jnp.where(quarter == b, moved, value)
        metric_out[pl.ds(32, 16), pl.ds(zz * LANES, LANES)] = value

    everything.wait_send()


def exchange(tiles, farm_area, capacity, offsets, state):
    any_space = pl.BlockSpec(memory_space=pl.ANY)
    vmem = pl.BlockSpec(memory_space=pltpu.VMEM)
    dma = pltpu.SemaphoreType.DMA
    f32, bf16 = jnp.float32, jnp.bfloat16
    return pl.pallas_call(
        exchange_kernel,
        out_shape=(
            pltpu.VMEM((M, AREAS), f32),
            pltpu.VMEM((QUADS, 4 * M, 4 * LANES), bf16),
        ),
        in_specs=[any_space] * 5,
        out_specs=(vmem, vmem),
        scratch_shapes=[
            pltpu.VMEM((1, F), jnp.int32),
            pltpu.VMEM((1, F), jnp.int32),
            pltpu.SMEM((16,), jnp.int32),
            pltpu.VMEM((8, 4, F), f32),
            pltpu.VMEM((8, 4, F), f32),
            pltpu.VMEM((PAD_X, 8 * F), bf16),
            pltpu.VMEM((PAD_Z, 8 * F), bf16),
            pltpu.VMEM((AREAS, 8 * F), bf16),
            pltpu.VMEM((AREAS, 8 * F), bf16),
            pltpu.VMEM((RING, KEEP_X, LANES), f32),
            pltpu.VMEM((RING, KEEP_Z, LANES), f32),
            pltpu.VMEM((3, KEEP_X, LANES), f32),
            pltpu.VMEM((3, KEEP_Z, LANES), f32),
            pltpu.VMEM((2, ROWS_X[1], 2 * LANES), f32),
            pltpu.VMEM((1, LANES), f32),
            pltpu.VMEM((1, LANES), f32),
            pltpu.VMEM((128, 2, LANES), f32),
            pltpu.VMEM((M, QUADS, 16, LANES), bf16),
            dma((6,)), dma((8,)), dma((8,)), dma((8,)), dma((8,)),
            dma((2, 8)), dma((2, 8)), dma((8,)), dma((8,)),
            dma((2, 3)), dma((2, 3)), dma((3,)), dma((3,)),
            dma, dma,
        ],
        compiler_params=pltpu.CompilerParams(
            collective_id=0, has_side_effects=True, vmem_limit_bytes=60 * 2**20),
        cost_estimate=pl.CostEstimate(
            flops=2 * 256 * 2048 * 512, bytes_accessed=5 * 2**20, transcendentals=0),
        name="exchange",
    )(tiles, farm_area, capacity, offsets, state)


def product_kernel(metric, slab, out, wide, lhs, stage, out_sem):
    values = metric[...]
    anomaly = values - jnp.mean(values, axis=0, keepdims=True)
    spread = jnp.sqrt(jnp.sum(anomaly * anomaly, axis=0, keepdims=True) / (M - 1))
    scores = anomaly / jnp.maximum(spread, spread_floor)
    scores = jnp.transpose(scores).astype(jnp.bfloat16)

    held = iota((M, 4 * M), 0)
    rest = held - 32
    member = jnp.where(
        held < 32,
        12 * (held >> 3) + (held & 7),
        12 * (rest >> 2) + 8 + (rest & 3))
    widen = ((iota((M, 4 * M), 1) >> 2) == member).astype(jnp.bfloat16)
    wide[...] = jnp.dot(scores, widen, preferred_element_type=jnp.float32).astype(jnp.bfloat16)
    repeat = ((iota((ROWS, ROWS // 4), 0) >> 2) == iota((ROWS, ROWS // 4), 1)).astype(
        jnp.bfloat16)
    keep = (iota((ROWS, 4 * M), 0) & 3) == (iota((ROWS, 4 * M), 1) & 3)
    areas = ROWS // 4

    half = 4 * AREAS // ROWS // 2

    def part(q, i):
        some = pl.ds(pl.multiple_of(2 * areas * q, 2 * areas), 2 * areas)
        return pltpu.make_async_copy(stage.at[some, i], out.at[some, i], out_sem.at[QUADS * q + i])

    def step(q, carry):
        first = [pl.multiple_of((2 * q + r) * areas, areas) for r in range(2)]
        for r in range(2):
            rows = jnp.dot(repeat, wide[pl.ds(first[r], areas)],
                           preferred_element_type=jnp.float32)
            lhs[r] = jnp.where(keep, rows, 0.0).astype(jnp.bfloat16)
        for i in range(QUADS):
            for r in range(2):
                parts = []
                for h in range(2):
                    acc = jnp.dot(lhs[r], slab[i, :, pl.ds(2 * LANES * h, 2 * LANES)],
                                  preferred_element_type=jnp.float32)
                    acc = (acc * (1.0 / (M - 1))).reshape(ROWS // 8, 8, 2 * LANES)
                    both = swap_halves(acc[:, :, :LANES], acc[:, :, LANES:])
                    parts.append(jnp.stack(both, axis=1).reshape(areas, 8, LANES))
                done = jnp.stack(parts, axis=1).reshape(areas, 16, LANES)
                stage[pl.ds(first[r], areas), i] = done.astype(jnp.bfloat16)
            part(q, i).start(priority=i % 2)
        return carry

    lax.fori_loop(0, half, step, 0)

    def finish(q, carry):
        for i in range(QUADS):
            part(q, i).wait()
        return carry

    lax.fori_loop(0, half, finish, 0)


def product(metric, slab):
    any_space = pl.BlockSpec(memory_space=pl.ANY)
    dma = pltpu.SemaphoreType.DMA
    return pl.pallas_call(
        product_kernel,
        out_shape=jax.ShapeDtypeStruct((AREAS, QUADS, 16, LANES), jnp.bfloat16),
        in_specs=[pl.BlockSpec(memory_space=pltpu.VMEM)] * 2,
        out_specs=any_space,
        scratch_shapes=[
            pltpu.VMEM((AREAS, 4 * M), jnp.bfloat16),
            pltpu.VMEM((2, ROWS, 4 * M), jnp.bfloat16),
            pltpu.VMEM((AREAS, QUADS, 16, LANES), jnp.bfloat16),
            dma((32,)),
        ],
        compiler_params=pltpu.CompilerParams(vmem_limit_bytes=32 * 2**20),
        cost_estimate=pl.CostEstimate(
            flops=2 * 2048 * 192 * 4096, bytes_accessed=20 * 2**20, transcendentals=0),
        name="product",
    )(metric, slab)


def body(tiles, farm_area, capacity, offsets, state):
    by_member = jnp.transpose(tiles, (1, 2, 0))
    columns = state.reshape(M, 2, 64, LANES)
    columns = jnp.transpose(columns, (0, 2, 1, 3)).reshape(M, QUADS, 16, LANES)
    metric, slab = exchange(
        by_member, farm_area.reshape(1, F), capacity.reshape(1, F), offsets, columns)
    out = product(metric, slab)
    out = jnp.transpose(out.reshape(AREAS, 64, 2, LANES), (0, 2, 1, 3))
    return out.reshape(AREAS, 2, 64 * LANES)


def solution(mesh):
    in_specs = (P("grid", None, None), P("grid"), P("grid"), P("grid"), P(None, "lev", "grid"))
    out_specs = P(None, "lev", "grid")
    return jax.shard_map(body, mesh=mesh, in_specs=in_specs, out_specs=out_specs, check_vma=False)
```

```python
import jax
import jax.numpy as jnp
from jax import lax
from jax.experimental import pallas as pl
from jax.experimental.pallas import tpu as pltpu
from jax.sharding import PartitionSpec as P

MESH = pl.DeviceIdType.MESH
M = 48
T = 144
F = 256
AREAS = 512
LANES = 128
RING = 4
ONES = 16
PAD_X = ONES + T
ROWS_Z = 80
PAD_Z = 96
HALF = 64
RAMPS = 132
RAMPS_Z = 68
KEEP_X = 152
KEEP_Z = 88
QUADS = 8
ROWS = 256
capacity_floor = 200.0
spread_floor = 0.05


def iota(shape, dim):
    return lax.broadcasted_iota(jnp.int32, shape, dim)


def swap_halves(u, v):
    low = iota(u.shape, 1) < 4
    crossed = pltpu.roll(jnp.where(low, v, u), 4, 1)
    return jnp.where(low, u, crossed), jnp.where(low, crossed, v)


def ramp_metric(power, offset, first, last):
    steps = power.shape[0]
    wide = jnp.broadcast_to(offset, power.shape).astype(jnp.int32)
    later = power
    for bit in (1, 2, 4, 8):
        later = jnp.where((wide & bit) != 0, pltpu.roll(later, steps - bit, 0), later)
    row = iota(power.shape, 0)
    inside = (row >= first) & (row < last)
    return jnp.max(jnp.where(inside, later - power, -3e38), axis=0, keepdims=True)


STEP = (0, 0, 1, 1, 3, 3, 2, 2)
BACK = (0, 1, 4, 5, 2, 3, 6, 7)
ORDER = (6, 7, 2, 4, 3, 5, 1)
NEAR = 6
STARTS, ROWS_X = (0, 96), (96, 48)


def exchange_kernel(
    tiles, farm_area, capacity, offsets, state, metric_out, slab_out,
    area_in, capacity_in, offsets_in,
    facts_x, facts_z, got_x, got_z, weight_x, weight_z,
    part_x, part_z, sum_x, sum_z, near_x, off_x, off_z,
    metric_x, metric_z, st,
    local_sem, fx_send, fx_recv, fz_send, fz_recv, x_send, x_recv, z_send, z_recv,
    bx_send, bx_recv, bz_send, bz_recv,
    x_sems, z_sems,
):
    g = lax.axis_index("grid")
    y = lax.axis_index("lev")
    z = lax.div(g, 8)
    x = lax.rem(lax.div(g, 2), 4)
    c = lax.rem(g, 2)
    mine_x = 2 * x + c
    mine_z = 2 * z + c
    xs = [x] + [lax.rem(x + d, 4) for d in range(1, 4)]
    zs = [z] + [lax.rem(z + d, 4) for d in range(1, 4)]
    ys = [y] + [lax.rem(y + d, 4) for d in range(1, 4)]
    cs = [c, 1 - c]

    def device(xx, zz, cc, yy):
        return (zz * 8 + xx * 2 + cc, yy)

    sibling = device(x, z, 1 - c, y)
    x_peers = [(xs[STEP[i]], cs[i % 2]) for i in range(8)]
    z_peers = [(zs[STEP[i]], cs[i % 2]) for i in range(8)]

    def remote(src, dst, send_sem, recv_sem, to):
        return pltpu.make_async_remote_copy(
            src_ref=src, dst_ref=dst, send_sem=send_sem, recv_sem=recv_sem,
            device_id=to, device_id_type=MESH)

    def wait_for(slot, send, recv):
        remote(slot, slot, send, recv, sibling).wait_recv()

    def loop(first, last):
        def run(body):
            lax.fori_loop(first, last, lambda i, carry: (body(i), carry)[1], 0)
        return run

    barrier = pltpu.get_barrier_semaphore()

    def greet(to):
        pl.semaphore_signal(barrier, inc=1, device_id=to, device_id_type=MESH)

    for i in ORDER:
        xx, cc = x_peers[i]
        greet(device(xx, z, cc, y))
        if i != 1:
            zz, cc = z_peers[i]
            greet(device(x, zz, cc, y))
    for d in (2, 1, 3):
        greet(device(x, z, c, ys[d]))

    def x_slot(i, half):
        return got_x.at[pl.ds(ONES + STARTS[half], ROWS_X[half]), pl.ds(F * i, F)]

    def z_slot(i):
        return got_z.at[pl.ds(0, ROWS_Z), pl.ds(F * i, F)]

    def x_tile(xx, cc):
        return tiles.at[12 * y + 2 * xx + cc]

    def z_tile(zz, cc):
        return tiles.at[12 * y + 8 + zz, pl.ds(pl.multiple_of(HALF * cc, HALF), ROWS_Z)]

    local = [
        pltpu.make_async_copy(farm_area, area_in, local_sem.at[0]),
        pltpu.make_async_copy(capacity, capacity_in, local_sem.at[1]),
        pltpu.make_async_copy(offsets, offsets_in, local_sem.at[2]),
        pltpu.make_async_copy(z_tile(z, c), z_slot(0), local_sem.at[3]),
        pltpu.make_async_copy(x_tile(x, c), got_x.at[pl.ds(ONES, T), pl.ds(0, F)], local_sem.at[4]),
        pltpu.make_async_copy(state, st, local_sem.at[5]),
    ]
    for copy in local:
        copy.start()
    def fx_copy(i):
        xx, cc = x_peers[i]
        return remote(facts_x.at[0], facts_x.at[BACK[i]], fx_send.at[i], fx_recv.at[BACK[i]],
                      device(xx, z, cc, y))

    def fz_copy(i):
        zz, cc = z_peers[i]
        return remote(facts_z.at[0], facts_z.at[BACK[i]], fz_send.at[i], fz_recv.at[BACK[i]],
                      device(x, zz, cc, y))

    def x_copy(i, half):
        xx, cc = x_peers[i]
        return remote(x_tile(xx, cc).at[pl.ds(STARTS[half], ROWS_X[half])], x_slot(BACK[i], half),
                      x_send.at[half, i], x_recv.at[half, BACK[i]], device(xx, z, cc, y))

    def z_copy(i):
        zz, cc = z_peers[i]
        return remote(z_tile(zz, cc), z_slot(BACK[i]), z_send.at[i], z_recv.at[BACK[i]],
                      device(x, zz, cc, y))

    sends = []

    def start(*copies):
        for copy in copies:
            copy.start()
            sends.append(copy)

    for copy in local[:3]:
        copy.wait()

    lane = iota((1, F), 1)
    offset = jnp.zeros((1, F), jnp.int32)
    for k in range(16):
        offset = jnp.where((lane & 15) == k, offsets_in[k], offset)
    area = area_in[...]
    turned = ((area >> 5) & 3) * 128 + (area >> 7) * 32 + (area & 31)
    for facts, ids, spot in ((facts_z, turned, mine_z), (facts_x, area, mine_x)):
        placed = jnp.where((lane >> 4) == spot, offset, 0)
        rows = jnp.concatenate(
            [ids, capacity_in[...], placed, jnp.zeros((1, F), jnp.int32)], axis=0)
        facts[0] = rows.astype(jnp.float32)

    pl.semaphore_wait(barrier, 16)
    for i in ORDER:
        start(fx_copy(i), fz_copy(i))
    for i in ORDER:
        start(x_copy(i, 0), z_copy(i))
    for i in ORDER[2:] + ORDER[:2]:
        start(x_copy(i, 1))

    got_x[pl.ds(0, ONES)] = jnp.ones((ONES, 8 * F), jnp.bfloat16)
    got_z[pl.ds(ROWS_Z, 16)] = jnp.ones((16, 8 * F), jnp.bfloat16)
    off_x[...] = jnp.zeros_like(off_x)
    off_z[...] = jnp.zeros_like(off_z)
    area_ids = iota((AREAS, F), 0).astype(jnp.float32)

    def weigh(i, facts, weight, off):
        rows = facts[i]
        off[...] = off[...] + rows[2:3, :LANES]
        placed = jnp.where(area_ids == rows[0:1], rows[1:2], 0.0)
        weight[:, pl.ds(pl.multiple_of(F * i, F), F)] = placed.astype(jnp.bfloat16)

    @loop(0, 8)
    def _(i):
        for facts, recv, send, weight, off in (
                (facts_z, fz_recv, fz_send, weight_z, off_z),
                (facts_x, fx_recv, fx_send, weight_x, off_x)):
            @pl.when(i > 0)
            def _():
                wait_for(facts.at[i], send.at[i], recv.at[i])

            weigh(i, facts, weight, off)

    def sum_up(values, weights):
        return lax.dot_general(values, weights, (((1,), (1,)), ((), ())),
                               preferred_element_type=jnp.float32)

    bz = []

    near, far = pl.ds(0, NEAR * F), pl.ds(NEAR * F, (8 - NEAR) * F)

    def block_pair(p):
        return lax.rem(z + 2 + p, 4), lax.rem(z + 1 + 3 * p, 4)

    def dot_x(first, count, p, columns):
        chosen = jnp.concatenate(
            [weight_x[pl.ds(pl.multiple_of(LANES * zz, LANES), LANES), columns]
             for zz in block_pair(p)], axis=0)
        return sum_up(got_x[pl.ds(first, count), columns], chosen)

    def sum_copy(half, rows, d, zz):
        return remote(part_x.at[zz, rows], sum_x.at[3 - d, rows], bx_send.at[half, d - 1],
                      bx_recv.at[half, 3 - d], device(x, zz, c, y))

    def leave(half, rows, p, value):
        for k, zz in enumerate(block_pair(p)):
            part_x[zz, rows] = value[:, k * LANES : (k + 1) * LANES]
        sum_copy(half, rows, 2 + p, block_pair(p)[0]).start()

        @pl.when(p == 0)
        def _():
            sum_copy(half, rows, 1, zs[1]).start()

    early_rows, late_rows = pl.ds(0, 8 + ROWS_X[0]), pl.ds(8 + ROWS_X[0], ROWS_X[1])
    local[4].wait()
    for i in range(1, 8):
        wait_for(x_slot(i, 0), x_send.at[0, i], x_recv.at[0, i])

    @loop(0, 2)
    def _(p):
        leave(0, early_rows, p, dot_x(0, ONES + ROWS_X[0], p, pl.ds(0, 8 * F))[8:])

    local[3].wait()
    for i in range(1, 8):
        wait_for(z_slot(i), z_send.at[i], z_recv.at[i])
    for h in range(2):
        value = sum_up(got_z[...], weight_z[pl.ds(2 * LANES * h, 2 * LANES)])
        for b in range(2):
            part_z[2 * h + b] = value[:KEEP_Z, b * LANES : (b + 1) * LANES]
    for d in (2, 1, 3):
        copy = remote(part_z.at[xs[d]], sum_z.at[3 - d], bz_send.at[d - 1], bz_recv.at[3 - d],
                      device(xs[d], z, c, y))
        copy.start()
        bz.append(copy)

    for i in range(1, NEAR):
        wait_for(x_slot(i, 1), x_send.at[1, i], x_recv.at[1, i])

    @loop(0, 2)
    def _(p):
        near_x[p] = dot_x(ONES + ROWS_X[0], ROWS_X[1], p, near)

    for i in range(NEAR, 8):
        wait_for(x_slot(i, 1), x_send.at[1, i], x_recv.at[1, i])

    @loop(0, 2)
    def _(p):
        leave(1, late_rows, p, near_x[p] + dot_x(ONES + ROWS_X[0], ROWS_X[1], p, far))

    bx = [[sum_copy(half, rows, d, zs[d]) for d in range(1, 4)]
          for half, rows in ((0, early_rows), (1, late_rows))]

    def whole(copies, own, others, rows):
        for copy in copies:
            copy.wait_recv()
        total = own[rows]
        for k in range(3):
            total = total + others[k, rows]
        return total

    spot = (4 * y + z) * 8 + mine_x

    def broadcast(metrics, sem):
        mine = metrics.at[spot]

        def one(xx, zz, cc, yy):
            remote(mine, mine, sem.at[0], sem.at[1], device(xx, zz, cc, yy)).start()

        @loop(0, 15)
        def _(k):
            step = 1 + lax.rem(k + 9, 15)
            yy, zz = lax.rem(y + lax.div(step, 4), 4), lax.rem(z + lax.rem(step, 4), 4)
            for i in (6, 7, 2, 3, 4, 5, 0, 1):
                xx, cc = x_peers[i]
                one(xx, zz, cc, yy)

        for i in ORDER:
            xx, cc = x_peers[i]
            one(xx, z, cc, y)
        others = metrics.at[pl.ds(0, 127)]
        return remote(others, others, sem.at[0], sem.at[1], sibling)

    last = whole(bz, part_z.at[x], sum_z, pl.ds(0, KEEP_Z))
    metric_z[spot] = ramp_metric(
        last[:ROWS_Z] / jnp.maximum(last[ROWS_Z : ROWS_Z + 1], capacity_floor),
        off_z[...], 0, RAMPS_Z)
    all_z = broadcast(metric_z, z_sems)
    first = whole(bx[0], part_x.at[z], sum_x, early_rows)
    total = jnp.maximum(first[:1], capacity_floor)
    power = first[8:] / total
    early = ramp_metric(power, off_x[...], 0, 84)
    last = whole(bx[1], part_x.at[z], sum_x, late_rows)
    power = jnp.concatenate([power[80:], last / total], axis=0)
    late = ramp_metric(power, off_x[...], 4, 52)
    metric_x[spot] = jnp.maximum(early, late)
    all_x = broadcast(metric_x, x_sems)

    local[5].wait()

    @loop(0, QUADS)
    def _(i):
        values = st[:, i].astype(jnp.float32).reshape(M, 2, 8, LANES)
        values = values - (jnp.sum(values, axis=0) / M)[None]
        pairs = values.reshape(M // 2, 2, 2, 8, LANES)
        for h in range(2):
            both = swap_halves(pairs[:, 0, h], pairs[:, 1, h])
            for k in range(2):
                slab_out[i, :, pl.ds((2 * h + k) * LANES, LANES)] = (
                    both[k].reshape(4 * M, LANES).astype(jnp.bfloat16))

    for copy in sends + bx[0] + bx[1] + bz:
        copy.wait_send()

    all_z.wait_recv()
    all_x.wait_recv()

    rows = metric_x.reshape(128, LANES)
    for yy in range(4):
        for zz in range(4):
            metric_out[pl.ds(8 * yy, 8), pl.ds(LANES * zz, LANES)] = (
                rows[pl.ds(8 * (4 * yy + zz), 8)])
    rows = metric_z.reshape(128, LANES)
    quarter = iota((16, LANES), 1) >> 5
    blocks = [jnp.maximum(rows[pl.ds(2 * b, 16, stride=8)], rows[pl.ds(2 * b + 1, 16, stride=8)])
              for b in range(RING)]
    for zz in range(4):
        value = jnp.zeros((16, LANES), jnp.float32)
        for b in range(RING):
            move = (32 * (b - zz)) % LANES
            moved = pltpu.roll(blocks[b], move, 1) if move else blocks[b]
            value = jnp.where(quarter == b, moved, value)
        metric_out[pl.ds(32, 16), pl.ds(zz * LANES, LANES)] = value

    all_z.wait_send()
    all_x.wait_send()


def exchange(tiles, farm_area, capacity, offsets, state):
    any_space = pl.BlockSpec(memory_space=pl.ANY)
    vmem = pl.BlockSpec(memory_space=pltpu.VMEM)
    dma = pltpu.SemaphoreType.DMA
    f32, bf16 = jnp.float32, jnp.bfloat16
    return pl.pallas_call(
        exchange_kernel,
        out_shape=(
            pltpu.VMEM((M, AREAS), f32),
            pltpu.VMEM((QUADS, 4 * M, 4 * LANES), bf16),
        ),
        in_specs=[any_space] * 5,
        out_specs=(vmem, vmem),
        scratch_shapes=[
            pltpu.VMEM((1, F), jnp.int32),
            pltpu.VMEM((1, F), jnp.int32),
            pltpu.SMEM((16,), jnp.int32),
            pltpu.VMEM((8, 4, F), f32),
            pltpu.VMEM((8, 4, F), f32),
            pltpu.VMEM((PAD_X, 8 * F), bf16),
            pltpu.VMEM((PAD_Z, 8 * F), bf16),
            pltpu.VMEM((AREAS, 8 * F), bf16),
            pltpu.VMEM((AREAS, 8 * F), bf16),
            pltpu.VMEM((RING, KEEP_X, LANES), f32),
            pltpu.VMEM((RING, KEEP_Z, LANES), f32),
            pltpu.VMEM((3, KEEP_X, LANES), f32),
            pltpu.VMEM((3, KEEP_Z, LANES), f32),
            pltpu.VMEM((2, ROWS_X[1], 2 * LANES), f32),
            pltpu.VMEM((1, LANES), f32),
            pltpu.VMEM((1, LANES), f32),
            pltpu.VMEM((128, 1, LANES), f32),
            pltpu.VMEM((128, 1, LANES), f32),
            pltpu.VMEM((M, QUADS, 16, LANES), bf16),
            dma((6,)), dma((8,)), dma((8,)), dma((8,)), dma((8,)),
            dma((2, 8)), dma((2, 8)), dma((8,)), dma((8,)),
            dma((2, 3)), dma((2, 3)), dma((3,)), dma((3,)),
            dma((2,)), dma((2,)),
        ],
        compiler_params=pltpu.CompilerParams(
            collective_id=0, has_side_effects=True, vmem_limit_bytes=60 * 2**20),
        cost_estimate=pl.CostEstimate(
            flops=2 * 256 * 2048 * 512, bytes_accessed=5 * 2**20, transcendentals=0),
        name="exchange",
    )(tiles, farm_area, capacity, offsets, state)


def product_kernel(metric, slab, out, wide, lhs, stage, out_sem):
    values = metric[...]
    anomaly = values - jnp.mean(values, axis=0, keepdims=True)
    spread = jnp.sqrt(jnp.sum(anomaly * anomaly, axis=0, keepdims=True) / (M - 1))
    scores = anomaly / jnp.maximum(spread, spread_floor)
    scores = jnp.transpose(scores).astype(jnp.bfloat16)

    held = iota((M, 4 * M), 0)
    rest = held - 32
    member = jnp.where(
        held < 32,
        12 * (held >> 3) + (held & 7),
        12 * (rest >> 2) + 8 + (rest & 3))
    widen = ((iota((M, 4 * M), 1) >> 2) == member).astype(jnp.bfloat16)
    wide[...] = jnp.dot(scores, widen, preferred_element_type=jnp.float32).astype(jnp.bfloat16)
    repeat = ((iota((ROWS, ROWS // 4), 0) >> 2) == iota((ROWS, ROWS // 4), 1)).astype(
        jnp.bfloat16)
    keep = (iota((ROWS, 4 * M), 0) & 3) == (iota((ROWS, 4 * M), 1) & 3)
    areas = ROWS // 4

    half = 4 * AREAS // ROWS // 2

    def part(q, i):
        some = pl.ds(pl.multiple_of(2 * areas * q, 2 * areas), 2 * areas)
        return pltpu.make_async_copy(stage.at[some, i], out.at[some, i], out_sem.at[QUADS * q + i])

    def step(q, carry):
        first = [pl.multiple_of((2 * q + r) * areas, areas) for r in range(2)]
        for r in range(2):
            rows = jnp.dot(repeat, wide[pl.ds(first[r], areas)],
                           preferred_element_type=jnp.float32)
            lhs[r] = jnp.where(keep, rows, 0.0).astype(jnp.bfloat16)
        for i in range(QUADS):
            for r in range(2):
                parts = []
                for h in range(2):
                    acc = jnp.dot(lhs[r], slab[i, :, pl.ds(2 * LANES * h, 2 * LANES)],
                                  preferred_element_type=jnp.float32)
                    acc = (acc * (1.0 / (M - 1))).reshape(ROWS // 8, 8, 2 * LANES)
                    both = swap_halves(acc[:, :, :LANES], acc[:, :, LANES:])
                    parts.append(jnp.stack(both, axis=1).reshape(areas, 8, LANES))
                done = jnp.stack(parts, axis=1).reshape(areas, 16, LANES)
                stage[pl.ds(first[r], areas), i] = done.astype(jnp.bfloat16)
            part(q, i).start(priority=i % 2)
        return carry

    lax.fori_loop(0, half, step, 0)

    def finish(q, carry):
        for i in range(QUADS):
            part(q, i).wait()
        return carry

    lax.fori_loop(0, half, finish, 0)


def product(metric, slab):
    any_space = pl.BlockSpec(memory_space=pl.ANY)
    dma = pltpu.SemaphoreType.DMA
    return pl.pallas_call(
        product_kernel,
        out_shape=jax.ShapeDtypeStruct((AREAS, QUADS, 16, LANES), jnp.bfloat16),
        in_specs=[pl.BlockSpec(memory_space=pltpu.VMEM)] * 2,
        out_specs=any_space,
        scratch_shapes=[
            pltpu.VMEM((AREAS, 4 * M), jnp.bfloat16),
            pltpu.VMEM((2, ROWS, 4 * M), jnp.bfloat16),
            pltpu.VMEM((AREAS, QUADS, 16, LANES), jnp.bfloat16),
            dma((32,)),
        ],
        compiler_params=pltpu.CompilerParams(vmem_limit_bytes=32 * 2**20),
        cost_estimate=pl.CostEstimate(
            flops=2 * 2048 * 192 * 4096, bytes_accessed=20 * 2**20, transcendentals=0),
        name="product",
    )(metric, slab)


def body(tiles, farm_area, capacity, offsets, state):
    by_member = jnp.transpose(tiles, (1, 2, 0))
    columns = state.reshape(M, 2, 64, LANES)
    columns = jnp.transpose(columns, (0, 2, 1, 3)).reshape(M, QUADS, 16, LANES)
    metric, slab = exchange(
        by_member, farm_area.reshape(1, F), capacity.reshape(1, F), offsets, columns)
    out = product(metric, slab)
    out = jnp.transpose(out.reshape(AREAS, 64, 2, LANES), (0, 2, 1, 3))
    return out.reshape(AREAS, 2, 64 * LANES)


def solution(mesh):
    in_specs = (P("grid", None, None), P("grid"), P("grid"), P("grid"), P(None, "lev", "grid"))
    out_specs = P(None, "lev", "grid")
    return jax.shard_map(body, mesh=mesh, in_specs=in_specs, out_specs=out_specs, check_vma=False)
```

```python
import jax
import jax.numpy as jnp
from jax import lax
from jax.experimental import pallas as pl
from jax.experimental.pallas import tpu as pltpu
from jax.sharding import PartitionSpec as P

MESH = pl.DeviceIdType.MESH
M = 48
T = 144
F = 256
AREAS = 512
LANES = 128
RING = 4
ONES = 16
PAD_X = ONES + T
ROWS_Z = 80
PAD_Z = 96
HALF = 64
RAMPS = 132
RAMPS_Z = 68
KEEP_X = 152
KEEP_Z = 88
QUADS = 8
ROWS = 256
capacity_floor = 200.0
spread_floor = 0.05


def iota(shape, dim):
    return lax.broadcasted_iota(jnp.int32, shape, dim)


def swap_halves(u, v):
    low = iota(u.shape, 1) < 4
    crossed = pltpu.roll(jnp.where(low, v, u), 4, 1)
    return jnp.where(low, u, crossed), jnp.where(low, crossed, v)


def ramp_metric(power, offset, first, last):
    steps = power.shape[0]
    wide = jnp.broadcast_to(offset, power.shape).astype(jnp.int32)
    later = power
    for bit in (1, 2, 4, 8):
        later = jnp.where((wide & bit) != 0, pltpu.roll(later, steps - bit, 0), later)
    row = iota(power.shape, 0)
    inside = (row >= first) & (row < last)
    return jnp.max(jnp.where(inside, later - power, -3e38), axis=0, keepdims=True)


STEP = (0, 0, 1, 1, 3, 3, 2, 2)
BACK = (0, 1, 4, 5, 2, 3, 6, 7)
ORDER = (6, 7, 2, 4, 3, 5, 1)
NEAR = 6
STARTS, ROWS_X = (0, 96), (96, 48)


def exchange_kernel(
    tiles, farm_area, capacity, offsets, state, metric_out, slab_out,
    area_in, capacity_in, offsets_in, near_tiles,
    facts_x, facts_z, got_x, got_z, weight_x, weight_z,
    part_x, part_z, sum_x, sum_z, near_x, off_x, off_z,
    metrics, st,
    local_sem, fx_send, fx_recv, fz_send, fz_recv, x_send, x_recv, z_send, z_recv,
    bx_send, bx_recv, bz_send, bz_recv,
    all_send, all_recv,
):
    g = lax.axis_index("grid")
    y = lax.axis_index("lev")
    z = lax.div(g, 8)
    x = lax.rem(lax.div(g, 2), 4)
    c = lax.rem(g, 2)
    mine_x = 2 * x + c
    mine_z = 2 * z + c
    xs = [x] + [lax.rem(x + d, 4) for d in range(1, 4)]
    zs = [z] + [lax.rem(z + d, 4) for d in range(1, 4)]
    ys = [y] + [lax.rem(y + d, 4) for d in range(1, 4)]
    cs = [c, 1 - c]

    def device(xx, zz, cc, yy):
        return (zz * 8 + xx * 2 + cc, yy)

    sibling = device(x, z, 1 - c, y)
    x_peers = [(xs[STEP[i]], cs[i % 2]) for i in range(8)]
    z_peers = [(zs[STEP[i]], cs[i % 2]) for i in range(8)]

    def remote(src, dst, send_sem, recv_sem, to):
        return pltpu.make_async_remote_copy(
            src_ref=src, dst_ref=dst, send_sem=send_sem, recv_sem=recv_sem,
            device_id=to, device_id_type=MESH)

    def wait_for(slot, send, recv):
        remote(slot, slot, send, recv, sibling).wait_recv()

    def loop(first, last):
        def run(body):
            lax.fori_loop(first, last, lambda i, carry: (body(i), carry)[1], 0)
        return run

    barrier = pltpu.get_barrier_semaphore()

    def greet(to):
        pl.semaphore_signal(barrier, inc=1, device_id=to, device_id_type=MESH)

    for i in ORDER:
        xx, cc = x_peers[i]
        greet(device(xx, z, cc, y))
        if i != 1:
            zz, cc = z_peers[i]
            greet(device(x, zz, cc, y))
    for d in (2, 1, 3):
        greet(device(x, z, c, ys[d]))

    def x_slot(i, half):
        return got_x.at[pl.ds(ONES + STARTS[half], ROWS_X[half]), pl.ds(F * i, F)]

    def z_slot(i):
        return got_z.at[pl.ds(0, ROWS_Z), pl.ds(F * i, F)]

    def x_tile(xx, cc):
        return near_tiles.at[2 * xx + cc]

    def z_tile(zz, cc):
        return near_tiles.at[8 + zz, pl.ds(pl.multiple_of(HALF * cc, HALF), ROWS_Z)]

    local = [
        pltpu.make_async_copy(farm_area, area_in, local_sem.at[0]),
        pltpu.make_async_copy(capacity, capacity_in, local_sem.at[1]),
        pltpu.make_async_copy(offsets, offsets_in, local_sem.at[2]),
        pltpu.make_async_copy(tiles.at[pl.ds(12 * y, 12)], near_tiles, local_sem.at[6]),
        pltpu.make_async_copy(
            tiles.at[12 * y + 8 + z, pl.ds(pl.multiple_of(HALF * c, HALF), ROWS_Z)],
            z_slot(0), local_sem.at[3]),
        pltpu.make_async_copy(
            tiles.at[12 * y + mine_x], got_x.at[pl.ds(ONES, T), pl.ds(0, F)], local_sem.at[4]),
        pltpu.make_async_copy(state, st, local_sem.at[5]),
    ]
    for copy in local:
        copy.start()
    def fx_copy(i):
        xx, cc = x_peers[i]
        return remote(facts_x.at[0], facts_x.at[BACK[i]], fx_send.at[i], fx_recv.at[BACK[i]],
                      device(xx, z, cc, y))

    def fz_copy(i):
        zz, cc = z_peers[i]
        return remote(facts_z.at[0], facts_z.at[BACK[i]], fz_send.at[i], fz_recv.at[BACK[i]],
                      device(x, zz, cc, y))

    def x_copy(i, half):
        xx, cc = x_peers[i]
        return remote(x_tile(xx, cc).at[pl.ds(STARTS[half], ROWS_X[half])], x_slot(BACK[i], half),
                      x_send.at[half, i], x_recv.at[half, BACK[i]], device(xx, z, cc, y))

    def z_copy(i):
        zz, cc = z_peers[i]
        return remote(z_tile(zz, cc), z_slot(BACK[i]), z_send.at[i], z_recv.at[BACK[i]],
                      device(x, zz, cc, y))

    sends = []

    def start(*copies):
        for copy in copies:
            copy.start()
            sends.append(copy)

    for copy in local[:3]:
        copy.wait()

    lane = iota((1, F), 1)
    offset = jnp.zeros((1, F), jnp.int32)
    for k in range(16):
        offset = jnp.where((lane & 15) == k, offsets_in[k], offset)
    area = area_in[...]
    turned = ((area >> 5) & 3) * 128 + (area >> 7) * 32 + (area & 31)
    for facts, ids, spot in ((facts_z, turned, mine_z), (facts_x, area, mine_x)):
        placed = jnp.where((lane >> 4) == spot, offset, 0)
        rows = jnp.concatenate(
            [ids, capacity_in[...], placed, jnp.zeros((1, F), jnp.int32)], axis=0)
        facts[0] = rows.astype(jnp.float32)

    pl.semaphore_wait(barrier, 16)
    for i in ORDER:
        start(fx_copy(i), fz_copy(i))
    local[3].wait()
    for i in ORDER:
        start(x_copy(i, 0), z_copy(i))
    for i in ORDER[2:] + ORDER[:2]:
        start(x_copy(i, 1))

    got_x[pl.ds(0, ONES)] = jnp.ones((ONES, 8 * F), jnp.bfloat16)
    got_z[pl.ds(ROWS_Z, 16)] = jnp.ones((16, 8 * F), jnp.bfloat16)
    off_x[...] = jnp.zeros_like(off_x)
    off_z[...] = jnp.zeros_like(off_z)
    area_ids = iota((AREAS, F), 0).astype(jnp.float32)

    def weigh(i, facts, weight, off):
        rows = facts[i]
        off[...] = off[...] + rows[2:3, :LANES]
        placed = jnp.where(area_ids == rows[0:1], rows[1:2], 0.0)
        weight[:, pl.ds(pl.multiple_of(F * i, F), F)] = placed.astype(jnp.bfloat16)

    @loop(0, 8)
    def _(i):
        for facts, recv, send, weight, off in (
                (facts_z, fz_recv, fz_send, weight_z, off_z),
                (facts_x, fx_recv, fx_send, weight_x, off_x)):
            @pl.when(i > 0)
            def _():
                wait_for(facts.at[i], send.at[i], recv.at[i])

            weigh(i, facts, weight, off)

    def sum_up(values, weights):
        return lax.dot_general(values, weights, (((1,), (1,)), ((), ())),
                               preferred_element_type=jnp.float32)

    bz = []

    near, far = pl.ds(0, NEAR * F), pl.ds(NEAR * F, (8 - NEAR) * F)

    def block_pair(p):
        return lax.rem(z + 2 + p, 4), lax.rem(z + 1 + 3 * p, 4)

    def dot_x(first, count, p, columns):
        chosen = jnp.concatenate(
            [weight_x[pl.ds(pl.multiple_of(LANES * zz, LANES), LANES), columns]
             for zz in block_pair(p)], axis=0)
        return sum_up(got_x[pl.ds(first, count), columns], chosen)

    def sum_copy(half, rows, d, zz):
        return remote(part_x.at[zz, rows], sum_x.at[3 - d, rows], bx_send.at[half, d - 1],
                      bx_recv.at[half, 3 - d], device(x, zz, c, y))

    def leave(half, rows, p, value):
        for k, zz in enumerate(block_pair(p)):
            part_x[zz, rows] = value[:, k * LANES : (k + 1) * LANES]
        sum_copy(half, rows, 2 + p, block_pair(p)[0]).start()

        @pl.when(p == 0)
        def _():
            sum_copy(half, rows, 1, zs[1]).start()

    early_rows, late_rows = pl.ds(0, 8 + ROWS_X[0]), pl.ds(8 + ROWS_X[0], ROWS_X[1])
    local[5].wait()
    for i in range(1, 8):
        wait_for(x_slot(i, 0), x_send.at[0, i], x_recv.at[0, i])

    @loop(0, 2)
    def _(p):
        leave(0, early_rows, p, dot_x(0, ONES + ROWS_X[0], p, pl.ds(0, 8 * F))[8:])

    local[4].wait()
    for i in range(1, 8):
        wait_for(z_slot(i), z_send.at[i], z_recv.at[i])
    for h in range(2):
        value = sum_up(got_z[...], weight_z[pl.ds(2 * LANES * h, 2 * LANES)])
        for b in range(2):
            part_z[2 * h + b] = value[:KEEP_Z, b * LANES : (b + 1) * LANES]
    for d in (2, 1, 3):
        copy = remote(part_z.at[xs[d]], sum_z.at[3 - d], bz_send.at[d - 1], bz_recv.at[3 - d],
                      device(xs[d], z, c, y))
        copy.start()
        bz.append(copy)

    for i in range(1, NEAR):
        wait_for(x_slot(i, 1), x_send.at[1, i], x_recv.at[1, i])

    @loop(0, 2)
    def _(p):
        near_x[p] = dot_x(ONES + ROWS_X[0], ROWS_X[1], p, near)

    for i in range(NEAR, 8):
        wait_for(x_slot(i, 1), x_send.at[1, i], x_recv.at[1, i])

    @loop(0, 2)
    def _(p):
        leave(1, late_rows, p, near_x[p] + dot_x(ONES + ROWS_X[0], ROWS_X[1], p, far))

    bx = [[sum_copy(half, rows, d, zs[d]) for d in range(1, 4)]
          for half, rows in ((0, early_rows), (1, late_rows))]

    def whole(copies, own, others, rows):
        for copy in copies:
            copy.wait_recv()
        total = own[rows]
        for k in range(3):
            total = total + others[k, rows]
        return total

    spot = (4 * y + z) * 8 + mine_x

    first = whole(bx[0], part_x.at[z], sum_x, early_rows)
    total = jnp.maximum(first[:1], capacity_floor)
    power = first[8:] / total
    early = ramp_metric(power, off_x[...], 0, 84)
    last = whole(bz, part_z.at[x], sum_z, pl.ds(0, KEEP_Z))
    metrics[spot, pl.ds(1, 1)] = ramp_metric(
        last[:ROWS_Z] / jnp.maximum(last[ROWS_Z : ROWS_Z + 1], capacity_floor),
        off_z[...], 0, RAMPS_Z)
    last = whole(bx[1], part_x.at[z], sum_x, late_rows)
    power = jnp.concatenate([power[80:], last / total], axis=0)
    late = ramp_metric(power, off_x[...], 4, 52)
    metrics[spot, pl.ds(0, 1)] = jnp.maximum(early, late)

    mine = metrics.at[spot]

    def broadcast(xx, zz, cc, yy):
        remote(mine, mine, all_send, all_recv, device(xx, zz, cc, yy)).start()

    @loop(0, 15)
    def _(k):
        step = 1 + lax.rem(k + 9, 15)
        yy, zz = lax.rem(y + lax.div(step, 4), 4), lax.rem(z + lax.rem(step, 4), 4)
        for i in (6, 7, 2, 3, 4, 5, 0, 1):
            xx, cc = x_peers[i]
            broadcast(xx, zz, cc, yy)

    for i in ORDER:
        xx, cc = x_peers[i]
        broadcast(xx, z, cc, y)

    local[6].wait()

    @loop(0, QUADS)
    def _(i):
        values = st[:, i].astype(jnp.float32).reshape(M, 2, 8, LANES)
        values = values - (jnp.sum(values, axis=0) / M)[None]
        pairs = values.reshape(M // 2, 2, 2, 8, LANES)
        for h in range(2):
            both = swap_halves(pairs[:, 0, h], pairs[:, 1, h])
            for k in range(2):
                slab_out[i, :, pl.ds((2 * h + k) * LANES, LANES)] = (
                    both[k].reshape(4 * M, LANES).astype(jnp.bfloat16))

    for copy in sends + bx[0] + bx[1] + bz:
        copy.wait_send()

    others = metrics.at[pl.ds(0, 127)]
    everything = remote(others, others, all_send, all_recv, sibling)
    everything.wait_recv()

    rows = metrics.reshape(256, LANES)
    for yy in range(4):
        for zz in range(4):
            metric_out[pl.ds(8 * yy, 8), pl.ds(LANES * zz, LANES)] = (
                rows[pl.ds(16 * (4 * yy + zz), 8, stride=2)])
    quarter = iota((16, LANES), 1) >> 5
    blocks = [jnp.maximum(rows[pl.ds(4 * b + 1, 16, stride=16)], rows[pl.ds(4 * b + 3, 16, stride=16)])
              for b in range(RING)]
    for zz in range(4):
        value = jnp.zeros((16, LANES), jnp.float32)
        for b in range(RING):
            move = (32 * (b - zz)) % LANES
            moved = pltpu.roll(blocks[b], move, 1) if move else blocks[b]
            value = jnp.where(quarter == b, moved, value)
        metric_out[pl.ds(32, 16), pl.ds(zz * LANES, LANES)] = value

    everything.wait_send()


def exchange(tiles, farm_area, capacity, offsets, state):
    any_space = pl.BlockSpec(memory_space=pl.ANY)
    vmem = pl.BlockSpec(memory_space=pltpu.VMEM)
    dma = pltpu.SemaphoreType.DMA
    f32, bf16 = jnp.float32, jnp.bfloat16
    return pl.pallas_call(
        exchange_kernel,
        out_shape=(
            pltpu.VMEM((M, AREAS), f32),
            pltpu.VMEM((QUADS, 4 * M, 4 * LANES), bf16),
        ),
        in_specs=[any_space] * 5,
        out_specs=(vmem, vmem),
        scratch_shapes=[
            pltpu.VMEM((1, F), jnp.int32),
            pltpu.VMEM((1, F), jnp.int32),
            pltpu.SMEM((16,), jnp.int32),
            pltpu.VMEM((12, T, F), bf16),
            pltpu.VMEM((8, 4, F), f32),
            pltpu.VMEM((8, 4, F), f32),
            pltpu.VMEM((PAD_X, 8 * F), bf16),
            pltpu.VMEM((PAD_Z, 8 * F), bf16),
            pltpu.VMEM((AREAS, 8 * F), bf16),
            pltpu.VMEM((AREAS, 8 * F), bf16),
            pltpu.VMEM((RING, KEEP_X, LANES), f32),
            pltpu.VMEM((RING, KEEP_Z, LANES), f32),
            pltpu.VMEM((3, KEEP_X, LANES), f32),
            pltpu.VMEM((3, KEEP_Z, LANES), f32),
            pltpu.VMEM((2, ROWS_X[1], 2 * LANES), f32),
            pltpu.VMEM((1, LANES), f32),
            pltpu.VMEM((1, LANES), f32),
            pltpu.VMEM((128, 2, LANES), f32),
            pltpu.VMEM((M, QUADS, 16, LANES), bf16),
            dma((7,)), dma((8,)), dma((8,)), dma((8,)), dma((8,)),
            dma((2, 8)), dma((2, 8)), dma((8,)), dma((8,)),
            dma((2, 3)), dma((2, 3)), dma((3,)), dma((3,)),
            dma, dma,
        ],
        compiler_params=pltpu.CompilerParams(
            collective_id=0, has_side_effects=True, vmem_limit_bytes=60 * 2**20),
        cost_estimate=pl.CostEstimate(
            flops=2 * 256 * 2048 * 512, bytes_accessed=5 * 2**20, transcendentals=0),
        name="exchange",
    )(tiles, farm_area, capacity, offsets, state)


def product_kernel(metric, slab, out, wide, lhs, stage, out_sem):
    values = metric[...]
    anomaly = values - jnp.mean(values, axis=0, keepdims=True)
    spread = jnp.sqrt(jnp.sum(anomaly * anomaly, axis=0, keepdims=True) / (M - 1))
    scores = anomaly / jnp.maximum(spread, spread_floor)
    scores = jnp.transpose(scores).astype(jnp.bfloat16)

    held = iota((M, 4 * M), 0)
    rest = held - 32
    member = jnp.where(
        held < 32,
        12 * (held >> 3) + (held & 7),
        12 * (rest >> 2) + 8 + (rest & 3))
    widen = ((iota((M, 4 * M), 1) >> 2) == member).astype(jnp.bfloat16)
    wide[...] = jnp.dot(scores, widen, preferred_element_type=jnp.float32).astype(jnp.bfloat16)
    repeat = ((iota((ROWS, ROWS // 4), 0) >> 2) == iota((ROWS, ROWS // 4), 1)).astype(
        jnp.bfloat16)
    keep = (iota((ROWS, 4 * M), 0) & 3) == (iota((ROWS, 4 * M), 1) & 3)
    areas = ROWS // 4

    half = 4 * AREAS // ROWS // 2

    def part(q, i):
        some = pl.ds(pl.multiple_of(2 * areas * q, 2 * areas), 2 * areas)
        return pltpu.make_async_copy(stage.at[some, i], out.at[some, i], out_sem.at[QUADS * q + i])

    def step(q, carry):
        first = [pl.multiple_of((2 * q + r) * areas, areas) for r in range(2)]
        for r in range(2):
            rows = jnp.dot(repeat, wide[pl.ds(first[r], areas)],
                           preferred_element_type=jnp.float32)
            lhs[r] = jnp.where(keep, rows, 0.0).astype(jnp.bfloat16)
        for i in range(QUADS):
            for r in range(2):
                parts = []
                for h in range(2):
                    acc = jnp.dot(lhs[r], slab[i, :, pl.ds(2 * LANES * h, 2 * LANES)],
                                  preferred_element_type=jnp.float32)
                    acc = (acc * (1.0 / (M - 1))).reshape(ROWS // 8, 8, 2 * LANES)
                    both = swap_halves(acc[:, :, :LANES], acc[:, :, LANES:])
                    parts.append(jnp.stack(both, axis=1).reshape(areas, 8, LANES))
                done = jnp.stack(parts, axis=1).reshape(areas, 16, LANES)
                stage[pl.ds(first[r], areas), i] = done.astype(jnp.bfloat16)
            part(q, i).start(priority=i % 2)
        return carry

    lax.fori_loop(0, half, step, 0)

    def finish(q, carry):
        for i in range(QUADS):
            part(q, i).wait()
        return carry

    lax.fori_loop(0, half, finish, 0)


def product(metric, slab):
    any_space = pl.BlockSpec(memory_space=pl.ANY)
    dma = pltpu.SemaphoreType.DMA
    return pl.pallas_call(
        product_kernel,
        out_shape=jax.ShapeDtypeStruct((AREAS, QUADS, 16, LANES), jnp.bfloat16),
        in_specs=[pl.BlockSpec(memory_space=pltpu.VMEM)] * 2,
        out_specs=any_space,
        scratch_shapes=[
            pltpu.VMEM((AREAS, 4 * M), jnp.bfloat16),
            pltpu.VMEM((2, ROWS, 4 * M), jnp.bfloat16),
            pltpu.VMEM((AREAS, QUADS, 16, LANES), jnp.bfloat16),
            dma((32,)),
        ],
        compiler_params=pltpu.CompilerParams(vmem_limit_bytes=32 * 2**20),
        cost_estimate=pl.CostEstimate(
            flops=2 * 2048 * 192 * 4096, bytes_accessed=20 * 2**20, transcendentals=0),
        name="product",
    )(metric, slab)


def body(tiles, farm_area, capacity, offsets, state):
    by_member = jnp.transpose(tiles, (1, 2, 0))
    columns = state.reshape(M, 2, 64, LANES)
    columns = jnp.transpose(columns, (0, 2, 1, 3)).reshape(M, QUADS, 16, LANES)
    metric, slab = exchange(
        by_member, farm_area.reshape(1, F), capacity.reshape(1, F), offsets, columns)
    out = product(metric, slab)
    out = jnp.transpose(out.reshape(AREAS, 64, 2, LANES), (0, 2, 1, 3))
    return out.reshape(AREAS, 2, 64 * LANES)


def solution(mesh):
    in_specs = (P("grid", None, None), P("grid"), P("grid"), P("grid"), P(None, "lev", "grid"))
    out_specs = P(None, "lev", "grid")
    return jax.shard_map(body, mesh=mesh, in_specs=in_specs, out_specs=out_specs, check_vma=False)
```

```python
import jax
import jax.numpy as jnp
from jax import lax
from jax.experimental import pallas as pl
from jax.experimental.pallas import tpu as pltpu
from jax.sharding import PartitionSpec as P

MESH = pl.DeviceIdType.MESH
M = 48
T = 144
F = 256
AREAS = 512
LANES = 128
RING = 4
ONES = 16
PAD_X = ONES + T
ROWS_Z = 80
PAD_Z = 96
HALF = 64
RAMPS = 132
RAMPS_Z = 68
KEEP_X = 152
KEEP_Z = 88
QUADS = 8
ROWS = 256
capacity_floor = 200.0
spread_floor = 0.05


def iota(shape, dim):
    return lax.broadcasted_iota(jnp.int32, shape, dim)


def swap_halves(u, v):
    low = iota(u.shape, 1) < 4
    crossed = pltpu.roll(jnp.where(low, v, u), 4, 1)
    return jnp.where(low, u, crossed), jnp.where(low, crossed, v)


def ramp_metric(power, offset, first, last):
    steps = power.shape[0]
    wide = jnp.broadcast_to(offset, power.shape).astype(jnp.int32)
    later = power
    for bit in (1, 2, 4, 8):
        later = jnp.where((wide & bit) != 0, pltpu.roll(later, steps - bit, 0), later)
    row = iota(power.shape, 0)
    inside = (row >= first) & (row < last)
    return jnp.max(jnp.where(inside, later - power, -3e38), axis=0, keepdims=True)


STEP = (0, 0, 1, 1, 3, 3, 2, 2)
BACK = (0, 1, 4, 5, 2, 3, 6, 7)
ORDER = (6, 7, 2, 4, 3, 5, 1)
NEAR = 6
STARTS, ROWS_X, SKIP = (0, 96), (96, 48), (ONES, 0)


def exchange_kernel(
    tiles, farm_area, capacity, offsets, state, metric_out, slab_out,
    area_in, capacity_in, offsets_in, near_tiles,
    facts_x, facts_z, got_a, got_b, got_z, weight_x, weight_z,
    part_x, part_z, sum_x, sum_z, near_x, off_x, off_z,
    metrics, st,
    local_sem, fx_send, fx_recv, fz_send, fz_recv, x_send, x_recv, z_send, z_recv,
    bx_send, bx_recv, bz_send, bz_recv,
    all_send, all_recv,
):
    g = lax.axis_index("grid")
    y = lax.axis_index("lev")
    z = lax.div(g, 8)
    x = lax.rem(lax.div(g, 2), 4)
    c = lax.rem(g, 2)
    mine_x = 2 * x + c
    mine_z = 2 * z + c
    xs = [x] + [lax.rem(x + d, 4) for d in range(1, 4)]
    zs = [z] + [lax.rem(z + d, 4) for d in range(1, 4)]
    ys = [y] + [lax.rem(y + d, 4) for d in range(1, 4)]
    cs = [c, 1 - c]

    def device(xx, zz, cc, yy):
        return (zz * 8 + xx * 2 + cc, yy)

    sibling = device(x, z, 1 - c, y)
    x_peers = [(xs[STEP[i]], cs[i % 2]) for i in range(8)]
    z_peers = [(zs[STEP[i]], cs[i % 2]) for i in range(8)]

    def remote(src, dst, send_sem, recv_sem, to):
        return pltpu.make_async_remote_copy(
            src_ref=src, dst_ref=dst, send_sem=send_sem, recv_sem=recv_sem,
            device_id=to, device_id_type=MESH)

    def wait_for(slot, send, recv):
        remote(slot, slot, send, recv, sibling).wait_recv()

    def loop(first, last):
        def run(body):
            lax.fori_loop(first, last, lambda i, carry: (body(i), carry)[1], 0)
        return run

    got_x = (got_a, got_b)
    barrier = pltpu.get_barrier_semaphore()

    def greet(to):
        pl.semaphore_signal(barrier, inc=1, device_id=to, device_id_type=MESH)

    for i in ORDER:
        xx, cc = x_peers[i]
        greet(device(xx, z, cc, y))
        if i != 1:
            zz, cc = z_peers[i]
            greet(device(x, zz, cc, y))
    for d in (2, 1, 3):
        greet(device(x, z, c, ys[d]))

    def x_slot(i, half):
        return got_x[half].at[i, pl.ds(SKIP[half], ROWS_X[half])]

    def z_slot(i):
        return got_z.at[i, pl.ds(0, ROWS_Z)]

    def x_tile(xx, cc):
        return near_tiles.at[2 * xx + cc]

    def z_tile(zz, cc):
        return near_tiles.at[8 + zz, pl.ds(pl.multiple_of(HALF * cc, HALF), ROWS_Z)]

    local = [
        pltpu.make_async_copy(farm_area, area_in, local_sem.at[0]),
        pltpu.make_async_copy(capacity, capacity_in, local_sem.at[1]),
        pltpu.make_async_copy(offsets, offsets_in, local_sem.at[2]),
        pltpu.make_async_copy(tiles.at[pl.ds(12 * y, 12)], near_tiles, local_sem.at[6]),
        pltpu.make_async_copy(
            tiles.at[12 * y + 8 + z, pl.ds(pl.multiple_of(HALF * c, HALF), ROWS_Z)],
            z_slot(0), local_sem.at[3]),
        pltpu.make_async_copy(
            tiles.at[12 * y + mine_x, pl.ds(STARTS[0], ROWS_X[0])], x_slot(0, 0),
            local_sem.at[4]),
        pltpu.make_async_copy(
            tiles.at[12 * y + mine_x, pl.ds(STARTS[1], ROWS_X[1])], x_slot(0, 1),
            local_sem.at[7]),
        pltpu.make_async_copy(state, st, local_sem.at[5]),
    ]
    for copy in local:
        copy.start()
    def fx_copy(i):
        xx, cc = x_peers[i]
        return remote(facts_x.at[0], facts_x.at[BACK[i]], fx_send.at[i], fx_recv.at[BACK[i]],
                      device(xx, z, cc, y))

    def fz_copy(i):
        zz, cc = z_peers[i]
        return remote(facts_z.at[0], facts_z.at[BACK[i]], fz_send.at[i], fz_recv.at[BACK[i]],
                      device(x, zz, cc, y))

    def x_copy(i, half):
        xx, cc = x_peers[i]
        return remote(x_tile(xx, cc).at[pl.ds(STARTS[half], ROWS_X[half])], x_slot(BACK[i], half),
                      x_send.at[half, i], x_recv.at[half, BACK[i]], device(xx, z, cc, y))

    def z_copy(i):
        zz, cc = z_peers[i]
        return remote(z_tile(zz, cc), z_slot(BACK[i]), z_send.at[i], z_recv.at[BACK[i]],
                      device(x, zz, cc, y))

    sends = []

    def start(*copies):
        for copy in copies:
            copy.start()
            sends.append(copy)

    for copy in local[:3]:
        copy.wait()

    lane = iota((1, F), 1)
    offset = jnp.zeros((1, F), jnp.int32)
    for k in range(16):
        offset = jnp.where((lane & 15) == k, offsets_in[k], offset)
    area = area_in[...]
    turned = ((area >> 5) & 3) * 128 + (area >> 7) * 32 + (area & 31)
    for facts, ids, spot in ((facts_z, turned, mine_z), (facts_x, area, mine_x)):
        placed = jnp.where((lane >> 4) == spot, offset, 0)
        rows = jnp.concatenate(
            [ids, capacity_in[...], placed, jnp.zeros((1, F), jnp.int32)], axis=0)
        facts[0] = rows.astype(jnp.float32)

    pl.semaphore_wait(barrier, 16)
    for i in ORDER:
        start(fx_copy(i), fz_copy(i))
    local[3].wait()
    for i in ORDER:
        start(x_copy(i, 0), z_copy(i))
    for i in ORDER[2:] + ORDER[:2]:
        start(x_copy(i, 1))

    got_a[:, pl.ds(0, ONES)] = jnp.ones((8, ONES, F), jnp.bfloat16)
    got_z[:, pl.ds(ROWS_Z, ONES)] = jnp.ones((8, ONES, F), jnp.bfloat16)
    off_x[...] = jnp.zeros_like(off_x)
    off_z[...] = jnp.zeros_like(off_z)
    area_ids = iota((AREAS, F), 0).astype(jnp.float32)

    def weigh(i, facts, weight, off):
        rows = facts[i]
        off[...] = off[...] + rows[2:3, :LANES]
        placed = jnp.where(area_ids == rows[0:1], rows[1:2], 0.0)
        weight[:, pl.ds(pl.multiple_of(F * i, F), F)] = placed.astype(jnp.bfloat16)

    @loop(0, 8)
    def _(i):
        for facts, recv, send, weight, off in (
                (facts_z, fz_recv, fz_send, weight_z, off_z),
                (facts_x, fx_recv, fx_send, weight_x, off_x)):
            @pl.when(i > 0)
            def _():
                wait_for(facts.at[i], send.at[i], recv.at[i])

            weigh(i, facts, weight, off)

    def sum_up(values, weights):
        return lax.dot_general(values, weights, (((1,), (1,)), ((), ())),
                               preferred_element_type=jnp.float32)

    bz = []

    near, far, all_slots = range(NEAR), range(NEAR, 8), range(8)

    def block_pair(p):
        return lax.rem(z + 2 + p, 4), lax.rem(z + 1 + 3 * p, 4)

    def side_by_side(got, slots):
        return jnp.concatenate([got[i] for i in slots], axis=1)

    def dot_x(half, p, slots):
        columns = pl.ds(F * slots[0], F * len(slots))
        chosen = jnp.concatenate(
            [weight_x[pl.ds(pl.multiple_of(LANES * zz, LANES), LANES), columns]
             for zz in block_pair(p)], axis=0)
        return sum_up(side_by_side(got_x[half], slots), chosen)

    def sum_copy(half, rows, d, zz):
        return remote(part_x.at[zz, rows], sum_x.at[3 - d, rows], bx_send.at[half, d - 1],
                      bx_recv.at[half, 3 - d], device(x, zz, c, y))

    def leave(half, rows, p, value):
        for k, zz in enumerate(block_pair(p)):
            part_x[zz, rows] = value[:, k * LANES : (k + 1) * LANES]
        sum_copy(half, rows, 2 + p, block_pair(p)[0]).start()

        @pl.when(p == 0)
        def _():
            sum_copy(half, rows, 1, zs[1]).start()

    early_rows, late_rows = pl.ds(0, 8 + ROWS_X[0]), pl.ds(8 + ROWS_X[0], ROWS_X[1])
    local[5].wait()
    for i in range(1, 8):
        wait_for(x_slot(i, 0), x_send.at[0, i], x_recv.at[0, i])

    @loop(0, 2)
    def _(p):
        leave(0, early_rows, p, dot_x(0, p, all_slots)[8:])

    local[4].wait()
    for i in range(1, 8):
        wait_for(z_slot(i), z_send.at[i], z_recv.at[i])
    for h in range(2):
        value = sum_up(side_by_side(got_z, all_slots), weight_z[pl.ds(2 * LANES * h, 2 * LANES)])
        for b in range(2):
            part_z[2 * h + b] = value[:KEEP_Z, b * LANES : (b + 1) * LANES]
    for d in (2, 1, 3):
        copy = remote(part_z.at[xs[d]], sum_z.at[3 - d], bz_send.at[d - 1], bz_recv.at[3 - d],
                      device(xs[d], z, c, y))
        copy.start()
        bz.append(copy)

    local[6].wait()
    for i in range(1, NEAR):
        wait_for(x_slot(i, 1), x_send.at[1, i], x_recv.at[1, i])

    @loop(0, 2)
    def _(p):
        near_x[p] = dot_x(1, p, near)

    for i in range(NEAR, 8):
        wait_for(x_slot(i, 1), x_send.at[1, i], x_recv.at[1, i])

    @loop(0, 2)
    def _(p):
        leave(1, late_rows, p, near_x[p] + dot_x(1, p, far))

    bx = [[sum_copy(half, rows, d, zs[d]) for d in range(1, 4)]
          for half, rows in ((0, early_rows), (1, late_rows))]

    def whole(copies, own, others, rows):
        for copy in copies:
            copy.wait_recv()
        total = own[rows]
        for k in range(3):
            total = total + others[k, rows]
        return total

    spot = (4 * y + z) * 8 + mine_x

    first = whole(bx[0], part_x.at[z], sum_x, early_rows)
    total = jnp.maximum(first[:1], capacity_floor)
    power = first[8:] / total
    early = ramp_metric(power, off_x[...], 0, 84)
    last = whole(bz, part_z.at[x], sum_z, pl.ds(0, KEEP_Z))
    metrics[spot, pl.ds(1, 1)] = ramp_metric(
        last[:ROWS_Z] / jnp.maximum(last[ROWS_Z : ROWS_Z + 1], capacity_floor),
        off_z[...], 0, RAMPS_Z)
    last = whole(bx[1], part_x.at[z], sum_x, late_rows)
    power = jnp.concatenate([power[80:], last / total], axis=0)
    late = ramp_metric(power, off_x[...], 4, 52)
    metrics[spot, pl.ds(0, 1)] = jnp.maximum(early, late)

    mine = metrics.at[spot]

    def broadcast(xx, zz, cc, yy):
        remote(mine, mine, all_send, all_recv, device(xx, zz, cc, yy)).start()

    @loop(0, 15)
    def _(k):
        step = 1 + lax.rem(k + 9, 15)
        yy, zz = lax.rem(y + lax.div(step, 4), 4), lax.rem(z + lax.rem(step, 4), 4)
        for i in (6, 7, 2, 3, 4, 5, 0, 1):
            xx, cc = x_peers[i]
            broadcast(xx, zz, cc, yy)

    for i in ORDER:
        xx, cc = x_peers[i]
        broadcast(xx, z, cc, y)

    local[7].wait()

    @loop(0, QUADS)
    def _(i):
        values = st[:, i].astype(jnp.float32).reshape(M, 2, 8, LANES)
        values = values - (jnp.sum(values, axis=0) / M)[None]
        pairs = values.reshape(M // 2, 2, 2, 8, LANES)
        for h in range(2):
            both = swap_halves(pairs[:, 0, h], pairs[:, 1, h])
            for k in range(2):
                slab_out[i, :, pl.ds((2 * h + k) * LANES, LANES)] = (
                    both[k].reshape(4 * M, LANES).astype(jnp.bfloat16))

    for copy in sends + bx[0] + bx[1] + bz:
        copy.wait_send()

    others = metrics.at[pl.ds(0, 127)]
    everything = remote(others, others, all_send, all_recv, sibling)
    everything.wait_recv()

    rows = metrics.reshape(256, LANES)
    for yy in range(4):
        for zz in range(4):
            metric_out[pl.ds(8 * yy, 8), pl.ds(LANES * zz, LANES)] = (
                rows[pl.ds(16 * (4 * yy + zz), 8, stride=2)])
    quarter = iota((16, LANES), 1) >> 5
    blocks = [jnp.maximum(rows[pl.ds(4 * b + 1, 16, stride=16)], rows[pl.ds(4 * b + 3, 16, stride=16)])
              for b in range(RING)]
    for zz in range(4):
        value = jnp.zeros((16, LANES), jnp.float32)
        for b in range(RING):
            move = (32 * (b - zz)) % LANES
            moved = pltpu.roll(blocks[b], move, 1) if move else blocks[b]
            value = jnp.where(quarter == b, moved, value)
        metric_out[pl.ds(32, 16), pl.ds(zz * LANES, LANES)] = value

    everything.wait_send()


def exchange(tiles, farm_area, capacity, offsets, state):
    any_space = pl.BlockSpec(memory_space=pl.ANY)
    vmem = pl.BlockSpec(memory_space=pltpu.VMEM)
    dma = pltpu.SemaphoreType.DMA
    f32, bf16 = jnp.float32, jnp.bfloat16
    return pl.pallas_call(
        exchange_kernel,
        out_shape=(
            pltpu.VMEM((M, AREAS), f32),
            pltpu.VMEM((QUADS, 4 * M, 4 * LANES), bf16),
        ),
        in_specs=[any_space] * 5,
        out_specs=(vmem, vmem),
        scratch_shapes=[
            pltpu.VMEM((1, F), jnp.int32),
            pltpu.VMEM((1, F), jnp.int32),
            pltpu.SMEM((16,), jnp.int32),
            pltpu.VMEM((12, T, F), bf16),
            pltpu.VMEM((8, 4, F), f32),
            pltpu.VMEM((8, 4, F), f32),
            pltpu.VMEM((8, ONES + ROWS_X[0], F), bf16),
            pltpu.VMEM((8, ROWS_X[1], F), bf16),
            pltpu.VMEM((8, ROWS_Z + ONES, F), bf16),
            pltpu.VMEM((AREAS, 8 * F), bf16),
            pltpu.VMEM((AREAS, 8 * F), bf16),
            pltpu.VMEM((RING, KEEP_X, LANES), f32),
            pltpu.VMEM((RING, KEEP_Z, LANES), f32),
            pltpu.VMEM((3, KEEP_X, LANES), f32),
            pltpu.VMEM((3, KEEP_Z, LANES), f32),
            pltpu.VMEM((2, ROWS_X[1], 2 * LANES), f32),
            pltpu.VMEM((1, LANES), f32),
            pltpu.VMEM((1, LANES), f32),
            pltpu.VMEM((128, 2, LANES), f32),
            pltpu.VMEM((M, QUADS, 16, LANES), bf16),
            dma((8,)), dma((8,)), dma((8,)), dma((8,)), dma((8,)),
            dma((2, 8)), dma((2, 8)), dma((8,)), dma((8,)),
            dma((2, 3)), dma((2, 3)), dma((3,)), dma((3,)),
            dma, dma,
        ],
        compiler_params=pltpu.CompilerParams(
            collective_id=0, has_side_effects=True, vmem_limit_bytes=60 * 2**20),
        cost_estimate=pl.CostEstimate(
            flops=2 * 256 * 2048 * 512, bytes_accessed=5 * 2**20, transcendentals=0),
        name="exchange",
    )(tiles, farm_area, capacity, offsets, state)


def product_kernel(metric, slab, out, wide, lhs, stage, out_sem):
    values = metric[...]
    anomaly = values - jnp.mean(values, axis=0, keepdims=True)
    spread = jnp.sqrt(jnp.sum(anomaly * anomaly, axis=0, keepdims=True) / (M - 1))
    scores = anomaly / jnp.maximum(spread, spread_floor)
    scores = jnp.transpose(scores).astype(jnp.bfloat16)

    held = iota((M, 4 * M), 0)
    rest = held - 32
    member = jnp.where(
        held < 32,
        12 * (held >> 3) + (held & 7),
        12 * (rest >> 2) + 8 + (rest & 3))
    widen = ((iota((M, 4 * M), 1) >> 2) == member).astype(jnp.bfloat16)
    wide[...] = jnp.dot(scores, widen, preferred_element_type=jnp.float32).astype(jnp.bfloat16)
    repeat = ((iota((ROWS, ROWS // 4), 0) >> 2) == iota((ROWS, ROWS // 4), 1)).astype(
        jnp.bfloat16)
    keep = (iota((ROWS, 4 * M), 0) & 3) == (iota((ROWS, 4 * M), 1) & 3)
    areas = ROWS // 4

    half = 4 * AREAS // ROWS // 2

    def part(q, i):
        some = pl.ds(pl.multiple_of(2 * areas * q, 2 * areas), 2 * areas)
        return pltpu.make_async_copy(stage.at[some, i], out.at[some, i], out_sem.at[QUADS * q + i])

    def step(q, carry):
        first = [pl.multiple_of((2 * q + r) * areas, areas) for r in range(2)]
        for r in range(2):
            rows = jnp.dot(repeat, wide[pl.ds(first[r], areas)],
                           preferred_element_type=jnp.float32)
            lhs[r] = jnp.where(keep, rows, 0.0).astype(jnp.bfloat16)
        for i in range(QUADS):
            for r in range(2):
                parts = []
                for h in range(2):
                    acc = jnp.dot(lhs[r], slab[i, :, pl.ds(2 * LANES * h, 2 * LANES)],
                                  preferred_element_type=jnp.float32)
                    acc = (acc * (1.0 / (M - 1))).reshape(ROWS // 8, 8, 2 * LANES)
                    both = swap_halves(acc[:, :, :LANES], acc[:, :, LANES:])
                    parts.append(jnp.stack(both, axis=1).reshape(areas, 8, LANES))
                done = jnp.stack(parts, axis=1).reshape(areas, 16, LANES)
                stage[pl.ds(first[r], areas), i] = done.astype(jnp.bfloat16)
            part(q, i).start(priority=i % 2)
        return carry

    lax.fori_loop(0, half, step, 0)

    def finish(q, carry):
        for i in range(QUADS):
            part(q, i).wait()
        return carry

    lax.fori_loop(0, half, finish, 0)


def product(metric, slab):
    any_space = pl.BlockSpec(memory_space=pl.ANY)
    dma = pltpu.SemaphoreType.DMA
    return pl.pallas_call(
        product_kernel,
        out_shape=jax.ShapeDtypeStruct((AREAS, QUADS, 16, LANES), jnp.bfloat16),
        in_specs=[pl.BlockSpec(memory_space=pltpu.VMEM)] * 2,
        out_specs=any_space,
        scratch_shapes=[
            pltpu.VMEM((AREAS, 4 * M), jnp.bfloat16),
            pltpu.VMEM((2, ROWS, 4 * M), jnp.bfloat16),
            pltpu.VMEM((AREAS, QUADS, 16, LANES), jnp.bfloat16),
            dma((32,)),
        ],
        compiler_params=pltpu.CompilerParams(vmem_limit_bytes=32 * 2**20),
        cost_estimate=pl.CostEstimate(
            flops=2 * 2048 * 192 * 4096, bytes_accessed=20 * 2**20, transcendentals=0),
        name="product",
    )(metric, slab)


def body(tiles, farm_area, capacity, offsets, state):
    by_member = jnp.transpose(tiles, (1, 2, 0))
    columns = state.reshape(M, 2, 64, LANES)
    columns = jnp.transpose(columns, (0, 2, 1, 3)).reshape(M, QUADS, 16, LANES)
    metric, slab = exchange(
        by_member, farm_area.reshape(1, F), capacity.reshape(1, F), offsets, columns)
    out = product(metric, slab)
    out = jnp.transpose(out.reshape(AREAS, 64, 2, LANES), (0, 2, 1, 3))
    return out.reshape(AREAS, 2, 64 * LANES)


def solution(mesh):
    in_specs = (P("grid", None, None), P("grid"), P("grid"), P("grid"), P(None, "lev", "grid"))
    out_specs = P(None, "lev", "grid")
    return jax.shard_map(body, mesh=mesh, in_specs=in_specs, out_specs=out_specs, check_vma=False)
```

```python
import jax
import jax.numpy as jnp
from jax import lax
from jax.experimental import pallas as pl
from jax.experimental.pallas import tpu as pltpu
from jax.sharding import PartitionSpec as P

MESH = pl.DeviceIdType.MESH
M = 48
T = 144
F = 256
AREAS = 512
LANES = 128
RING = 4
ONES = 16
PAD_X = ONES + T
ROWS_Z = 80
PAD_Z = 96
HALF = 64
RAMPS = 132
RAMPS_Z = 68
KEEP_X = 152
KEEP_Z = 88
QUADS = 8
ROWS = 256
capacity_floor = 200.0
spread_floor = 0.05


def iota(shape, dim):
    return lax.broadcasted_iota(jnp.int32, shape, dim)


def swap_halves(u, v):
    low = iota(u.shape, 1) < 4
    crossed = pltpu.roll(jnp.where(low, v, u), 4, 1)
    return jnp.where(low, u, crossed), jnp.where(low, crossed, v)


def ramp_metric(power, offset, first, last):
    steps = power.shape[0]
    wide = jnp.broadcast_to(offset, power.shape).astype(jnp.int32)
    later = power
    for bit in (1, 2, 4, 8):
        later = jnp.where((wide & bit) != 0, pltpu.roll(later, steps - bit, 0), later)
    row = iota(power.shape, 0)
    inside = (row >= first) & (row < last)
    return jnp.max(jnp.where(inside, later - power, -3e38), axis=0, keepdims=True)


STEP = (0, 0, 1, 1, 3, 3, 2, 2)
BACK = (0, 1, 4, 5, 2, 3, 6, 7)
ORDER = (6, 7, 2, 4, 3, 5, 1)
NEAR = 6
STARTS, ROWS_X, SKIP = (0, 96), (96, 48), (ONES, 0)


def exchange_kernel(
    tiles, farm_area, capacity, offsets, state, metric_out, slab_out,
    area_in, capacity_in, offsets_in, near_tiles,
    facts_x, facts_z, got_a, got_b, got_z, weight_x, weight_z,
    part_x, part_z, sum_x, sum_z, near_x, off_x, off_z,
    metrics, st,
    local_sem, fx_send, fx_recv, fz_send, fz_recv, x_send, x_recv, z_send, z_recv,
    bx_send, bx_recv, bz_send, bz_recv,
    all_send, all_recv,
):
    g = lax.axis_index("grid")
    y = lax.axis_index("lev")
    z = lax.div(g, 8)
    x = lax.rem(lax.div(g, 2), 4)
    c = lax.rem(g, 2)
    mine_x = 2 * x + c
    mine_z = 2 * z + c
    xs = [x] + [lax.rem(x + d, 4) for d in range(1, 4)]
    zs = [z] + [lax.rem(z + d, 4) for d in range(1, 4)]
    ys = [y] + [lax.rem(y + d, 4) for d in range(1, 4)]
    cs = [c, 1 - c]

    def device(xx, zz, cc, yy):
        return (zz * 8 + xx * 2 + cc, yy)

    sibling = device(x, z, 1 - c, y)
    x_peers = [(xs[STEP[i]], cs[i % 2]) for i in range(8)]
    z_peers = [(zs[STEP[i]], cs[i % 2]) for i in range(8)]

    def remote(src, dst, send_sem, recv_sem, to):
        return pltpu.make_async_remote_copy(
            src_ref=src, dst_ref=dst, send_sem=send_sem, recv_sem=recv_sem,
            device_id=to, device_id_type=MESH)

    def wait_for(slot, send, recv):
        remote(slot, slot, send, recv, sibling).wait_recv()

    def loop(first, last):
        def run(body):
            lax.fori_loop(first, last, lambda i, carry: (body(i), carry)[1], 0)
        return run

    got_x = (got_a, got_b)
    barrier = pltpu.get_barrier_semaphore()

    def greet(to):
        pl.semaphore_signal(barrier, inc=1, device_id=to, device_id_type=MESH)

    for i in ORDER:
        xx, cc = x_peers[i]
        greet(device(xx, z, cc, y))
        if i != 1:
            zz, cc = z_peers[i]
            greet(device(x, zz, cc, y))
    for d in (2, 1, 3):
        greet(device(x, z, c, ys[d]))

    def x_slot(i, half):
        return got_x[half].at[i, pl.ds(SKIP[half], ROWS_X[half])]

    def z_slot(i):
        return got_z.at[i, pl.ds(0, ROWS_Z)]

    def x_tile(xx, cc):
        return near_tiles.at[2 * xx + cc]

    def z_tile(zz, cc):
        return near_tiles.at[8 + zz, pl.ds(pl.multiple_of(HALF * cc, HALF), ROWS_Z)]

    local = [
        pltpu.make_async_copy(farm_area, area_in, local_sem.at[0]),
        pltpu.make_async_copy(capacity, capacity_in, local_sem.at[1]),
        pltpu.make_async_copy(offsets, offsets_in, local_sem.at[2]),
        pltpu.make_async_copy(tiles.at[pl.ds(12 * y, 12)], near_tiles, local_sem.at[6]),
        pltpu.make_async_copy(
            tiles.at[12 * y + 8 + z, pl.ds(pl.multiple_of(HALF * c, HALF), ROWS_Z)],
            z_slot(0), local_sem.at[3]),
        pltpu.make_async_copy(
            tiles.at[12 * y + mine_x, pl.ds(STARTS[0], ROWS_X[0])], x_slot(0, 0),
            local_sem.at[4]),
        pltpu.make_async_copy(
            tiles.at[12 * y + mine_x, pl.ds(STARTS[1], ROWS_X[1])], x_slot(0, 1),
            local_sem.at[7]),
        pltpu.make_async_copy(state, st, local_sem.at[5]),
    ]
    for copy in local:
        copy.start()
    def fx_copy(i):
        xx, cc = x_peers[i]
        return remote(facts_x.at[0], facts_x.at[BACK[i]], fx_send.at[i], fx_recv.at[BACK[i]],
                      device(xx, z, cc, y))

    def fz_copy(i):
        zz, cc = z_peers[i]
        return remote(facts_z.at[0], facts_z.at[BACK[i]], fz_send.at[i], fz_recv.at[BACK[i]],
                      device(x, zz, cc, y))

    def x_copy(i, half):
        xx, cc = x_peers[i]
        return remote(x_tile(xx, cc).at[pl.ds(STARTS[half], ROWS_X[half])], x_slot(BACK[i], half),
                      x_send.at[half, i], x_recv.at[half, BACK[i]], device(xx, z, cc, y))

    def z_copy(i):
        zz, cc = z_peers[i]
        return remote(z_tile(zz, cc), z_slot(BACK[i]), z_send.at[i], z_recv.at[BACK[i]],
                      device(x, zz, cc, y))

    sends = []

    def start(*copies):
        for copy in copies:
            copy.start()
            sends.append(copy)

    for copy in local[:3]:
        copy.wait()

    lane = iota((1, F), 1)
    offset = jnp.zeros((1, F), jnp.int32)
    for k in range(16):
        offset = jnp.where((lane & 15) == k, offsets_in[k], offset)
    area = area_in[...]
    turned = ((area >> 5) & 3) * 128 + (area >> 7) * 32 + (area & 31)
    for facts, ids, spot in ((facts_z, turned, mine_z), (facts_x, area, mine_x)):
        placed = jnp.where((lane >> 4) == spot, offset, 0)
        rows = jnp.concatenate(
            [ids, capacity_in[...], placed, jnp.zeros((1, F), jnp.int32)], axis=0)
        facts[0] = rows.astype(jnp.float32)

    pl.semaphore_wait(barrier, 16)
    for i in ORDER:
        start(fx_copy(i), fz_copy(i))
    local[3].wait()
    for i in ORDER:
        start(x_copy(i, 0), z_copy(i))
    for i in ORDER[2:] + ORDER[:2]:
        start(x_copy(i, 1))

    got_a[:, pl.ds(0, ONES)] = jnp.ones((8, ONES, F), jnp.bfloat16)
    got_z[:, pl.ds(ROWS_Z, ONES)] = jnp.ones((8, ONES, F), jnp.bfloat16)
    off_x[...] = jnp.zeros_like(off_x)
    off_z[...] = jnp.zeros_like(off_z)
    area_ids = iota((AREAS, F), 0).astype(jnp.float32)

    def weigh(i, facts, weight, off):
        rows = facts[i]
        off[...] = off[...] + rows[2:3, :LANES]
        placed = jnp.where(area_ids == rows[0:1], rows[1:2], 0.0)
        weight[:, pl.ds(pl.multiple_of(F * i, F), F)] = placed.astype(jnp.bfloat16)

    @loop(0, 8)
    def _(i):
        for facts, recv, send, weight, off in (
                (facts_z, fz_recv, fz_send, weight_z, off_z),
                (facts_x, fx_recv, fx_send, weight_x, off_x)):
            @pl.when(i > 0)
            def _():
                wait_for(facts.at[i], send.at[i], recv.at[i])

            weigh(i, facts, weight, off)

    def sum_up(values, weights):
        return lax.dot_general(values, weights, (((1,), (1,)), ((), ())),
                               preferred_element_type=jnp.float32)

    bz = []

    near, far, all_slots = range(NEAR), range(NEAR, 8), range(8)

    def block_pair(p):
        return lax.rem(z + 2 + p, 4), lax.rem(z + 1 + 3 * p, 4)

    def side_by_side(got, slots):
        return jnp.concatenate([got[i] for i in slots], axis=1)

    def dot_x(half, p, slots):
        columns = pl.ds(F * slots[0], F * len(slots))
        chosen = jnp.concatenate(
            [weight_x[pl.ds(pl.multiple_of(LANES * zz, LANES), LANES), columns]
             for zz in block_pair(p)], axis=0)
        return sum_up(side_by_side(got_x[half], slots), chosen)

    def sum_copy(half, rows, d, zz):
        return remote(part_x.at[zz, rows], sum_x.at[3 - d, rows], bx_send.at[half, d - 1],
                      bx_recv.at[half, 3 - d], device(x, zz, c, y))

    def leave(half, rows, p, value):
        for k, zz in enumerate(block_pair(p)):
            part_x[zz, rows] = value[:, k * LANES : (k + 1) * LANES]
        sum_copy(half, rows, 2 + p, block_pair(p)[0]).start()

        @pl.when(p == 0)
        def _():
            sum_copy(half, rows, 1, zs[1]).start()

    early_rows, late_rows = pl.ds(0, 8 + ROWS_X[0]), pl.ds(8 + ROWS_X[0], ROWS_X[1])
    local[5].wait()
    for i in range(1, 8):
        wait_for(x_slot(i, 0), x_send.at[0, i], x_recv.at[0, i])

    @loop(0, 2)
    def _(p):
        leave(0, early_rows, p, dot_x(0, p, all_slots)[8:])

    local[4].wait()
    for i in range(1, 8):
        wait_for(z_slot(i), z_send.at[i], z_recv.at[i])
    for h in range(2):
        value = sum_up(side_by_side(got_z, all_slots), weight_z[pl.ds(2 * LANES * h, 2 * LANES)])
        for b in range(2):
            part_z[2 * h + b] = value[:KEEP_Z, b * LANES : (b + 1) * LANES]
    for d in (2, 1, 3):
        copy = remote(part_z.at[xs[d]], sum_z.at[3 - d], bz_send.at[d - 1], bz_recv.at[3 - d],
                      device(xs[d], z, c, y))
        copy.start()
        bz.append(copy)

    local[6].wait()
    for i in range(1, NEAR):
        wait_for(x_slot(i, 1), x_send.at[1, i], x_recv.at[1, i])

    @loop(0, 2)
    def _(p):
        near_x[p] = dot_x(1, p, near)

    for i in range(NEAR, 8):
        wait_for(x_slot(i, 1), x_send.at[1, i], x_recv.at[1, i])

    @loop(0, 2)
    def _(p):
        leave(1, late_rows, p, near_x[p] + dot_x(1, p, far))

    bx = [[sum_copy(half, rows, d, zs[d]) for d in range(1, 4)]
          for half, rows in ((0, early_rows), (1, late_rows))]

    def whole(copies, own, others, rows):
        for copy in copies:
            copy.wait_recv()
        total = own[rows]
        for k in range(3):
            total = total + others[k, rows]
        return total

    spot = (4 * y + z) * 8 + mine_x

    first = whole(bx[0], part_x.at[z], sum_x, early_rows)
    total = jnp.maximum(first[:1], capacity_floor)
    power = first[8:] / total
    early = ramp_metric(power, off_x[...], 0, 84)
    last = whole(bz, part_z.at[x], sum_z, pl.ds(0, KEEP_Z))
    metrics[spot, pl.ds(1, 1)] = ramp_metric(
        last[:ROWS_Z] / jnp.maximum(last[ROWS_Z : ROWS_Z + 1], capacity_floor),
        off_z[...], 0, RAMPS_Z)
    last = whole(bx[1], part_x.at[z], sum_x, late_rows)
    power = jnp.concatenate([power[80:], last / total], axis=0)
    late = ramp_metric(power, off_x[...], 4, 52)
    metrics[spot, pl.ds(0, 1)] = jnp.maximum(early, late)

    mine = metrics.at[spot]

    def hops(where):
        dy, dz, i = where
        return sum(min(d, 4 - d) for d in (dy, dz, STEP[i]))

    others = [(dy, dz, i) for dy in range(4) for dz in range(4) for i in range(8)][1:]
    for dy, dz, i in sorted(others, key=hops, reverse=True):
        xx, cc = x_peers[i]
        remote(mine, mine, all_send, all_recv, device(xx, zs[dz], cc, ys[dy])).start()

    local[7].wait()

    @loop(0, QUADS)
    def _(i):
        values = st[:, i].astype(jnp.float32).reshape(M, 2, 8, LANES)
        values = values - (jnp.sum(values, axis=0) / M)[None]
        pairs = values.reshape(M // 2, 2, 2, 8, LANES)
        for h in range(2):
            both = swap_halves(pairs[:, 0, h], pairs[:, 1, h])
            for k in range(2):
                slab_out[i, :, pl.ds((2 * h + k) * LANES, LANES)] = (
                    both[k].reshape(4 * M, LANES).astype(jnp.bfloat16))

    for copy in sends + bx[0] + bx[1] + bz:
        copy.wait_send()

    others = metrics.at[pl.ds(0, 127)]
    everything = remote(others, others, all_send, all_recv, sibling)
    everything.wait_recv()

    rows = metrics.reshape(256, LANES)
    for yy in range(4):
        for zz in range(4):
            metric_out[pl.ds(8 * yy, 8), pl.ds(LANES * zz, LANES)] = (
                rows[pl.ds(16 * (4 * yy + zz), 8, stride=2)])
    quarter = iota((16, LANES), 1) >> 5
    blocks = [jnp.maximum(rows[pl.ds(4 * b + 1, 16, stride=16)], rows[pl.ds(4 * b + 3, 16, stride=16)])
              for b in range(RING)]
    for zz in range(4):
        value = jnp.zeros((16, LANES), jnp.float32)
        for b in range(RING):
            move = (32 * (b - zz)) % LANES
            moved = pltpu.roll(blocks[b], move, 1) if move else blocks[b]
            value = jnp.where(quarter == b, moved, value)
        metric_out[pl.ds(32, 16), pl.ds(zz * LANES, LANES)] = value

    everything.wait_send()


def exchange(tiles, farm_area, capacity, offsets, state):
    any_space = pl.BlockSpec(memory_space=pl.ANY)
    vmem = pl.BlockSpec(memory_space=pltpu.VMEM)
    dma = pltpu.SemaphoreType.DMA
    f32, bf16 = jnp.float32, jnp.bfloat16
    return pl.pallas_call(
        exchange_kernel,
        out_shape=(
            pltpu.VMEM((M, AREAS), f32),
            pltpu.VMEM((QUADS, 4 * M, 4 * LANES), bf16),
        ),
        in_specs=[any_space] * 5,
        out_specs=(vmem, vmem),
        scratch_shapes=[
            pltpu.VMEM((1, F), jnp.int32),
            pltpu.VMEM((1, F), jnp.int32),
            pltpu.SMEM((16,), jnp.int32),
            pltpu.VMEM((12, T, F), bf16),
            pltpu.VMEM((8, 4, F), f32),
            pltpu.VMEM((8, 4, F), f32),
            pltpu.VMEM((8, ONES + ROWS_X[0], F), bf16),
            pltpu.VMEM((8, ROWS_X[1], F), bf16),
            pltpu.VMEM((8, ROWS_Z + ONES, F), bf16),
            pltpu.VMEM((AREAS, 8 * F), bf16),
            pltpu.VMEM((AREAS, 8 * F), bf16),
            pltpu.VMEM((RING, KEEP_X, LANES), f32),
            pltpu.VMEM((RING, KEEP_Z, LANES), f32),
            pltpu.VMEM((3, KEEP_X, LANES), f32),
            pltpu.VMEM((3, KEEP_Z, LANES), f32),
            pltpu.VMEM((2, ROWS_X[1], 2 * LANES), f32),
            pltpu.VMEM((1, LANES), f32),
            pltpu.VMEM((1, LANES), f32),
            pltpu.VMEM((128, 2, LANES), f32),
            pltpu.VMEM((M, QUADS, 16, LANES), bf16),
            dma((8,)), dma((8,)), dma((8,)), dma((8,)), dma((8,)),
            dma((2, 8)), dma((2, 8)), dma((8,)), dma((8,)),
            dma((2, 3)), dma((2, 3)), dma((3,)), dma((3,)),
            dma, dma,
        ],
        compiler_params=pltpu.CompilerParams(
            collective_id=0, has_side_effects=True, vmem_limit_bytes=60 * 2**20),
        cost_estimate=pl.CostEstimate(
            flops=2 * 256 * 2048 * 512, bytes_accessed=5 * 2**20, transcendentals=0),
        name="exchange",
    )(tiles, farm_area, capacity, offsets, state)


def product_kernel(metric, slab, out, wide, lhs, stage, out_sem):
    values = metric[...]
    anomaly = values - jnp.mean(values, axis=0, keepdims=True)
    spread = jnp.sqrt(jnp.sum(anomaly * anomaly, axis=0, keepdims=True) / (M - 1))
    scores = anomaly / jnp.maximum(spread, spread_floor)
    scores = jnp.transpose(scores).astype(jnp.bfloat16)

    held = iota((M, 4 * M), 0)
    rest = held - 32
    member = jnp.where(
        held < 32,
        12 * (held >> 3) + (held & 7),
        12 * (rest >> 2) + 8 + (rest & 3))
    widen = ((iota((M, 4 * M), 1) >> 2) == member).astype(jnp.bfloat16)
    wide[...] = jnp.dot(scores, widen, preferred_element_type=jnp.float32).astype(jnp.bfloat16)
    repeat = ((iota((ROWS, ROWS // 4), 0) >> 2) == iota((ROWS, ROWS // 4), 1)).astype(
        jnp.bfloat16)
    keep = (iota((ROWS, 4 * M), 0) & 3) == (iota((ROWS, 4 * M), 1) & 3)
    areas = ROWS // 4

    half = 4 * AREAS // ROWS // 2

    def part(q, i):
        some = pl.ds(pl.multiple_of(2 * areas * q, 2 * areas), 2 * areas)
        return pltpu.make_async_copy(stage.at[some, i], out.at[some, i], out_sem.at[QUADS * q + i])

    def step(q, carry):
        first = [pl.multiple_of((2 * q + r) * areas, areas) for r in range(2)]
        for r in range(2):
            rows = jnp.dot(repeat, wide[pl.ds(first[r], areas)],
                           preferred_element_type=jnp.float32)
            lhs[r] = jnp.where(keep, rows, 0.0).astype(jnp.bfloat16)
        for i in range(QUADS):
            for r in range(2):
                parts = []
                for h in range(2):
                    acc = jnp.dot(lhs[r], slab[i, :, pl.ds(2 * LANES * h, 2 * LANES)],
                                  preferred_element_type=jnp.float32)
                    acc = (acc * (1.0 / (M - 1))).reshape(ROWS // 8, 8, 2 * LANES)
                    both = swap_halves(acc[:, :, :LANES], acc[:, :, LANES:])
                    parts.append(jnp.stack(both, axis=1).reshape(areas, 8, LANES))
                done = jnp.stack(parts, axis=1).reshape(areas, 16, LANES)
                stage[pl.ds(first[r], areas), i] = done.astype(jnp.bfloat16)
            part(q, i).start(priority=i % 2)
        return carry

    lax.fori_loop(0, half, step, 0)

    def finish(q, carry):
        for i in range(QUADS):
            part(q, i).wait()
        return carry

    lax.fori_loop(0, half, finish, 0)


def product(metric, slab):
    any_space = pl.BlockSpec(memory_space=pl.ANY)
    dma = pltpu.SemaphoreType.DMA
    return pl.pallas_call(
        product_kernel,
        out_shape=jax.ShapeDtypeStruct((AREAS, QUADS, 16, LANES), jnp.bfloat16),
        in_specs=[pl.BlockSpec(memory_space=pltpu.VMEM)] * 2,
        out_specs=any_space,
        scratch_shapes=[
            pltpu.VMEM((AREAS, 4 * M), jnp.bfloat16),
            pltpu.VMEM((2, ROWS, 4 * M), jnp.bfloat16),
            pltpu.VMEM((AREAS, QUADS, 16, LANES), jnp.bfloat16),
            dma((32,)),
        ],
        compiler_params=pltpu.CompilerParams(vmem_limit_bytes=32 * 2**20),
        cost_estimate=pl.CostEstimate(
            flops=2 * 2048 * 192 * 4096, bytes_accessed=20 * 2**20, transcendentals=0),
        name="product",
    )(metric, slab)


def body(tiles, farm_area, capacity, offsets, state):
    by_member = jnp.transpose(tiles, (1, 2, 0))
    columns = state.reshape(M, 2, 64, LANES)
    columns = jnp.transpose(columns, (0, 2, 1, 3)).reshape(M, QUADS, 16, LANES)
    metric, slab = exchange(
        by_member, farm_area.reshape(1, F), capacity.reshape(1, F), offsets, columns)
    out = product(metric, slab)
    out = jnp.transpose(out.reshape(AREAS, 64, 2, LANES), (0, 2, 1, 3))
    return out.reshape(AREAS, 2, 64 * LANES)


def solution(mesh):
    in_specs = (P("grid", None, None), P("grid"), P("grid"), P("grid"), P(None, "lev", "grid"))
    out_specs = P(None, "lev", "grid")
    return jax.shard_map(body, mesh=mesh, in_specs=in_specs, out_specs=out_specs, check_vma=False)
```

```python
import jax
import jax.numpy as jnp
from jax import lax
from jax.experimental import pallas as pl
from jax.experimental.pallas import tpu as pltpu
from jax.sharding import PartitionSpec as P

MESH = pl.DeviceIdType.MESH
M = 48
T = 144
F = 256
AREAS = 512
LANES = 128
RING = 4
ONES = 16
PAD_X = ONES + T
ROWS_Z = 80
PAD_Z = 96
HALF = 64
RAMPS = 132
RAMPS_Z = 68
KEEP_X = 152
KEEP_Z = 88
QUADS = 8
ROWS = 256
capacity_floor = 200.0
spread_floor = 0.05


def iota(shape, dim):
    return lax.broadcasted_iota(jnp.int32, shape, dim)


def swap_halves(u, v):
    low = iota(u.shape, 1) < 4
    crossed = pltpu.roll(jnp.where(low, v, u), 4, 1)
    return jnp.where(low, u, crossed), jnp.where(low, crossed, v)


def ramp_metric(power, offset, first, last):
    steps = power.shape[0]
    wide = jnp.broadcast_to(offset, power.shape).astype(jnp.int32)
    later = power
    for bit in (1, 2, 4, 8):
        later = jnp.where((wide & bit) != 0, pltpu.roll(later, steps - bit, 0), later)
    row = iota(power.shape, 0)
    inside = (row >= first) & (row < last)
    return jnp.max(jnp.where(inside, later - power, -3e38), axis=0, keepdims=True)


STEP = (0, 0, 1, 1, 3, 3, 2, 2)
BACK = (0, 1, 4, 5, 2, 3, 6, 7)
ORDER = (6, 7, 2, 4, 3, 5, 1)
NEAR = 6
STARTS, ROWS_X, SKIP = (0, 96), (96, 48), (ONES, 0)


def exchange_kernel(
    tiles, farm_area, capacity, offsets, state, metric_out, slab_out,
    area_in, capacity_in, offsets_in, near_tiles,
    facts_x, facts_z, got_a, got_b, got_z, weight_x, weight_z,
    part_x, part_z, sum_x, sum_z, near_x, off_x, off_z,
    metrics, st,
    local_sem, fx_send, fx_recv, fz_send, fz_recv, x_send, x_recv, z_send, z_recv,
    bx_send, bx_recv, bz_send, bz_recv,
    all_send, all_recv,
):
    g = lax.axis_index("grid")
    y = lax.axis_index("lev")
    z = lax.div(g, 8)
    x = lax.rem(lax.div(g, 2), 4)
    c = lax.rem(g, 2)
    mine_x = 2 * x + c
    mine_z = 2 * z + c
    xs = [x] + [lax.rem(x + d, 4) for d in range(1, 4)]
    zs = [z] + [lax.rem(z + d, 4) for d in range(1, 4)]
    ys = [y] + [lax.rem(y + d, 4) for d in range(1, 4)]
    cs = [c, 1 - c]

    def device(xx, zz, cc, yy):
        return (zz * 8 + xx * 2 + cc, yy)

    sibling = device(x, z, 1 - c, y)
    x_peers = [(xs[STEP[i]], cs[i % 2]) for i in range(8)]
    z_peers = [(zs[STEP[i]], cs[i % 2]) for i in range(8)]

    def remote(src, dst, send_sem, recv_sem, to):
        return pltpu.make_async_remote_copy(
            src_ref=src, dst_ref=dst, send_sem=send_sem, recv_sem=recv_sem,
            device_id=to, device_id_type=MESH)

    def wait_for(slot, send, recv):
        remote(slot, slot, send, recv, sibling).wait_recv()

    def loop(first, last):
        def run(body):
            lax.fori_loop(first, last, lambda i, carry: (body(i), carry)[1], 0)
        return run

    got_x = (got_a, got_b)
    barrier = pltpu.get_barrier_semaphore()

    def greet(to):
        pl.semaphore_signal(barrier, inc=1, device_id=to, device_id_type=MESH)

    for i in ORDER:
        xx, cc = x_peers[i]
        greet(device(xx, z, cc, y))
        if i != 1:
            zz, cc = z_peers[i]
            greet(device(x, zz, cc, y))
    for d in (2, 1, 3):
        greet(device(x, z, c, ys[d]))

    def x_slot(i, half):
        return got_x[half].at[i, pl.ds(SKIP[half], ROWS_X[half])]

    def z_slot(i):
        return got_z.at[i, pl.ds(0, ROWS_Z)]

    def x_tile(xx, cc):
        return near_tiles.at[2 * xx + cc]

    def z_tile(zz, cc):
        return near_tiles.at[8 + zz, pl.ds(pl.multiple_of(HALF * cc, HALF), ROWS_Z)]

    local = [
        pltpu.make_async_copy(farm_area, area_in, local_sem.at[0]),
        pltpu.make_async_copy(capacity, capacity_in, local_sem.at[1]),
        pltpu.make_async_copy(offsets, offsets_in, local_sem.at[2]),
        pltpu.make_async_copy(tiles.at[pl.ds(12 * y, 12)], near_tiles, local_sem.at[6]),
        pltpu.make_async_copy(
            tiles.at[12 * y + 8 + z, pl.ds(pl.multiple_of(HALF * c, HALF), ROWS_Z)],
            z_slot(0), local_sem.at[3]),
        pltpu.make_async_copy(
            tiles.at[12 * y + mine_x, pl.ds(STARTS[0], ROWS_X[0])], x_slot(0, 0),
            local_sem.at[4]),
        pltpu.make_async_copy(
            tiles.at[12 * y + mine_x, pl.ds(STARTS[1], ROWS_X[1])], x_slot(0, 1),
            local_sem.at[7]),
        pltpu.make_async_copy(state, st, local_sem.at[5]),
    ]
    for copy in local[:4]:
        copy.start()
    def fx_copy(i):
        xx, cc = x_peers[i]
        return remote(facts_x.at[0], facts_x.at[BACK[i]], fx_send.at[i], fx_recv.at[BACK[i]],
                      device(xx, z, cc, y))

    def fz_copy(i):
        zz, cc = z_peers[i]
        return remote(facts_z.at[0], facts_z.at[BACK[i]], fz_send.at[i], fz_recv.at[BACK[i]],
                      device(x, zz, cc, y))

    def x_copy(i, half):
        xx, cc = x_peers[i]
        return remote(x_tile(xx, cc).at[pl.ds(STARTS[half], ROWS_X[half])], x_slot(BACK[i], half),
                      x_send.at[half, i], x_recv.at[half, BACK[i]], device(xx, z, cc, y))

    def z_copy(i):
        zz, cc = z_peers[i]
        return remote(z_tile(zz, cc), z_slot(BACK[i]), z_send.at[i], z_recv.at[BACK[i]],
                      device(x, zz, cc, y))

    sends = []

    def start(*copies):
        for copy in copies:
            copy.start()
            sends.append(copy)

    for copy in local[:3]:
        copy.wait()

    lane = iota((1, F), 1)
    offset = jnp.zeros((1, F), jnp.int32)
    for k in range(16):
        offset = jnp.where((lane & 15) == k, offsets_in[k], offset)
    area = area_in[...]
    turned = ((area >> 5) & 3) * 128 + (area >> 7) * 32 + (area & 31)
    for facts, ids, spot in ((facts_z, turned, mine_z), (facts_x, area, mine_x)):
        placed = jnp.where((lane >> 4) == spot, offset, 0)
        rows = jnp.concatenate(
            [ids, capacity_in[...], placed, jnp.zeros((1, F), jnp.int32)], axis=0)
        facts[0] = rows.astype(jnp.float32)

    pl.semaphore_wait(barrier, 16)
    for i in ORDER:
        start(fx_copy(i), fz_copy(i))
    local[3].wait()
    for i in ORDER:
        start(x_copy(i, 0), z_copy(i))
    for i in ORDER[2:] + ORDER[:2]:
        start(x_copy(i, 1))
    for copy in local[4:]:
        copy.start()

    got_a[:, pl.ds(0, ONES)] = jnp.ones((8, ONES, F), jnp.bfloat16)
    got_z[:, pl.ds(ROWS_Z, ONES)] = jnp.ones((8, ONES, F), jnp.bfloat16)
    off_x[...] = jnp.zeros_like(off_x)
    off_z[...] = jnp.zeros_like(off_z)
    area_ids = iota((AREAS, F), 0).astype(jnp.float32)

    def weigh(i, facts, weight, off):
        rows = facts[i]
        off[...] = off[...] + rows[2:3, :LANES]
        placed = jnp.where(area_ids == rows[0:1], rows[1:2], 0.0)
        weight[:, pl.ds(pl.multiple_of(F * i, F), F)] = placed.astype(jnp.bfloat16)

    @loop(0, 8)
    def _(i):
        for facts, recv, send, weight, off in (
                (facts_z, fz_recv, fz_send, weight_z, off_z),
                (facts_x, fx_recv, fx_send, weight_x, off_x)):
            @pl.when(i > 0)
            def _():
                wait_for(facts.at[i], send.at[i], recv.at[i])

            weigh(i, facts, weight, off)

    def sum_up(values, weights):
        return lax.dot_general(values, weights, (((1,), (1,)), ((), ())),
                               preferred_element_type=jnp.float32)

    bz = []

    near, far, all_slots = range(NEAR), range(NEAR, 8), range(8)

    def block_pair(p):
        return lax.rem(z + 2 + p, 4), lax.rem(z + 1 + 3 * p, 4)

    def side_by_side(got, slots):
        return jnp.concatenate([got[i] for i in slots], axis=1)

    def dot_x(half, p, slots):
        columns = pl.ds(F * slots[0], F * len(slots))
        chosen = jnp.concatenate(
            [weight_x[pl.ds(pl.multiple_of(LANES * zz, LANES), LANES), columns]
             for zz in block_pair(p)], axis=0)
        return sum_up(side_by_side(got_x[half], slots), chosen)

    def sum_copy(half, rows, d, zz):
        return remote(part_x.at[zz, rows], sum_x.at[3 - d, rows], bx_send.at[half, d - 1],
                      bx_recv.at[half, 3 - d], device(x, zz, c, y))

    def leave(half, rows, p, value):
        for k, zz in enumerate(block_pair(p)):
            part_x[zz, rows] = value[:, k * LANES : (k + 1) * LANES]
        sum_copy(half, rows, 2 + p, block_pair(p)[0]).start()

        @pl.when(p == 0)
        def _():
            sum_copy(half, rows, 1, zs[1]).start()

    early_rows, late_rows = pl.ds(0, 8 + ROWS_X[0]), pl.ds(8 + ROWS_X[0], ROWS_X[1])
    local[5].wait()
    for i in range(1, 8):
        wait_for(x_slot(i, 0), x_send.at[0, i], x_recv.at[0, i])

    @loop(0, 2)
    def _(p):
        leave(0, early_rows, p, dot_x(0, p, all_slots)[8:])

    local[4].wait()
    for i in range(1, 8):
        wait_for(z_slot(i), z_send.at[i], z_recv.at[i])
    for h in range(2):
        value = sum_up(side_by_side(got_z, all_slots), weight_z[pl.ds(2 * LANES * h, 2 * LANES)])
        for b in range(2):
            part_z[2 * h + b] = value[:KEEP_Z, b * LANES : (b + 1) * LANES]
    for d in (2, 1, 3):
        copy = remote(part_z.at[xs[d]], sum_z.at[3 - d], bz_send.at[d - 1], bz_recv.at[3 - d],
                      device(xs[d], z, c, y))
        copy.start()
        bz.append(copy)

    local[6].wait()
    for i in range(1, NEAR):
        wait_for(x_slot(i, 1), x_send.at[1, i], x_recv.at[1, i])

    @loop(0, 2)
    def _(p):
        near_x[p] = dot_x(1, p, near)

    for i in range(NEAR, 8):
        wait_for(x_slot(i, 1), x_send.at[1, i], x_recv.at[1, i])

    @loop(0, 2)
    def _(p):
        leave(1, late_rows, p, near_x[p] + dot_x(1, p, far))

    bx = [[sum_copy(half, rows, d, zs[d]) for d in range(1, 4)]
          for half, rows in ((0, early_rows), (1, late_rows))]

    def whole(copies, own, others, rows):
        for copy in copies:
            copy.wait_recv()
        total = own[rows]
        for k in range(3):
            total = total + others[k, rows]
        return total

    spot = (4 * y + z) * 8 + mine_x

    first = whole(bx[0], part_x.at[z], sum_x, early_rows)
    total = jnp.maximum(first[:1], capacity_floor)
    power = first[8:] / total
    early = ramp_metric(power, off_x[...], 0, 84)
    last = whole(bz, part_z.at[x], sum_z, pl.ds(0, KEEP_Z))
    metrics[spot, pl.ds(1, 1)] = ramp_metric(
        last[:ROWS_Z] / jnp.maximum(last[ROWS_Z : ROWS_Z + 1], capacity_floor),
        off_z[...], 0, RAMPS_Z)
    last = whole(bx[1], part_x.at[z], sum_x, late_rows)
    power = jnp.concatenate([power[80:], last / total], axis=0)
    late = ramp_metric(power, off_x[...], 4, 52)
    metrics[spot, pl.ds(0, 1)] = jnp.maximum(early, late)

    mine = metrics.at[spot]

    def hops(where):
        dy, dz, i = where
        return sum(min(d, 4 - d) for d in (dy, dz, STEP[i]))

    others = [(dy, dz, i) for dy in range(4) for dz in range(4) for i in range(8)][1:]
    for dy, dz, i in sorted(others, key=hops, reverse=True):
        xx, cc = x_peers[i]
        remote(mine, mine, all_send, all_recv, device(xx, zs[dz], cc, ys[dy])).start()

    local[7].wait()

    @loop(0, QUADS)
    def _(i):
        values = st[:, i].astype(jnp.float32).reshape(M, 2, 8, LANES)
        values = values - (jnp.sum(values, axis=0) / M)[None]
        pairs = values.reshape(M // 2, 2, 2, 8, LANES)
        for h in range(2):
            both = swap_halves(pairs[:, 0, h], pairs[:, 1, h])
            for k in range(2):
                slab_out[i, :, pl.ds((2 * h + k) * LANES, LANES)] = (
                    both[k].reshape(4 * M, LANES).astype(jnp.bfloat16))

    for copy in sends + bx[0] + bx[1] + bz:
        copy.wait_send()

    others = metrics.at[pl.ds(0, 127)]
    everything = remote(others, others, all_send, all_recv, sibling)
    everything.wait_recv()

    rows = metrics.reshape(256, LANES)
    for yy in range(4):
        for zz in range(4):
            metric_out[pl.ds(8 * yy, 8), pl.ds(LANES * zz, LANES)] = (
                rows[pl.ds(16 * (4 * yy + zz), 8, stride=2)])
    quarter = iota((16, LANES), 1) >> 5
    blocks = [jnp.maximum(rows[pl.ds(4 * b + 1, 16, stride=16)], rows[pl.ds(4 * b + 3, 16, stride=16)])
              for b in range(RING)]
    for zz in range(4):
        value = jnp.zeros((16, LANES), jnp.float32)
        for b in range(RING):
            move = (32 * (b - zz)) % LANES
            moved = pltpu.roll(blocks[b], move, 1) if move else blocks[b]
            value = jnp.where(quarter == b, moved, value)
        metric_out[pl.ds(32, 16), pl.ds(zz * LANES, LANES)] = value

    everything.wait_send()


def exchange(tiles, farm_area, capacity, offsets, state):
    any_space = pl.BlockSpec(memory_space=pl.ANY)
    vmem = pl.BlockSpec(memory_space=pltpu.VMEM)
    dma = pltpu.SemaphoreType.DMA
    f32, bf16 = jnp.float32, jnp.bfloat16
    return pl.pallas_call(
        exchange_kernel,
        out_shape=(
            pltpu.VMEM((M, AREAS), f32),
            pltpu.VMEM((QUADS, 4 * M, 4 * LANES), bf16),
        ),
        in_specs=[any_space] * 5,
        out_specs=(vmem, vmem),
        scratch_shapes=[
            pltpu.VMEM((1, F), jnp.int32),
            pltpu.VMEM((1, F), jnp.int32),
            pltpu.SMEM((16,), jnp.int32),
            pltpu.VMEM((12, T, F), bf16),
            pltpu.VMEM((8, 4, F), f32),
            pltpu.VMEM((8, 4, F), f32),
            pltpu.VMEM((8, ONES + ROWS_X[0], F), bf16),
            pltpu.VMEM((8, ROWS_X[1], F), bf16),
            pltpu.VMEM((8, ROWS_Z + ONES, F), bf16),
            pltpu.VMEM((AREAS, 8 * F), bf16),
            pltpu.VMEM((AREAS, 8 * F), bf16),
            pltpu.VMEM((RING, KEEP_X, LANES), f32),
            pltpu.VMEM((RING, KEEP_Z, LANES), f32),
            pltpu.VMEM((3, KEEP_X, LANES), f32),
            pltpu.VMEM((3, KEEP_Z, LANES), f32),
            pltpu.VMEM((2, ROWS_X[1], 2 * LANES), f32),
            pltpu.VMEM((1, LANES), f32),
            pltpu.VMEM((1, LANES), f32),
            pltpu.VMEM((128, 2, LANES), f32),
            pltpu.VMEM((M, QUADS, 16, LANES), bf16),
            dma((8,)), dma((8,)), dma((8,)), dma((8,)), dma((8,)),
            dma((2, 8)), dma((2, 8)), dma((8,)), dma((8,)),
            dma((2, 3)), dma((2, 3)), dma((3,)), dma((3,)),
            dma, dma,
        ],
        compiler_params=pltpu.CompilerParams(
            collective_id=0, has_side_effects=True, vmem_limit_bytes=60 * 2**20),
        cost_estimate=pl.CostEstimate(
            flops=2 * 256 * 2048 * 512, bytes_accessed=5 * 2**20, transcendentals=0),
        name="exchange",
    )(tiles, farm_area, capacity, offsets, state)


def product_kernel(metric, slab, out, wide, lhs, stage, out_sem):
    values = metric[...]
    anomaly = values - jnp.mean(values, axis=0, keepdims=True)
    spread = jnp.sqrt(jnp.sum(anomaly * anomaly, axis=0, keepdims=True) / (M - 1))
    scores = anomaly / jnp.maximum(spread, spread_floor)
    scores = jnp.transpose(scores).astype(jnp.bfloat16)

    held = iota((M, 4 * M), 0)
    rest = held - 32
    member = jnp.where(
        held < 32,
        12 * (held >> 3) + (held & 7),
        12 * (rest >> 2) + 8 + (rest & 3))
    widen = ((iota((M, 4 * M), 1) >> 2) == member).astype(jnp.bfloat16)
    wide[...] = jnp.dot(scores, widen, preferred_element_type=jnp.float32).astype(jnp.bfloat16)
    repeat = ((iota((ROWS, ROWS // 4), 0) >> 2) == iota((ROWS, ROWS // 4), 1)).astype(
        jnp.bfloat16)
    keep = (iota((ROWS, 4 * M), 0) & 3) == (iota((ROWS, 4 * M), 1) & 3)
    areas = ROWS // 4

    half = 4 * AREAS // ROWS // 2

    def part(q, i):
        some = pl.ds(pl.multiple_of(2 * areas * q, 2 * areas), 2 * areas)
        return pltpu.make_async_copy(stage.at[some, i], out.at[some, i], out_sem.at[QUADS * q + i])

    def step(q, carry):
        first = [pl.multiple_of((2 * q + r) * areas, areas) for r in range(2)]
        for r in range(2):
            rows = jnp.dot(repeat, wide[pl.ds(first[r], areas)],
                           preferred_element_type=jnp.float32)
            lhs[r] = jnp.where(keep, rows, 0.0).astype(jnp.bfloat16)
        for i in range(QUADS):
            for r in range(2):
                parts = []
                for h in range(2):
                    acc = jnp.dot(lhs[r], slab[i, :, pl.ds(2 * LANES * h, 2 * LANES)],
                                  preferred_element_type=jnp.float32)
                    acc = (acc * (1.0 / (M - 1))).reshape(ROWS // 8, 8, 2 * LANES)
                    both = swap_halves(acc[:, :, :LANES], acc[:, :, LANES:])
                    parts.append(jnp.stack(both, axis=1).reshape(areas, 8, LANES))
                done = jnp.stack(parts, axis=1).reshape(areas, 16, LANES)
                stage[pl.ds(first[r], areas), i] = done.astype(jnp.bfloat16)
            part(q, i).start(priority=i % 2)
        return carry

    lax.fori_loop(0, half, step, 0)

    def finish(q, carry):
        for i in range(QUADS):
            part(q, i).wait()
        return carry

    lax.fori_loop(0, half, finish, 0)


def product(metric, slab):
    any_space = pl.BlockSpec(memory_space=pl.ANY)
    dma = pltpu.SemaphoreType.DMA
    return pl.pallas_call(
        product_kernel,
        out_shape=jax.ShapeDtypeStruct((AREAS, QUADS, 16, LANES), jnp.bfloat16),
        in_specs=[pl.BlockSpec(memory_space=pltpu.VMEM)] * 2,
        out_specs=any_space,
        scratch_shapes=[
            pltpu.VMEM((AREAS, 4 * M), jnp.bfloat16),
            pltpu.VMEM((2, ROWS, 4 * M), jnp.bfloat16),
            pltpu.VMEM((AREAS, QUADS, 16, LANES), jnp.bfloat16),
            dma((32,)),
        ],
        compiler_params=pltpu.CompilerParams(vmem_limit_bytes=32 * 2**20),
        cost_estimate=pl.CostEstimate(
            flops=2 * 2048 * 192 * 4096, bytes_accessed=20 * 2**20, transcendentals=0),
        name="product",
    )(metric, slab)


def body(tiles, farm_area, capacity, offsets, state):
    by_member = jnp.transpose(tiles, (1, 2, 0))
    columns = state.reshape(M, 2, 64, LANES)
    columns = jnp.transpose(columns, (0, 2, 1, 3)).reshape(M, QUADS, 16, LANES)
    metric, slab = exchange(
        by_member, farm_area.reshape(1, F), capacity.reshape(1, F), offsets, columns)
    out = product(metric, slab)
    out = jnp.transpose(out.reshape(AREAS, 64, 2, LANES), (0, 2, 1, 3))
    return out.reshape(AREAS, 2, 64 * LANES)


def solution(mesh):
    in_specs = (P("grid", None, None), P("grid"), P("grid"), P("grid"), P(None, "lev", "grid"))
    out_specs = P(None, "lev", "grid")
    return jax.shard_map(body, mesh=mesh, in_specs=in_specs, out_specs=out_specs, check_vma=False)
```

```python
import jax
import jax.numpy as jnp
from jax import lax
from jax.experimental import pallas as pl
from jax.experimental.pallas import tpu as pltpu
from jax.sharding import PartitionSpec as P

MESH = pl.DeviceIdType.MESH
M = 48
T = 144
F = 256
AREAS = 512
LANES = 128
RING = 4
ONES = 16
PAD_X = ONES + T
ROWS_Z = 80
PAD_Z = 96
HALF = 64
RAMPS = 132
RAMPS_Z = 68
KEEP_X = 152
KEEP_Z = 88
QUADS = 8
ROWS = 256
capacity_floor = 200.0
spread_floor = 0.05


def iota(shape, dim):
    return lax.broadcasted_iota(jnp.int32, shape, dim)


def swap_halves(u, v):
    low = iota(u.shape, 1) < 4
    crossed = pltpu.roll(jnp.where(low, v, u), 4, 1)
    return jnp.where(low, u, crossed), jnp.where(low, crossed, v)


def ramp_metric(power, offset, first, last):
    steps = power.shape[0]
    wide = jnp.broadcast_to(offset, power.shape).astype(jnp.int32)
    later = power
    for bit in (1, 2, 4, 8):
        later = jnp.where((wide & bit) != 0, pltpu.roll(later, steps - bit, 0), later)
    row = iota(power.shape, 0)
    inside = (row >= first) & (row < last)
    return jnp.max(jnp.where(inside, later - power, -3e38), axis=0, keepdims=True)


STEP = (0, 0, 1, 1, 3, 3, 2, 2)
BACK = (0, 1, 4, 5, 2, 3, 6, 7)
ORDER = (6, 7, 2, 4, 3, 5, 1)
NEAR = 6
STARTS, ROWS_X, SKIP = (0, 96), (96, 48), (ONES, 0)


def exchange_kernel(
    tiles, farm_area, capacity, offsets, state, metric_out, slab_out,
    area_in, capacity_in, offsets_in, near_tiles,
    facts_x, facts_z, got_a, got_b, got_z, weight_x, weight_z,
    part_x, part_z, sum_x, sum_z, near_x, off_x, off_z,
    metrics, st,
    local_sem, fx_send, fx_recv, fz_send, fz_recv, x_send, x_recv, z_send, z_recv,
    bx_send, bx_recv, bz_send, bz_recv,
    all_send, all_recv,
):
    g = lax.axis_index("grid")
    y = lax.axis_index("lev")
    z = lax.div(g, 8)
    x = lax.rem(lax.div(g, 2), 4)
    c = lax.rem(g, 2)
    mine_x = 2 * x + c
    mine_z = 2 * z + c
    xs = [x] + [lax.rem(x + d, 4) for d in range(1, 4)]
    zs = [z] + [lax.rem(z + d, 4) for d in range(1, 4)]
    ys = [y] + [lax.rem(y + d, 4) for d in range(1, 4)]
    cs = [c, 1 - c]

    def device(xx, zz, cc, yy):
        return (zz * 8 + xx * 2 + cc, yy)

    sibling = device(x, z, 1 - c, y)
    x_peers = [(xs[STEP[i]], cs[i % 2]) for i in range(8)]
    z_peers = [(zs[STEP[i]], cs[i % 2]) for i in range(8)]

    def remote(src, dst, send_sem, recv_sem, to):
        return pltpu.make_async_remote_copy(
            src_ref=src, dst_ref=dst, send_sem=send_sem, recv_sem=recv_sem,
            device_id=to, device_id_type=MESH)

    def wait_for(slot, send, recv):
        remote(slot, slot, send, recv, sibling).wait_recv()

    def loop(first, last):
        def run(body):
            lax.fori_loop(first, last, lambda i, carry: (body(i), carry)[1], 0)
        return run

    got_x = (got_a, got_b)
    barrier = pltpu.get_barrier_semaphore()

    def greet(to):
        pl.semaphore_signal(barrier, inc=1, device_id=to, device_id_type=MESH)

    for i in ORDER:
        xx, cc = x_peers[i]
        greet(device(xx, z, cc, y))
        if i != 1:
            zz, cc = z_peers[i]
            greet(device(x, zz, cc, y))
    for d in (2, 1, 3):
        greet(device(x, z, c, ys[d]))

    def x_slot(i, half):
        return got_x[half].at[i, pl.ds(SKIP[half], ROWS_X[half])]

    def z_slot(i):
        return got_z.at[i, pl.ds(0, ROWS_Z)]

    def x_tile(xx, cc):
        return near_tiles.at[2 * xx + cc]

    def z_tile(zz, cc):
        return near_tiles.at[8 + zz, pl.ds(pl.multiple_of(HALF * cc, HALF), ROWS_Z)]

    local = [
        pltpu.make_async_copy(farm_area, area_in, local_sem.at[0]),
        pltpu.make_async_copy(capacity, capacity_in, local_sem.at[1]),
        pltpu.make_async_copy(offsets, offsets_in, local_sem.at[2]),
        pltpu.make_async_copy(tiles.at[pl.ds(12 * y, 12)], near_tiles, local_sem.at[6]),
        pltpu.make_async_copy(
            tiles.at[12 * y + 8 + z, pl.ds(pl.multiple_of(HALF * c, HALF), ROWS_Z)],
            z_slot(0), local_sem.at[3]),
        pltpu.make_async_copy(
            tiles.at[12 * y + mine_x, pl.ds(STARTS[0], ROWS_X[0])], x_slot(0, 0),
            local_sem.at[4]),
        pltpu.make_async_copy(
            tiles.at[12 * y + mine_x, pl.ds(STARTS[1], ROWS_X[1])], x_slot(0, 1),
            local_sem.at[7]),
        pltpu.make_async_copy(state, st, local_sem.at[5]),
    ]
    for copy in local[:4]:
        copy.start()
    def fx_copy(i):
        xx, cc = x_peers[i]
        return remote(facts_x.at[0], facts_x.at[BACK[i]], fx_send.at[i], fx_recv.at[BACK[i]],
                      device(xx, z, cc, y))

    def fz_copy(i):
        zz, cc = z_peers[i]
        return remote(facts_z.at[0], facts_z.at[BACK[i]], fz_send.at[i], fz_recv.at[BACK[i]],
                      device(x, zz, cc, y))

    def x_copy(i, half):
        xx, cc = x_peers[i]
        return remote(x_tile(xx, cc).at[pl.ds(STARTS[half], ROWS_X[half])], x_slot(BACK[i], half),
                      x_send.at[half, i], x_recv.at[half, BACK[i]], device(xx, z, cc, y))

    def z_copy(i):
        zz, cc = z_peers[i]
        return remote(z_tile(zz, cc), z_slot(BACK[i]), z_send.at[i], z_recv.at[BACK[i]],
                      device(x, zz, cc, y))

    sends = []

    def start(*copies):
        for copy in copies:
            copy.start()
            sends.append(copy)

    for copy in local[:3]:
        copy.wait()

    lane = iota((1, F), 1)
    offset = jnp.zeros((1, F), jnp.int32)
    for k in range(16):
        offset = jnp.where((lane & 15) == k, offsets_in[k], offset)
    area = area_in[...]
    turned = ((area >> 5) & 3) * 128 + (area >> 7) * 32 + (area & 31)
    for facts, ids, spot in ((facts_z, turned, mine_z), (facts_x, area, mine_x)):
        placed = jnp.where((lane >> 4) == spot, offset, 0)
        rows = jnp.concatenate(
            [ids, capacity_in[...], placed, jnp.zeros((1, F), jnp.int32)], axis=0)
        facts[0] = rows.astype(jnp.float32)

    pl.semaphore_wait(barrier, 16)
    for i in ORDER:
        start(fx_copy(i), fz_copy(i))
    local[3].wait()
    for i in ORDER:
        start(x_copy(i, 0), z_copy(i))
    for i in ORDER[2:] + ORDER[:2]:
        start(x_copy(i, 1))
    for copy in local[4:]:
        copy.start()

    got_a[:, pl.ds(0, ONES)] = jnp.ones((8, ONES, F), jnp.bfloat16)
    got_z[:, pl.ds(ROWS_Z, ONES)] = jnp.ones((8, ONES, F), jnp.bfloat16)
    off_x[...] = jnp.zeros_like(off_x)
    off_z[...] = jnp.zeros_like(off_z)
    area_ids = iota((AREAS, F), 0).astype(jnp.float32)

    def weigh(i, facts, weight, off):
        rows = facts[i]
        off[...] = off[...] + rows[2:3, :LANES]
        placed = jnp.where(area_ids == rows[0:1], rows[1:2], 0.0)
        weight[:, pl.ds(pl.multiple_of(F * i, F), F)] = placed.astype(jnp.bfloat16)

    @loop(0, 8)
    def _(i):
        for facts, recv, send, weight, off in (
                (facts_z, fz_recv, fz_send, weight_z, off_z),
                (facts_x, fx_recv, fx_send, weight_x, off_x)):
            @pl.when(i > 0)
            def _():
                wait_for(facts.at[i], send.at[i], recv.at[i])

            weigh(i, facts, weight, off)

    def sum_up(values, weights):
        return lax.dot_general(values, weights, (((1,), (1,)), ((), ())),
                               preferred_element_type=jnp.float32)

    bz = []

    near, far, all_slots = range(NEAR), range(NEAR, 8), range(8)

    def block_pair(p):
        return lax.rem(z + 2 + p, 4), lax.rem(z + 1 + 3 * p, 4)

    def side_by_side(got, slots):
        return jnp.concatenate([got[i] for i in slots], axis=1)

    def dot_x(half, p, slots):
        columns = pl.ds(F * slots[0], F * len(slots))
        chosen = jnp.concatenate(
            [weight_x[pl.ds(pl.multiple_of(LANES * zz, LANES), LANES), columns]
             for zz in block_pair(p)], axis=0)
        return sum_up(side_by_side(got_x[half], slots), chosen)

    def sum_copy(half, rows, d, zz):
        return remote(part_x.at[zz, rows], sum_x.at[3 - d, rows], bx_send.at[half, d - 1],
                      bx_recv.at[half, 3 - d], device(x, zz, c, y))

    def leave(half, rows, p, value):
        for k, zz in enumerate(block_pair(p)):
            part_x[zz, rows] = value[:, k * LANES : (k + 1) * LANES]
        sum_copy(half, rows, 2 + p, block_pair(p)[0]).start()

        @pl.when(p == 0)
        def _():
            sum_copy(half, rows, 1, zs[1]).start()

    early_rows, late_rows = pl.ds(0, 8 + ROWS_X[0]), pl.ds(8 + ROWS_X[0], ROWS_X[1])
    local[5].wait()
    for i in range(1, 8):
        wait_for(x_slot(i, 0), x_send.at[0, i], x_recv.at[0, i])

    @loop(0, 2)
    def _(p):
        leave(0, early_rows, p, dot_x(0, p, all_slots)[8:])

    local[4].wait()
    for i in range(1, 8):
        wait_for(z_slot(i), z_send.at[i], z_recv.at[i])
    for h in range(2):
        value = sum_up(side_by_side(got_z, all_slots), weight_z[pl.ds(2 * LANES * h, 2 * LANES)])
        for b in range(2):
            part_z[2 * h + b] = value[:KEEP_Z, b * LANES : (b + 1) * LANES]
    for d in (2, 1, 3):
        copy = remote(part_z.at[xs[d]], sum_z.at[3 - d], bz_send.at[d - 1], bz_recv.at[3 - d],
                      device(xs[d], z, c, y))
        copy.start()
        bz.append(copy)

    local[6].wait()
    for i in range(1, NEAR):
        wait_for(x_slot(i, 1), x_send.at[1, i], x_recv.at[1, i])

    @loop(0, 2)
    def _(p):
        near_x[p] = dot_x(1, p, near)

    for i in range(NEAR, 8):
        wait_for(x_slot(i, 1), x_send.at[1, i], x_recv.at[1, i])

    @loop(0, 2)
    def _(p):
        leave(1, late_rows, p, near_x[p] + dot_x(1, p, far))

    bx = [[sum_copy(half, rows, d, zs[d]) for d in range(1, 4)]
          for half, rows in ((0, early_rows), (1, late_rows))]

    def whole(copies, own, others, rows):
        for copy in copies:
            copy.wait_recv()
        total = own[rows]
        for k in range(3):
            total = total + others[k, rows]
        return total

    spot = (4 * y + z) * 8 + mine_x

    first = whole(bx[0], part_x.at[z], sum_x, early_rows)
    total = jnp.maximum(first[:1], capacity_floor)
    power = first[8:] / total
    early = ramp_metric(power, off_x[...], 0, 84)
    last = whole(bz, part_z.at[x], sum_z, pl.ds(0, KEEP_Z))
    metrics[spot, pl.ds(1, 1)] = ramp_metric(
        last[:ROWS_Z] / jnp.maximum(last[ROWS_Z : ROWS_Z + 1], capacity_floor),
        off_z[...], 0, RAMPS_Z)
    last = whole(bx[1], part_x.at[z], sum_x, late_rows)
    power = jnp.concatenate([power[80:], last / total], axis=0)
    late = ramp_metric(power, off_x[...], 4, 52)
    metrics[spot, pl.ds(0, 1)] = jnp.maximum(early, late)

    mine = metrics.at[spot]

    def hops(where):
        dy, dz, i = where
        return sum(min(d, 4 - d) for d in (dy, dz, STEP[i]))

    others = [(dy, dz, i) for dy in range(4) for dz in range(4) for i in range(8)][1:]
    for dy, dz, i in sorted(others, key=hops, reverse=True):
        xx, cc = x_peers[i]
        remote(mine, mine, all_send, all_recv, device(xx, zs[dz], cc, ys[dy])).start()

    local[7].wait()

    @loop(0, QUADS)
    def _(i):
        values = st[:, i].astype(jnp.float32).reshape(M, 2, 8, LANES)
        values = values - (jnp.sum(values, axis=0) / M)[None]
        pairs = values.reshape(M // 2, 2, 2, 8, LANES)
        for h in range(2):
            both = swap_halves(pairs[:, 0, h], pairs[:, 1, h])
            for k in range(2):
                slab_out[i, :, pl.ds((2 * h + k) * LANES, LANES)] = (
                    both[k].reshape(4 * M, LANES).astype(jnp.bfloat16))

    for copy in sends + bx[0] + bx[1] + bz:
        copy.wait_send()

    others = metrics.at[pl.ds(0, 127)]
    everything = remote(others, others, all_send, all_recv, sibling)
    everything.wait_recv()

    rows = metrics.reshape(256, LANES)
    for yy in range(4):
        for zz in range(4):
            metric_out[pl.ds(8 * yy, 8), pl.ds(LANES * zz, LANES)] = (
                rows[pl.ds(16 * (4 * yy + zz), 8, stride=2)])
    quarter = iota((16, LANES), 1) >> 5
    blocks = [jnp.maximum(rows[pl.ds(4 * b + 1, 16, stride=16)], rows[pl.ds(4 * b + 3, 16, stride=16)])
              for b in range(RING)]
    for zz in range(4):
        value = jnp.zeros((16, LANES), jnp.float32)
        for b in range(RING):
            move = (32 * (b - zz)) % LANES
            moved = pltpu.roll(blocks[b], move, 1) if move else blocks[b]
            value = jnp.where(quarter == b, moved, value)
        metric_out[pl.ds(32, 16), pl.ds(zz * LANES, LANES)] = value

    everything.wait_send()


def exchange(tiles, farm_area, capacity, offsets, state):
    any_space = pl.BlockSpec(memory_space=pl.ANY)
    vmem = pl.BlockSpec(memory_space=pltpu.VMEM)
    dma = pltpu.SemaphoreType.DMA
    f32, bf16 = jnp.float32, jnp.bfloat16
    return pl.pallas_call(
        exchange_kernel,
        out_shape=(
            pltpu.VMEM((M, AREAS), f32),
            pltpu.VMEM((QUADS, 4 * M, 4 * LANES), bf16),
        ),
        in_specs=[any_space] * 5,
        out_specs=(vmem, vmem),
        scratch_shapes=[
            pltpu.VMEM((1, F), jnp.int32),
            pltpu.VMEM((1, F), jnp.int32),
            pltpu.SMEM((16,), jnp.int32),
            pltpu.VMEM((12, T, F), bf16),
            pltpu.VMEM((8, 4, F), f32),
            pltpu.VMEM((8, 4, F), f32),
            pltpu.VMEM((8, ONES + ROWS_X[0], F), bf16),
            pltpu.VMEM((8, ROWS_X[1], F), bf16),
            pltpu.VMEM((8, ROWS_Z + ONES, F), bf16),
            pltpu.VMEM((AREAS, 8 * F), bf16),
            pltpu.VMEM((AREAS, 8 * F), bf16),
            pltpu.VMEM((RING, KEEP_X, LANES), f32),
            pltpu.VMEM((RING, KEEP_Z, LANES), f32),
            pltpu.VMEM((3, KEEP_X, LANES), f32),
            pltpu.VMEM((3, KEEP_Z, LANES), f32),
            pltpu.VMEM((2, ROWS_X[1], 2 * LANES), f32),
            pltpu.VMEM((1, LANES), f32),
            pltpu.VMEM((1, LANES), f32),
            pltpu.VMEM((128, 2, LANES), f32),
            pltpu.VMEM((M, QUADS, 16, LANES), bf16),
            dma((8,)), dma((8,)), dma((8,)), dma((8,)), dma((8,)),
            dma((2, 8)), dma((2, 8)), dma((8,)), dma((8,)),
            dma((2, 3)), dma((2, 3)), dma((3,)), dma((3,)),
            dma, dma,
        ],
        compiler_params=pltpu.CompilerParams(
            collective_id=0, has_side_effects=True, vmem_limit_bytes=60 * 2**20),
        cost_estimate=pl.CostEstimate(
            flops=2 * 256 * 2048 * 512, bytes_accessed=5 * 2**20, transcendentals=0),
        name="exchange",
    )(tiles, farm_area, capacity, offsets, state)


def product_kernel(metric, slab, out, wide, lhs, stage, out_sem):
    values = metric[...]
    anomaly = values - jnp.mean(values, axis=0, keepdims=True)
    spread = jnp.sqrt(jnp.sum(anomaly * anomaly, axis=0, keepdims=True) / (M - 1))
    scores = anomaly / jnp.maximum(spread, spread_floor)
    scores = jnp.transpose(scores).astype(jnp.bfloat16)

    held = iota((M, 4 * M), 0)
    rest = held - 32
    member = jnp.where(
        held < 32,
        12 * (held >> 3) + (held & 7),
        12 * (rest >> 2) + 8 + (rest & 3))
    widen = ((iota((M, 4 * M), 1) >> 2) == member).astype(jnp.bfloat16)
    wide[...] = jnp.dot(scores, widen, preferred_element_type=jnp.float32).astype(jnp.bfloat16)
    repeat = ((iota((ROWS, ROWS // 4), 0) >> 2) == iota((ROWS, ROWS // 4), 1)).astype(
        jnp.bfloat16)
    keep = (iota((ROWS, 4 * M), 0) & 3) == (iota((ROWS, 4 * M), 1) & 3)
    areas = ROWS // 4

    half = 4 * AREAS // ROWS // 2

    def part(q, i):
        some = pl.ds(pl.multiple_of(2 * areas * q, 2 * areas), 2 * areas)
        return pltpu.make_async_copy(stage.at[some, i], out.at[some, i], out_sem.at[QUADS * q + i])

    def make(q, slot):
        for r in range(2):
            rows = pl.ds(pl.multiple_of((2 * q + r) * areas, areas), areas)
            repeated = jnp.dot(repeat, wide[rows], preferred_element_type=jnp.float32)
            lhs[slot, r] = jnp.where(keep, repeated, 0.0).astype(jnp.bfloat16)

    make(0, 0)

    def step(q, carry):
        first = [pl.multiple_of((2 * q + r) * areas, areas) for r in range(2)]
        slot = q & 1
        for i in range(QUADS):
            for r in range(2):
                parts = []
                for h in range(2):
                    acc = jnp.dot(lhs[slot, r], slab[i, :, pl.ds(2 * LANES * h, 2 * LANES)],
                                  preferred_element_type=jnp.float32)
                    acc = (acc * (1.0 / (M - 1))).reshape(ROWS // 8, 8, 2 * LANES)
                    both = swap_halves(acc[:, :, :LANES], acc[:, :, LANES:])
                    parts.append(jnp.stack(both, axis=1).reshape(areas, 8, LANES))
                done = jnp.stack(parts, axis=1).reshape(areas, 16, LANES)
                stage[pl.ds(first[r], areas), i] = done.astype(jnp.bfloat16)
            part(q, i).start()
        make((q + 1) & 3, 1 - slot)
        return carry

    lax.fori_loop(0, half, step, 0)

    def finish(q, carry):
        for i in range(QUADS):
            part(q, i).wait()
        return carry

    lax.fori_loop(0, half, finish, 0)


def product(metric, slab):
    any_space = pl.BlockSpec(memory_space=pl.ANY)
    dma = pltpu.SemaphoreType.DMA
    return pl.pallas_call(
        product_kernel,
        out_shape=jax.ShapeDtypeStruct((AREAS, QUADS, 16, LANES), jnp.bfloat16),
        in_specs=[pl.BlockSpec(memory_space=pltpu.VMEM)] * 2,
        out_specs=any_space,
        scratch_shapes=[
            pltpu.VMEM((AREAS, 4 * M), jnp.bfloat16),
            pltpu.VMEM((2, 2, ROWS, 4 * M), jnp.bfloat16),
            pltpu.VMEM((AREAS, QUADS, 16, LANES), jnp.bfloat16),
            dma((32,)),
        ],
        compiler_params=pltpu.CompilerParams(vmem_limit_bytes=32 * 2**20),
        cost_estimate=pl.CostEstimate(
            flops=2 * 2048 * 192 * 4096, bytes_accessed=20 * 2**20, transcendentals=0),
        name="product",
    )(metric, slab)


def body(tiles, farm_area, capacity, offsets, state):
    by_member = jnp.transpose(tiles, (1, 2, 0))
    columns = state.reshape(M, 2, 64, LANES)
    columns = jnp.transpose(columns, (0, 2, 1, 3)).reshape(M, QUADS, 16, LANES)
    metric, slab = exchange(
        by_member, farm_area.reshape(1, F), capacity.reshape(1, F), offsets, columns)
    out = product(metric, slab)
    out = jnp.transpose(out.reshape(AREAS, 64, 2, LANES), (0, 2, 1, 3))
    return out.reshape(AREAS, 2, 64 * LANES)


def solution(mesh):
    in_specs = (P("grid", None, None), P("grid"), P("grid"), P("grid"), P(None, "lev", "grid"))
    out_specs = P(None, "lev", "grid")
    return jax.shard_map(body, mesh=mesh, in_specs=in_specs, out_specs=out_specs, check_vma=False)
```

```python
import jax
import jax.numpy as jnp
from jax import lax
from jax.experimental import pallas as pl
from jax.experimental.pallas import tpu as pltpu
from jax.sharding import PartitionSpec as P

MESH = pl.DeviceIdType.MESH
M = 48
T = 144
F = 256
AREAS = 512
LANES = 128
RING = 4
ONES = 16
PAD_X = ONES + T
ROWS_Z = 80
PAD_Z = 96
HALF = 64
RAMPS = 132
RAMPS_Z = 68
KEEP_X = 152
KEEP_Z = 88
QUADS = 8
ROWS = 256
capacity_floor = 200.0
spread_floor = 0.05


def iota(shape, dim):
    return lax.broadcasted_iota(jnp.int32, shape, dim)


def swap_halves(u, v):
    low = iota(u.shape, 1) < 4
    crossed = pltpu.roll(jnp.where(low, v, u), 4, 1)
    return jnp.where(low, u, crossed), jnp.where(low, crossed, v)


def ramp_metric(power, offset, first, last):
    steps = power.shape[0]
    wide = jnp.broadcast_to(offset, power.shape).astype(jnp.int32)
    later = power
    for bit in (1, 2, 4, 8):
        later = jnp.where((wide & bit) != 0, pltpu.roll(later, steps - bit, 0), later)
    row = iota(power.shape, 0)
    inside = (row >= first) & (row < last)
    return jnp.max(jnp.where(inside, later - power, -3e38), axis=0, keepdims=True)


STEP = (0, 0, 1, 1, 3, 3, 2, 2)
BACK = (0, 1, 4, 5, 2, 3, 6, 7)
ORDER = (6, 7, 2, 4, 3, 5, 1)
NEAR = 6
STARTS, ROWS_X, SKIP = (0, 96), (96, 48), (ONES, 0)


def exchange_kernel(
    tiles, farm_area, capacity, offsets, state, metric_out, slab_out,
    area_in, capacity_in, offsets_in, near_tiles,
    facts_x, facts_z, got_a, got_b, got_z, weight_x, weight_z,
    part_x, part_z, sum_x, sum_z, near_x, off_x, off_z,
    metrics, st,
    local_sem, fx_send, fx_recv, fz_send, fz_recv, x_send, x_recv, z_send, z_recv,
    bx_send, bx_recv, bz_send, bz_recv,
    all_send, all_recv,
):
    g = lax.axis_index("grid")
    y = lax.axis_index("lev")
    z = lax.div(g, 8)
    x = lax.rem(lax.div(g, 2), 4)
    c = lax.rem(g, 2)
    mine_x = 2 * x + c
    mine_z = 2 * z + c
    xs = [x] + [lax.rem(x + d, 4) for d in range(1, 4)]
    zs = [z] + [lax.rem(z + d, 4) for d in range(1, 4)]
    ys = [y] + [lax.rem(y + d, 4) for d in range(1, 4)]
    cs = [c, 1 - c]

    def device(xx, zz, cc, yy):
        return (zz * 8 + xx * 2 + cc, yy)

    sibling = device(x, z, 1 - c, y)
    x_peers = [(xs[STEP[i]], cs[i % 2]) for i in range(8)]
    z_peers = [(zs[STEP[i]], cs[i % 2]) for i in range(8)]

    def remote(src, dst, send_sem, recv_sem, to):
        return pltpu.make_async_remote_copy(
            src_ref=src, dst_ref=dst, send_sem=send_sem, recv_sem=recv_sem,
            device_id=to, device_id_type=MESH)

    def wait_for(slot, send, recv):
        remote(slot, slot, send, recv, sibling).wait_recv()

    def loop(first, last):
        def run(body):
            lax.fori_loop(first, last, lambda i, carry: (body(i), carry)[1], 0)
        return run

    got_x = (got_a, got_b)
    barrier = pltpu.get_barrier_semaphore()

    def greet(to):
        pl.semaphore_signal(barrier, inc=1, device_id=to, device_id_type=MESH)

    for i in ORDER:
        xx, cc = x_peers[i]
        greet(device(xx, z, cc, y))
        if i != 1:
            zz, cc = z_peers[i]
            greet(device(x, zz, cc, y))
    for d in (2, 1, 3):
        greet(device(x, z, c, ys[d]))

    def x_slot(i, half):
        return got_x[half].at[i, pl.ds(SKIP[half], ROWS_X[half])]

    def z_slot(i):
        return got_z.at[i, pl.ds(0, ROWS_Z)]

    def x_tile(xx, cc):
        return near_tiles.at[2 * xx + cc]

    def z_tile(zz, cc):
        return near_tiles.at[8 + zz, pl.ds(pl.multiple_of(HALF * cc, HALF), ROWS_Z)]

    local = [
        pltpu.make_async_copy(farm_area, area_in, local_sem.at[0]),
        pltpu.make_async_copy(capacity, capacity_in, local_sem.at[1]),
        pltpu.make_async_copy(offsets, offsets_in, local_sem.at[2]),
        pltpu.make_async_copy(tiles.at[pl.ds(12 * y, 12)], near_tiles, local_sem.at[6]),
        pltpu.make_async_copy(
            tiles.at[12 * y + 8 + z, pl.ds(pl.multiple_of(HALF * c, HALF), ROWS_Z)],
            z_slot(0), local_sem.at[3]),
        pltpu.make_async_copy(
            tiles.at[12 * y + mine_x, pl.ds(STARTS[0], ROWS_X[0])], x_slot(0, 0),
            local_sem.at[4]),
        pltpu.make_async_copy(
            tiles.at[12 * y + mine_x, pl.ds(STARTS[1], ROWS_X[1])], x_slot(0, 1),
            local_sem.at[7]),
        pltpu.make_async_copy(state, st, local_sem.at[5]),
    ]
    for copy in local[:4]:
        copy.start()
    def fx_copy(i):
        xx, cc = x_peers[i]
        return remote(facts_x.at[0], facts_x.at[BACK[i]], fx_send.at[i], fx_recv.at[BACK[i]],
                      device(xx, z, cc, y))

    def fz_copy(i):
        zz, cc = z_peers[i]
        return remote(facts_z.at[0], facts_z.at[BACK[i]], fz_send.at[i], fz_recv.at[BACK[i]],
                      device(x, zz, cc, y))

    def x_copy(i, half):
        xx, cc = x_peers[i]
        return remote(x_tile(xx, cc).at[pl.ds(STARTS[half], ROWS_X[half])], x_slot(BACK[i], half),
                      x_send.at[half, i], x_recv.at[half, BACK[i]], device(xx, z, cc, y))

    def z_copy(i):
        zz, cc = z_peers[i]
        return remote(z_tile(zz, cc), z_slot(BACK[i]), z_send.at[i], z_recv.at[BACK[i]],
                      device(x, zz, cc, y))

    sends = []

    def start(*copies):
        for copy in copies:
            copy.start()
            sends.append(copy)

    for copy in local[:3]:
        copy.wait()

    lane = iota((1, F), 1)
    offset = jnp.zeros((1, F), jnp.int32)
    for k in range(16):
        offset = jnp.where((lane & 15) == k, offsets_in[k], offset)
    area = area_in[...]
    turned = ((area >> 5) & 3) * 128 + (area >> 7) * 32 + (area & 31)
    for facts, ids, spot in ((facts_z, turned, mine_z), (facts_x, area, mine_x)):
        placed = jnp.where((lane >> 4) == spot, offset, 0)
        rows = jnp.concatenate([ids, capacity_in[...] + 256 * placed], axis=0)
        facts[0] = rows.astype(jnp.float32)

    pl.semaphore_wait(barrier, 16)
    for i in ORDER:
        start(fx_copy(i), fz_copy(i))
    local[3].wait()
    for i in ORDER:
        start(x_copy(i, 0), z_copy(i))
    for i in ORDER[2:] + ORDER[:2]:
        start(x_copy(i, 1))
    for copy in local[4:]:
        copy.start()

    got_a[:, pl.ds(0, ONES)] = jnp.ones((8, ONES, F), jnp.bfloat16)
    got_z[:, pl.ds(ROWS_Z, ONES)] = jnp.ones((8, ONES, F), jnp.bfloat16)
    off_x[...] = jnp.zeros_like(off_x)
    off_z[...] = jnp.zeros_like(off_z)
    area_ids = iota((AREAS, F), 0).astype(jnp.float32)

    def weigh(i, facts, weight, off):
        rows = facts[i]
        shift = jnp.floor(rows[1:2] * (1 / 256))
        off[...] = off[...] + shift[:, :LANES]
        placed = jnp.where(area_ids == rows[0:1], rows[1:2] - 256 * shift, 0.0)
        weight[:, pl.ds(pl.multiple_of(F * i, F), F)] = placed.astype(jnp.bfloat16)

    @loop(0, 8)
    def _(i):
        for facts, recv, send, weight, off in (
                (facts_z, fz_recv, fz_send, weight_z, off_z),
                (facts_x, fx_recv, fx_send, weight_x, off_x)):
            @pl.when(i > 0)
            def _():
                wait_for(facts.at[i], send.at[i], recv.at[i])

            weigh(i, facts, weight, off)

    def sum_up(values, weights):
        return lax.dot_general(values, weights, (((1,), (1,)), ((), ())),
                               preferred_element_type=jnp.float32)

    bz = []

    near, far, all_slots = range(NEAR), range(NEAR, 8), range(8)

    def block_pair(p):
        return lax.rem(z + 2 + p, 4), lax.rem(z + 1 + 3 * p, 4)

    def side_by_side(got, slots):
        return jnp.concatenate([got[i] for i in slots], axis=1)

    def dot_x(half, p, slots):
        columns = pl.ds(F * slots[0], F * len(slots))
        chosen = jnp.concatenate(
            [weight_x[pl.ds(pl.multiple_of(LANES * zz, LANES), LANES), columns]
             for zz in block_pair(p)], axis=0)
        return sum_up(side_by_side(got_x[half], slots), chosen)

    def sum_copy(half, rows, d, zz):
        return remote(part_x.at[zz, rows], sum_x.at[3 - d, rows], bx_send.at[half, d - 1],
                      bx_recv.at[half, 3 - d], device(x, zz, c, y))

    def leave(half, rows, p, value):
        for k, zz in enumerate(block_pair(p)):
            part_x[zz, rows] = value[:, k * LANES : (k + 1) * LANES]
        sum_copy(half, rows, 2 + p, block_pair(p)[0]).start()

        @pl.when(p == 0)
        def _():
            sum_copy(half, rows, 1, zs[1]).start()

    early_rows, late_rows = pl.ds(0, 8 + ROWS_X[0]), pl.ds(8 + ROWS_X[0], ROWS_X[1])
    local[5].wait()
    for i in range(1, 8):
        wait_for(x_slot(i, 0), x_send.at[0, i], x_recv.at[0, i])

    @loop(0, 2)
    def _(p):
        leave(0, early_rows, p, dot_x(0, p, all_slots)[8:])

    local[4].wait()
    for i in range(1, 8):
        wait_for(z_slot(i), z_send.at[i], z_recv.at[i])
    for h in range(2):
        value = sum_up(side_by_side(got_z, all_slots), weight_z[pl.ds(2 * LANES * h, 2 * LANES)])
        for b in range(2):
            part_z[2 * h + b] = value[:KEEP_Z, b * LANES : (b + 1) * LANES]
    for d in (2, 1, 3):
        copy = remote(part_z.at[xs[d]], sum_z.at[3 - d], bz_send.at[d - 1], bz_recv.at[3 - d],
                      device(xs[d], z, c, y))
        copy.start()
        bz.append(copy)

    local[6].wait()
    for i in range(1, NEAR):
        wait_for(x_slot(i, 1), x_send.at[1, i], x_recv.at[1, i])

    @loop(0, 2)
    def _(p):
        near_x[p] = dot_x(1, p, near)

    for i in range(NEAR, 8):
        wait_for(x_slot(i, 1), x_send.at[1, i], x_recv.at[1, i])

    @loop(0, 2)
    def _(p):
        leave(1, late_rows, p, near_x[p] + dot_x(1, p, far))

    bx = [[sum_copy(half, rows, d, zs[d]) for d in range(1, 4)]
          for half, rows in ((0, early_rows), (1, late_rows))]

    def whole(copies, own, others, rows):
        for copy in copies:
            copy.wait_recv()
        total = own[rows]
        for k in range(3):
            total = total + others[k, rows]
        return total

    spot = (4 * y + z) * 8 + mine_x

    first = whole(bx[0], part_x.at[z], sum_x, early_rows)
    total = jnp.maximum(first[:1], capacity_floor)
    power = first[8:] / total
    early = ramp_metric(power, off_x[...], 0, 84)
    last = whole(bz, part_z.at[x], sum_z, pl.ds(0, KEEP_Z))
    metrics[spot, pl.ds(1, 1)] = ramp_metric(
        last[:ROWS_Z] / jnp.maximum(last[ROWS_Z : ROWS_Z + 1], capacity_floor),
        off_z[...], 0, RAMPS_Z)
    last = whole(bx[1], part_x.at[z], sum_x, late_rows)
    power = jnp.concatenate([power[80:], last / total], axis=0)
    late = ramp_metric(power, off_x[...], 4, 52)
    metrics[spot, pl.ds(0, 1)] = jnp.maximum(early, late)

    mine = metrics.at[spot]

    def hops(where):
        dy, dz, i = where
        return sum(min(d, 4 - d) for d in (dy, dz, STEP[i]))

    others = [(dy, dz, i) for dy in range(4) for dz in range(4) for i in range(8)][1:]
    for dy, dz, i in sorted(others, key=hops, reverse=True):
        xx, cc = x_peers[i]
        remote(mine, mine, all_send, all_recv, device(xx, zs[dz], cc, ys[dy])).start()

    local[7].wait()

    @loop(0, QUADS)
    def _(i):
        values = st[:, i].astype(jnp.float32).reshape(M, 2, 8, LANES)
        values = values - (jnp.sum(values, axis=0) / M)[None]
        pairs = values.reshape(M // 2, 2, 2, 8, LANES)
        for h in range(2):
            both = swap_halves(pairs[:, 0, h], pairs[:, 1, h])
            for k in range(2):
                slab_out[i, :, pl.ds((2 * h + k) * LANES, LANES)] = (
                    both[k].reshape(4 * M, LANES).astype(jnp.bfloat16))

    for copy in sends + bx[0] + bx[1] + bz:
        copy.wait_send()

    others = metrics.at[pl.ds(0, 127)]
    everything = remote(others, others, all_send, all_recv, sibling)
    everything.wait_recv()

    rows = metrics.reshape(256, LANES)
    for yy in range(4):
        for zz in range(4):
            metric_out[pl.ds(8 * yy, 8), pl.ds(LANES * zz, LANES)] = (
                rows[pl.ds(16 * (4 * yy + zz), 8, stride=2)])
    quarter = iota((16, LANES), 1) >> 5
    blocks = [jnp.maximum(rows[pl.ds(4 * b + 1, 16, stride=16)], rows[pl.ds(4 * b + 3, 16, stride=16)])
              for b in range(RING)]
    for zz in range(4):
        value = jnp.zeros((16, LANES), jnp.float32)
        for b in range(RING):
            move = (32 * (b - zz)) % LANES
            moved = pltpu.roll(blocks[b], move, 1) if move else blocks[b]
            value = jnp.where(quarter == b, moved, value)
        metric_out[pl.ds(32, 16), pl.ds(zz * LANES, LANES)] = value

    everything.wait_send()


def exchange(tiles, farm_area, capacity, offsets, state):
    any_space = pl.BlockSpec(memory_space=pl.ANY)
    vmem = pl.BlockSpec(memory_space=pltpu.VMEM)
    dma = pltpu.SemaphoreType.DMA
    f32, bf16 = jnp.float32, jnp.bfloat16
    return pl.pallas_call(
        exchange_kernel,
        out_shape=(
            pltpu.VMEM((M, AREAS), f32),
            pltpu.VMEM((QUADS, 4 * M, 4 * LANES), bf16),
        ),
        in_specs=[any_space] * 5,
        out_specs=(vmem, vmem),
        scratch_shapes=[
            pltpu.VMEM((1, F), jnp.int32),
            pltpu.VMEM((1, F), jnp.int32),
            pltpu.SMEM((16,), jnp.int32),
            pltpu.VMEM((12, T, F), bf16),
            pltpu.VMEM((8, 2, F), f32),
            pltpu.VMEM((8, 2, F), f32),
            pltpu.VMEM((8, ONES + ROWS_X[0], F), bf16),
            pltpu.VMEM((8, ROWS_X[1], F), bf16),
            pltpu.VMEM((8, ROWS_Z + ONES, F), bf16),
            pltpu.VMEM((AREAS, 8 * F), bf16),
            pltpu.VMEM((AREAS, 8 * F), bf16),
            pltpu.VMEM((RING, KEEP_X, LANES), f32),
            pltpu.VMEM((RING, KEEP_Z, LANES), f32),
            pltpu.VMEM((3, KEEP_X, LANES), f32),
            pltpu.VMEM((3, KEEP_Z, LANES), f32),
            pltpu.VMEM((2, ROWS_X[1], 2 * LANES), f32),
            pltpu.VMEM((1, LANES), f32),
            pltpu.VMEM((1, LANES), f32),
            pltpu.VMEM((128, 2, LANES), f32),
            pltpu.VMEM((M, QUADS, 16, LANES), bf16),
            dma((8,)), dma((8,)), dma((8,)), dma((8,)), dma((8,)),
            dma((2, 8)), dma((2, 8)), dma((8,)), dma((8,)),
            dma((2, 3)), dma((2, 3)), dma((3,)), dma((3,)),
            dma, dma,
        ],
        compiler_params=pltpu.CompilerParams(
            collective_id=0, has_side_effects=True, vmem_limit_bytes=60 * 2**20),
        cost_estimate=pl.CostEstimate(
            flops=2 * 256 * 2048 * 512, bytes_accessed=5 * 2**20, transcendentals=0),
        name="exchange",
    )(tiles, farm_area, capacity, offsets, state)


def product_kernel(metric, slab, out, wide, lhs, stage, out_sem):
    values = metric[...]
    anomaly = values - jnp.mean(values, axis=0, keepdims=True)
    spread = jnp.sqrt(jnp.sum(anomaly * anomaly, axis=0, keepdims=True) / (M - 1))
    scores = anomaly / jnp.maximum(spread, spread_floor)
    scores = jnp.transpose(scores).astype(jnp.bfloat16)

    held = iota((M, 4 * M), 0)
    rest = held - 32
    member = jnp.where(
        held < 32,
        12 * (held >> 3) + (held & 7),
        12 * (rest >> 2) + 8 + (rest & 3))
    widen = ((iota((M, 4 * M), 1) >> 2) == member).astype(jnp.bfloat16)
    wide[...] = jnp.dot(scores, widen, preferred_element_type=jnp.float32).astype(jnp.bfloat16)
    repeat = ((iota((ROWS, ROWS // 4), 0) >> 2) == iota((ROWS, ROWS // 4), 1)).astype(
        jnp.bfloat16)
    keep = (iota((ROWS, 4 * M), 0) & 3) == (iota((ROWS, 4 * M), 1) & 3)
    areas = ROWS // 4

    half = 4 * AREAS // ROWS // 2

    def part(q, i):
        some = pl.ds(pl.multiple_of(2 * areas * q, 2 * areas), 2 * areas)
        return pltpu.make_async_copy(stage.at[some, i], out.at[some, i], out_sem.at[QUADS * q + i])

    def make(q, slot):
        for r in range(2):
            rows = pl.ds(pl.multiple_of((2 * q + r) * areas, areas), areas)
            repeated = jnp.dot(repeat, wide[rows], preferred_element_type=jnp.float32)
            lhs[slot, r] = jnp.where(keep, repeated, 0.0).astype(jnp.bfloat16)

    make(0, 0)

    def step(q, carry):
        first = [pl.multiple_of((2 * q + r) * areas, areas) for r in range(2)]
        slot = q & 1
        for i in range(QUADS):
            for r in range(2):
                parts = []
                for h in range(2):
                    acc = jnp.dot(lhs[slot, r], slab[i, :, pl.ds(2 * LANES * h, 2 * LANES)],
                                  preferred_element_type=jnp.float32)
                    acc = (acc * (1.0 / (M - 1))).reshape(ROWS // 8, 8, 2 * LANES)
                    both = swap_halves(acc[:, :, :LANES], acc[:, :, LANES:])
                    parts.append(jnp.stack(both, axis=1).reshape(areas, 8, LANES))
                done = jnp.stack(parts, axis=1).reshape(areas, 16, LANES)
                stage[pl.ds(first[r], areas), i] = done.astype(jnp.bfloat16)
            part(q, i).start()
        make((q + 1) & 3, 1 - slot)
        return carry

    lax.fori_loop(0, half, step, 0)

    def finish(q, carry):
        for i in range(QUADS):
            part(q, i).wait()
        return carry

    lax.fori_loop(0, half, finish, 0)


def product(metric, slab):
    any_space = pl.BlockSpec(memory_space=pl.ANY)
    dma = pltpu.SemaphoreType.DMA
    return pl.pallas_call(
        product_kernel,
        out_shape=jax.ShapeDtypeStruct((AREAS, QUADS, 16, LANES), jnp.bfloat16),
        in_specs=[pl.BlockSpec(memory_space=pltpu.VMEM)] * 2,
        out_specs=any_space,
        scratch_shapes=[
            pltpu.VMEM((AREAS, 4 * M), jnp.bfloat16),
            pltpu.VMEM((2, 2, ROWS, 4 * M), jnp.bfloat16),
            pltpu.VMEM((AREAS, QUADS, 16, LANES), jnp.bfloat16),
            dma((32,)),
        ],
        compiler_params=pltpu.CompilerParams(vmem_limit_bytes=32 * 2**20),
        cost_estimate=pl.CostEstimate(
            flops=2 * 2048 * 192 * 4096, bytes_accessed=20 * 2**20, transcendentals=0),
        name="product",
    )(metric, slab)


def body(tiles, farm_area, capacity, offsets, state):
    by_member = jnp.transpose(tiles, (1, 2, 0))
    columns = state.reshape(M, 2, 64, LANES)
    columns = jnp.transpose(columns, (0, 2, 1, 3)).reshape(M, QUADS, 16, LANES)
    metric, slab = exchange(
        by_member, farm_area.reshape(1, F), capacity.reshape(1, F), offsets, columns)
    out = product(metric, slab)
    out = jnp.transpose(out.reshape(AREAS, 64, 2, LANES), (0, 2, 1, 3))
    return out.reshape(AREAS, 2, 64 * LANES)


def solution(mesh):
    in_specs = (P("grid", None, None), P("grid"), P("grid"), P("grid"), P(None, "lev", "grid"))
    out_specs = P(None, "lev", "grid")
    return jax.shard_map(body, mesh=mesh, in_specs=in_specs, out_specs=out_specs, check_vma=False)
```
